128 devices in a mesh: gx: 4 (over z), yz: 32 (over y, x, core).
Axes of the slice: x: 4, y: 4, z: 4, core: 2. Of those that a mesh axis runs over, the one named last changes fastest.
Arguments:
- coarse_density: float32 [128, 1024, 128], P('gx', 'yz'), may hold values from 0.5 to 2
- coarse_velocity: float32 [3, 128, 1024, 128], P(None, 'gx', 'yz'), may hold values from -3 to 3
- coarse_pressure: float32 [128, 1024, 128], P('gx', 'yz'), may hold values from 0.5 to 2
- coarse_bins: int32 [128, 1024], P('gx', 'yz'), may hold values from 0 to 1998
- fine_density: float32 [4096, 8, 8, 256], P(('gx', 'yz')), may hold values from 0.5 to 2
- fine_velocity: float32 [3, 4096, 8, 8, 256], P(None, ('gx', 'yz')), may hold values from -3 to 3
- fine_pressure: float32 [4096, 8, 8, 256], P(('gx', 'yz')), may hold values from 0.5 to 2
- fine_bins: int32 [4096, 8, 8], P(('gx', 'yz')), may hold values from 0 to 1998
- patch_host: int32 [4096], replicated, may hold values from 0 to 31, as said below
- patch_spot: int32 [4096], replicated, may hold values from 0 to 35, as said below
- heat_rate: float32 [2000], replicated, may hold values from 1 to 16
- cool_rate: float32 [2000], replicated, may hold values from 1 to 16
Outputs:
- coarse_state: float32 [5, 128, 1024, 128], P(None, 'gx', 'yz')
- fine_state: float32 [5, 4096, 8, 8, 256], P(None, ('gx', 'yz'))
The draws below stay inside these ranges and needn't reach their ends.
Inputs may be any that keep to these rules, and one draw needn't show every extreme that they name: Patch p is held by device p // 32 of the mesh (gx slowest) and lies in the block of the device of the same gx row whose yz index is patch_host[p]. Of one device's 32 patches at most 2 have the same host, and one block hosts at most 36 patches; both bounds are reached. `patch_spot`: patches of one gx row with the same host have different places.
All inputs are finite; a program needn't handle non-finite values.
Results may differ from the reference program's by a relative error of at most 0.00002.
Values sent between devices are 32-bit elements; how exact they have to be, the bound alone decides.
No kernel may reach another device: no remote copies, remote signals or barrier semaphores. Data moves between devices by JAX's collectives and lax.ppermute only.
A program may use at most 640 MiB of HBM per device.

```python
import math
import jax
import jax.numpy as jnp
from jax import lax

BX = 32
BY = 32
NZ = 128
K = 32
PF = 8
NB = 2000
FOOT = 4
FZ = 256
SY = 6
SPOTS = 36
HMAX = 36
NX = 128
NY = 1024
NPT = 4096
N_GX = 4
N_YZ = 32


def patch_layout(key):

    def one_row(row_key):
        keys = jax.random.split(row_key, 5)
        ranks = jnp.arange(N_YZ, dtype=jnp.int32)
        owners = jax.random.permutation(keys[0], N_YZ).astype(jnp.int32)
        excess = HMAX - K
        others = N_YZ - 1
        loss = jnp.where(ranks == 0, 0, excess // others + (ranks - 1 < excess % others).astype(jnp.int32))
        moved = jax.random.randint(keys[1], (N_YZ,), 0, 3, dtype=jnp.int32)
        gained = jnp.where((ranks % 2 == 1) & (ranks + 1 < N_YZ), moved, 0)
        given = jnp.where((ranks % 2 == 0) & (ranks >= 2), jnp.roll(gained, 1), 0)
        hosted = jnp.where(ranks == 0, HMAX, K - loss + gained - given).astype(jnp.int32)
        ends = jnp.cumsum(hosted).astype(jnp.int32)
        starts = ends - hosted
        places = jnp.arange(K * N_YZ, dtype=jnp.int32)
        place_rank = jnp.sum((places[:, None] >= ends[None, :]).astype(jnp.int32), axis=1)
        within = places - starts[place_rank]
        place_owner = owners[place_rank]
        spot_tables = jax.vmap(lambda sub: jax.random.permutation(sub, SPOTS))(jax.random.split(keys[2], N_YZ)).astype(jnp.int32)
        place_spot = spot_tables[place_owner, within]
        custodian_ranks = jax.random.permutation(keys[3], N_YZ).astype(jnp.int32)
        orders = jax.vmap(lambda sub: jax.random.permutation(sub, K))(jax.random.split(keys[4], N_YZ)).astype(jnp.int32)
        holder = custodian_ranks[places % N_YZ]
        column = orders[holder, places // N_YZ]
        host_table = jnp.zeros((N_YZ, K), jnp.int32).at[holder, column].set(place_owner)
        spot_table = jnp.zeros((N_YZ, K), jnp.int32).at[holder, column].set(place_spot)
        return (host_table.reshape(-1), spot_table.reshape(-1))
    hosts, spots = jax.vmap(one_row)(jax.random.split(key, N_GX))
    return (hosts.reshape(-1), spots.reshape(-1))


def draw_patch_host(key, part):
    hosts, spots = patch_layout(key)
    return hosts


def draw_patch_spot(key, part):
    hosts, spots = patch_layout(key)
    return spots


def place_ends(values, rng, low, largest):
    index_at = [jax.random.randint(jax.random.fold_in(rng, axis), (), 0, length) for axis, length in enumerate(values.shape)]
    longest = values.shape.index(max(values.shape))
    next_to = index_at[:longest] + [(index_at[longest] + 1) % values.shape[longest]] + index_at[longest + 1:]
    return values.at[tuple(index_at)].set(low).at[tuple(next_to)].set(largest)


def level_of(rng, dims, shards, low, top_value):
    gain = 1.0
    for dim, blocks in shards:
        draws = jax.random.uniform(jax.random.fold_in(jax.random.fold_in(rng, 6), dim), (blocks,), jnp.float32, low / len(shards), top_value / len(shards))
        gain = gain * jnp.repeat(jnp.exp(draws), dims[dim] // blocks).reshape((-1,) + (1,) * (len(dims) - 1 - dim))
    return gain


def bell_draw(stream_key, shape, spread, reach, cuts=(), kind=jnp.bfloat16):
    values = jax.random.normal(stream_key, shape, jnp.float32) * spread
    if len(cuts) > 0:
        values = level_of(stream_key, shape, cuts, -0.22, 0.18) * values
    return jnp.clip(values, min=-reach, max=reach).astype(kind)


def setup_inputs(seed: int = 0) -> dict:
    key_of = jax.random.split(jax.random.key(seed), 13)
    return {
        "coarse_density": jnp.clip(jnp.exp(math.log(2.0) - 1.3862944 * jax.random.uniform(key_of[0], (NX, NY, NZ), jnp.float32) ** level_of(key_of[0], (NX, NY, NZ), ((0, 4), (1, 32)), -0.2, 0.2)), 0.5, 2.0),
        "coarse_velocity": bell_draw(key_of[1], (3, NX, NY, NZ), 0.5, 3.0, ((1, 4), (2, 32)), jnp.float32),
        "coarse_pressure": jnp.clip(jnp.exp(math.log(2.0) - 1.3862944 * jax.random.uniform(key_of[2], (NX, NY, NZ), jnp.float32) ** level_of(key_of[2], (NX, NY, NZ), ((0, 4), (1, 32)), -0.2, 0.2)), 0.5, 2.0),
        "coarse_bins": place_ends(jax.random.randint(key_of[3], (NX, NY), 0, NB - 1), jax.random.fold_in(key_of[3], 1), 0, (NB - 1) - 1).astype(jnp.int32),
        "fine_density": jnp.clip(jnp.exp(math.log(2.0) - 1.3862944 * jax.random.uniform(key_of[4], (NPT, PF, PF, FZ), jnp.float32) ** level_of(key_of[4], (NPT, PF, PF, FZ), ((0, 128),), -0.2, 0.2)), 0.5, 2.0),
        "fine_velocity": bell_draw(key_of[5], (3, NPT, PF, PF, FZ), 0.5, 3.0, ((1, 128),), jnp.float32),
        "fine_pressure": jnp.clip(jnp.exp(math.log(2.0) - 1.3862944 * jax.random.uniform(key_of[6], (NPT, PF, PF, FZ), jnp.float32) ** level_of(key_of[6], (NPT, PF, PF, FZ), ((0, 128),), -0.2, 0.2)), 0.5, 2.0),
        "fine_bins": place_ends(jax.random.randint(key_of[7], (NPT, PF, PF), 0, NB - 1), jax.random.fold_in(key_of[7], 1), 0, (NB - 1) - 1).astype(jnp.int32),
        "patch_host": draw_patch_host(jax.random.fold_in(key_of[12], 71), 0),
        "patch_spot": draw_patch_spot(jax.random.fold_in(key_of[12], 71), 0),
        "heat_rate": jnp.clip(jnp.exp(jax.random.uniform(key_of[10], (NB,), jnp.float32, math.log(1.0), math.log(16.0))), 1.0, 16.0),
        "cool_rate": jnp.clip(jnp.exp(jax.random.uniform(key_of[11], (NB,), jnp.float32, math.log(1.0), math.log(16.0))), 1.0, 16.0),
    }


GAMMA = 5.0 / 3.0
STEP = 0.02
FINE_STEP = 0.04

def conserved(physical_variables_vector):
    matter_per_volume = physical_variables_vector[0]
    flow_speed = physical_variables_vector[1:4]
    pressure = physical_variables_vector[4]
    kinetic = 0.5 * matter_per_volume * (flow_speed[0] * flow_speed[0] + flow_speed[1] * flow_speed[1] + flow_speed[2] * flow_speed[2])
    return jnp.concatenate([matter_per_volume[None], matter_per_volume[None] * flow_speed, (pressure / (GAMMA - 1.0) + kinetic)[None]], axis=0)

def euler_flux(physical_variables_vector, amounts, direction):
    normal_speed = physical_variables_vector[1 + direction]
    pressure = physical_variables_vector[4]
    entries = [amounts[1 + direction]]
    for component in range(3):
        momentum = amounts[1 + component] * normal_speed
        if component == direction:
            momentum = momentum + pressure
        entries.append(momentum)
    entries.append((amounts[4] + pressure) * normal_speed)
    return jnp.stack(entries)

def rusanov(left, left_amounts, right, right_amounts, direction):
    left_speed = jnp.abs(left[1 + direction]) + jnp.sqrt(GAMMA * left[4] / left[0])
    right_speed = jnp.abs(right[1 + direction]) + jnp.sqrt(GAMMA * right[4] / right[0])
    fastest = jnp.maximum(left_speed, right_speed)
    average = 0.5 * (euler_flux(left, left_amounts, direction) + euler_flux(right, right_amounts, direction))
    return average - 0.5 * fastest * (right_amounts - left_amounts)

def energy_source(physical_variables_vector, bins, heat_rate, cool_rate):
    matter_per_volume = physical_variables_vector[0]
    thermal_kelvin = physical_variables_vector[4] / matter_per_volume
    blending_share = thermal_kelvin / (1.0 + thermal_kelvin)
    heating = (1.0 - blending_share) * jnp.take(heat_rate, bins) + blending_share * jnp.take(heat_rate, bins + 1)
    cooling = (1.0 - blending_share) * jnp.take(cool_rate, bins) + blending_share * jnp.take(cool_rate, bins + 1)
    return matter_per_volume * heating - matter_per_volume * matter_per_volume * cooling

def spread_columns(columns):
    return jnp.repeat(jnp.repeat(columns, 2, axis=1), 2, axis=2)

def fine_step(physical_variables_vector, rim, bins, heat_rate, cool_rate):
    width = physical_variables_vector.shape[1]
    half = width // 2
    depth = physical_variables_vector.shape[3] // 2
    ghost_low_x = spread_columns(rim[:, 0:half])
    ghost_high_x = spread_columns(rim[:, half:2 * half])
    ghost_low_y = spread_columns(rim[:, 2 * half:3 * half])
    ghost_high_y = spread_columns(rim[:, 3 * half:4 * half])
    amounts = conserved(physical_variables_vector)
    along_x = jnp.concatenate([ghost_low_x[:, None], physical_variables_vector, ghost_high_x[:, None]], axis=1)
    amounts_x = jnp.concatenate([conserved(ghost_low_x)[:, None], amounts, conserved(ghost_high_x)[:, None]], axis=1)
    flux_x = rusanov(along_x[:, :-1], amounts_x[:, :-1], along_x[:, 1:], amounts_x[:, 1:], 0)
    along_y = jnp.concatenate([ghost_low_y[:, :, None], physical_variables_vector, ghost_high_y[:, :, None]], axis=2)
    amounts_y = jnp.concatenate([conserved(ghost_low_y)[:, :, None], amounts, conserved(ghost_high_y)[:, :, None]], axis=2)
    flux_y = rusanov(along_y[:, :, :-1], amounts_y[:, :, :-1], along_y[:, :, 1:], amounts_y[:, :, 1:], 1)
    flux_z = rusanov(physical_variables_vector, amounts, jnp.roll(physical_variables_vector, -1, 3), jnp.roll(amounts, -1, 3), 2)
    change = flux_x[:, 1:] - flux_x[:, :-1] + (flux_y[:, :, 1:] - flux_y[:, :, :-1]) + (flux_z - jnp.roll(flux_z, 1, 3))
    updated = amounts - FINE_STEP * change
    updated = updated.at[4].add(STEP * energy_source(physical_variables_vector, bins[:, :, None], heat_rate, cool_rate))
    averaged = updated.reshape(5, half, 2, half, 2, depth, 2).sum(axis=(2, 4, 6)) * 0.125
    averaged = averaged.reshape(5, half * half, depth)

    def face_mean(face):
        return face.reshape(5, half, 2, depth, 2).sum(axis=(2, 4)) * 0.25
    sums = jnp.concatenate([averaged, face_mean(flux_x[:, 0]), face_mean(flux_x[:, width]), face_mean(flux_y[:, :, 0]), face_mean(flux_y[:, :, width])], axis=1)
    return (updated, sums)

def reference(coarse_density, coarse_velocity, coarse_pressure, coarse_bins, fine_density, fine_velocity, fine_pressure, fine_bins, patch_host, patch_spot, heat_rate, cool_rate):
    physical_variables_vector = jnp.concatenate([coarse_density[None], coarse_velocity, coarse_pressure[None]], axis=0)
    amounts = conserved(physical_variables_vector)
    fluxes = []
    change = None
    for direction in range(3):
        axis_index = direction + 1
        face_flux = rusanov(physical_variables_vector, amounts, jnp.roll(physical_variables_vector, -1, axis_index), jnp.roll(amounts, -1, axis_index), direction)
        fluxes.append(face_flux)
        difference = face_flux - jnp.roll(face_flux, 1, axis_index)
        change = difference if change is None else change + difference
    updated = amounts - STEP * change
    updated = updated.at[4].add(STEP * energy_source(physical_variables_vector, coarse_bins[:, :, None], heat_rate, cool_rate))
    patch_index_list = jnp.arange(NPT, dtype=jnp.int32)
    row_ids = patch_index_list // (K * N_YZ)
    start_x = (row_ids * BX + 1 + 5 * (patch_spot // SY))[:, None]
    start_y = (patch_host * BY + 1 + 5 * (patch_spot % SY))[:, None]
    offsets = jnp.arange(FOOT, dtype=jnp.int32)[None, :]
    low = jnp.zeros_like(offsets)
    rim_x = jnp.concatenate([start_x - 1 + low, start_x + FOOT + low, start_x + offsets, start_x + offsets], axis=1)
    rim_y = jnp.concatenate([start_y + offsets, start_y + offsets, start_y - 1 + low, start_y + FOOT + low], axis=1)
    rims = jnp.moveaxis(physical_variables_vector[:, rim_x, rim_y, :], 0, 1)
    fine_primitive = jnp.moveaxis(jnp.concatenate([fine_density[None], fine_velocity, fine_pressure[None]], axis=0), 0, 1)
    fine_new, sums = lax.map(lambda items: fine_step(items[0], items[1], items[2], heat_rate, cool_rate), (fine_primitive, rims, fine_bins))
    sums = jnp.moveaxis(sums, 0, 1)
    flux_x = fluxes[0]
    flux_y = fluxes[1]
    coarse_xlo = flux_x[:, start_x - 1 + low, start_y + offsets]
    coarse_xhi = flux_x[:, start_x + FOOT - 1 + low, start_y + offsets]
    coarse_ylo = flux_y[:, start_x + offsets, start_y - 1 + low]
    coarse_yhi = flux_y[:, start_x + offsets, start_y + FOOT - 1 + low]
    cells = FOOT * FOOT
    deltas = jnp.concatenate([STEP * (coarse_xlo - sums[:, :, cells:cells + FOOT]), STEP * (sums[:, :, cells + FOOT:cells + 2 * FOOT] - coarse_xhi), STEP * (coarse_ylo - sums[:, :, cells + 2 * FOOT:cells + 3 * FOOT]), STEP * (sums[:, :, cells + 3 * FOOT:cells + 4 * FOOT] - coarse_yhi)], axis=2)
    updated = updated.at[:, rim_x, rim_y, :].add(deltas)
    squares = jnp.arange(cells, dtype=jnp.int32)[None, :]
    foot_x = start_x + squares // FOOT
    foot_y = start_y + squares % FOOT
    updated = updated.at[:, foot_x, foot_y, :].set(sums[:, :, 0:cells])
    return (updated, jnp.moveaxis(fine_new, 0, 1))
```

```python
import functools

import jax
import jax.numpy as jnp
from jax import lax
from jax.experimental import pallas as pl
from jax.experimental.pallas import tpu as pltpu
from jax.sharding import PartitionSpec as P

GAMMA = 5.0 / 3.0
STEP = 0.02
HALF = 0.5 * STEP
FOOT = 4
SIDE = 5
CAP = 2
F32 = jnp.float32
VMEM = pltpu.VMEM
SMEM = pltpu.SMEM
MIB = 1024 * 1024
GRANT = 56 * MIB


def conserve(rho, ux, uy, uz, p):
    mx, my, mz = rho * ux, rho * uy, rho * uz
    xx, yy, zz = mx * ux, my * uy, mz * uz
    energy = 1.5 * p + 0.5 * (xx + yy + zz)
    return {
        "amounts": (rho, mx, my, mz, energy),
        "speed": (ux, uy, uz),
        "p": p,
        "square": (xx, yy, zz),
        "cross": {},
    }


def sound_of(p, rho):
    square = GAMMA * (p / rho)
    return square * lax.rsqrt(square)


def derive(prim):
    rho, p = prim[0], prim[4]
    both = rho + p
    common = p / (rho * both)
    square = GAMMA * (common * both)
    cell = conserve(*prim)
    cell["sound"] = square * lax.rsqrt(square)
    cell["share"] = common * rho
    return cell


def again(rho, ux, uy, uz, p, sound):
    cell = conserve(rho, ux, uy, uz, p)
    cell["sound"] = sound
    return cell


def directed(cell, d):
    amounts, p = cell["amounts"], cell["p"]
    u = cell["speed"][d]
    flux = [amounts[1 + d]]
    for k in range(3):
        if k == d:
            flux.append(cell["square"][d] + p)
            continue
        pair = (min(k, d), max(k, d))
        if pair not in cell["cross"]:
            cell["cross"][pair] = amounts[1 + pair[0]] * cell["speed"][pair[1]]
        flux.append(cell["cross"][pair])
    flux.append((amounts[4] + p) * u)
    return (amounts, flux, jnp.abs(u) + cell["sound"])


def twice_flux(left, right):
    fastest = jnp.maximum(left[2], right[2])
    return [
        (left[1][c] + right[1][c]) - fastest * (right[0][c] - left[0][c]) for c in range(5)
    ]


def shifted(cell, shift, axis):
    rho, p = cell["amounts"][0], cell["p"]
    values = (rho,) + cell["speed"] + (p, cell["sound"])
    return again(*[pltpu.roll(v, shift, axis) for v in values])


def source_term(rho, share, rates):
    heat, heat_slope, cool, cool_slope = rates
    return rho * ((heat + share * heat_slope) - rho * (cool + share * cool_slope))


def lane_pick(tile, lane):
    index = jnp.full((8, 128), lane, jnp.int32)
    return jnp.take_along_axis(tile, index, axis=1, mode="promise_in_bounds")


def pack_kernel(
    corner_ref, rho_hbm, vel_hbm, p_hbm, rim_ref, xa_ref, xb_ref, ya_ref, yb_ref, cell_ref, sem
):
    sources = [rho_hbm, vel_hbm.at[0], vel_hbm.at[1], vel_hbm.at[2], p_hbm]
    copies = [pltpu.make_async_copy(f, cell_ref.at[c], sem.at[c]) for c, f in enumerate(sources)]
    for copy in copies:
        copy.start()
    for copy in copies:
        copy.wait()
    fields = [cell_ref.at[c] for c in range(5)]
    width = 32
    rows = cell_ref.shape[1]

    def one(s, carry):
        base = corner_ref[s]

        @pl.when(base >= 0)
        def _():
            for c, f in enumerate(fields):
                rim_ref[s, c, 0:4, :] = f[pl.ds(base - width, 4), :]
                rim_ref[s, c, 4:8, :] = f[pl.ds(base + FOOT * width, 4), :]
                rim_ref[s, c, 8:12, :] = f[pl.ds(base - 1, 4, stride=width), :]
                rim_ref[s, c, 12:16, :] = f[pl.ds(base + FOOT, 4, stride=width), :]

        return carry

    for c, f in enumerate(fields):
        xa_ref[c] = f[0:width, :]
        xb_ref[c] = f[rows - width : rows, :]
        ya_ref[c] = f[pl.ds(0, width, stride=width), :]
        yb_ref[c] = f[pl.ds(width - 1, width, stride=width), :]
    lax.fori_loop(0, rim_ref.shape[0], one, 0)


def pack(corners, rho, vel, p, slots):
    whole = pl.BlockSpec(memory_space=VMEM)
    edge = jax.ShapeDtypeStruct((5, 32, 128), F32)
    return pl.pallas_call(
        pack_kernel,
        out_shape=[jax.ShapeDtypeStruct((slots, 5, 16, 128), F32), edge, edge, edge, edge],
        in_specs=[pl.BlockSpec(memory_space=SMEM)] + [pl.BlockSpec(memory_space=pl.ANY)] * 3,
        out_specs=[whole] * 5,
        scratch_shapes=[pltpu.VMEM((5,) + rho.shape, F32), pltpu.SemaphoreType.DMA((5,))],
        compiler_params=pltpu.CompilerParams(vmem_limit_bytes=GRANT),
        cost_estimate=pl.CostEstimate(flops=0, bytes_accessed=6 * MIB, transcendentals=0),
        name="pack_rims",
    )(corners, rho, vel, p)


def rates_kernel(bins_ref, table_ref, out_ref):
    for g in range(bins_ref.shape[0] // 8):
        rows = slice(8 * g, 8 * g + 8)
        low = None
        for step in range(2):
            b = bins_ref[rows, :] + step
            line = b // 128
            lane = b - line * 128
            found = [jnp.zeros((8, 128), F32) for _ in range(2)]
            for r in range(16):
                hit = line == r
                for t in range(2):
                    entry = jnp.broadcast_to(table_ref[t, r : r + 1, :], (8, 128))
                    value = jnp.take_along_axis(entry, lane, axis=1, mode="promise_in_bounds")
                    found[t] = jnp.where(hit, value, found[t])
            for t in range(2):
                entry = found[t] if step == 0 else found[t] - low[t]
                out_ref[2 * t + step, rows, :] = STEP * entry
            low = found


def look_up(bins, tables):
    whole = pl.BlockSpec(memory_space=VMEM)
    return pl.pallas_call(
        rates_kernel,
        out_shape=jax.ShapeDtypeStruct((4,) + bins.shape, F32),
        in_specs=[whole, whole],
        out_specs=whole,
        cost_estimate=pl.CostEstimate(flops=MIB, bytes_accessed=MIB, transcendentals=0),
        name="rate_lookup",
    )(bins, tables)


PITCH = 48
LOW = 8


def coarse_kernel(
    corner_ref, rho_ref, vel_ref, p_ref, xlo_ref, xhi_ref, ylo_ref, yhi_ref, rate_ref,
    out_ref, cell_ref, fx_ref, fy_ref,
):
    width = 32
    fields = [rho_ref, vel_ref.at[0], vel_ref.at[1], vel_ref.at[2], p_ref]

    def keep(prim, index):
        for n, v in enumerate(prim):
            cell_ref[n, index, :] = v
        cell_ref[5, index, :] = sound_of(prim[4], prim[0])

    def fill(x, carry):
        for q in range(4):
            rows = pl.ds(x * width + 8 * q, 8)
            keep([f[rows, :] for f in fields], pl.ds((x + 1) * PITCH + LOW + 8 * q, 8))
        return carry

    lax.fori_loop(0, width, fill, 0)
    for q in range(4):
        rows = slice(8 * q, 8 * q + 8)
        keep([xlo_ref[c, rows, :] for c in range(5)], pl.ds(LOW + 8 * q, 8))
        keep([xhi_ref[c, rows, :] for c in range(5)], pl.ds(33 * PITCH + LOW + 8 * q, 8))
        first = (8 * q + 1) * PITCH + LOW
        keep([ylo_ref[c, rows, :] for c in range(5)], pl.ds(first - 1, 8, stride=PITCH))
        keep([yhi_ref[c, rows, :] for c in range(5)], pl.ds(first + width, 8, stride=PITCH))

    def fetch(row):
        return again(*[cell_ref[n, pl.ds(row, 8), :] for n in range(6)])

    def step(x, carry):
        result = []
        for q in range(4):
            below = carry[5 * q : 5 * q + 5]
            row = (x + 1) * PITCH + LOW + 8 * q
            here = fetch(row)
            above = twice_flux(directed(here, 0), directed(fetch(row + PITCH), 0))
            y_here = directed(here, 1)
            y_high = twice_flux(y_here, directed(fetch(row + 1), 1))
            y_low = twice_flux(directed(fetch(row - 1), 1), y_here)
            z_high = twice_flux(directed(here, 2), directed(shifted(here, 127, 1), 2))
            rates = [lane_pick(rate_ref[t, 16 + 8 * q : 24 + 8 * q, :], x) for t in range(4)]
            rho = here["amounts"][0]
            gain = source_term(rho, here["p"] / (rho + here["p"]), rates)
            flat = pl.ds(x * width + 8 * q, 8)
            for c in range(5):
                change = (
                    (above[c] - below[c])
                    + (y_high[c] - y_low[c])
                    + (z_high[c] - pltpu.roll(z_high[c], 1, 1))
                )
                value = here["amounts"][c] - HALF * change
                if c == 4:
                    value = value + gain
                out_ref[c, flat, :] = value
                fx_ref[c, flat, :] = above[c]
                fy_ref[c, flat, :] = y_high[c]
            result += above
        return tuple(result)

    first = []
    for q in range(4):
        row = LOW + 8 * q
        first += twice_flux(directed(fetch(row), 0), directed(fetch(row + PITCH), 0))
    lax.fori_loop(0, width, step, tuple(first))

    def reflux(s, carry):
        base = corner_ref[s]

        @pl.when(base >= 0)
        def _():
            places = (
                (pl.ds(base - width, 4), pl.ds(base - width, 4), fx_ref, HALF),
                (
                    pl.ds(base + FOOT * width, 4),
                    pl.ds(base + (FOOT - 1) * width, 4),
                    fx_ref,
                    -HALF,
                ),
                (
                    pl.ds(base - 1, 4, stride=width),
                    pl.ds(base - 1, 4, stride=width),
                    fy_ref,
                    HALF,
                ),
                (
                    pl.ds(base + FOOT, 4, stride=width),
                    pl.ds(base + FOOT - 1, 4, stride=width),
                    fy_ref,
                    -HALF,
                ),
            )
            values = [
                [out_ref[c, a, :] + w * f[c, b, :] for a, b, f, w in places] for c in range(5)
            ]
            for c in range(5):
                for n in range(4):
                    out_ref[c, places[n][0], :] = values[c][n]

        return carry

    lax.fori_loop(0, corner_ref.shape[0], reflux, 0)


def coarse_step(corners, rho, vel, p, xlo, xhi, ylo, yhi, rates):
    whole = pl.BlockSpec(memory_space=VMEM)
    cells = rho.shape[0]
    return pl.pallas_call(
        coarse_kernel,
        out_shape=jax.ShapeDtypeStruct((5, cells, 128), F32),
        in_specs=[pl.BlockSpec(memory_space=SMEM)] + [whole] * 8,
        out_specs=whole,
        scratch_shapes=[
            pltpu.VMEM((6, 34 * PITCH, 128), F32),
            pltpu.VMEM((5, cells, 128), F32),
            pltpu.VMEM((5, cells, 128), F32),
        ],
        compiler_params=pltpu.CompilerParams(vmem_limit_bytes=32 * MIB),
        cost_estimate=pl.CostEstimate(
            flops=300 * cells * 128, bytes_accessed=30 * MIB, transcendentals=0
        ),
        name="coarse_step",
    )(corners, rho, vel, p, xlo, xhi, ylo, yhi, rates)


def take_lanes(tile, index):
    return jnp.take_along_axis(tile, index, axis=1, mode="promise_in_bounds")


def fold(even, odd):
    row = lax.broadcasted_iota(jnp.int32, (8, 128), 0)
    lane = lax.broadcasted_iota(jnp.int32, (8, 128), 1)
    halves = []
    for h in range(2):
        a, b = even[:, 128 * h : 128 * h + 128], odd[:, 128 * h : 128 * h + 128]
        a = a + pltpu.roll(a, 7, 0)
        b = b + pltpu.roll(b, 1, 0)
        m = jnp.where(row % 2 == 0, a, b)
        halves.append(m + pltpu.roll(m, 127 if h == 0 else 1, 1))
    mixed = jnp.where(lane % 2 == 0, halves[0], halves[1])
    return take_lanes(mixed, jnp.where(lane < 64, 2 * lane, 2 * lane - 127))


def patch_update(prim_refs, p_index, rates_at, faces, emit, on_plane=None):
    row = lax.broadcasted_iota(jnp.int32, (8, 256), 0)

    def plane(i):
        return [f[p_index, 8 * i : 8 * i + 8, :] for f in prim_refs]

    prim = plane(0)
    if on_plane is not None:
        on_plane(0, prim)
    here = derive(prim)
    below = None if faces is None else [faces(c, 0, slice(0, 8)) for c in range(5)]
    for i in range(8):
        if i < 7:
            prim = plane(i + 1)
            if on_plane is not None:
                on_plane(i + 1, prim)
            after = derive(prim)
            above = twice_flux(directed(here, 0), directed(after, 0))
        else:
            after = None
            above = None if faces is None else [faces(c, 1, slice(0, 8)) for c in range(5)]
        y_here = directed(here, 1)
        y_flux = twice_flux(y_here, directed(shifted(here, 7, 0), 1))
        z_here = directed(here, 2)
        z_flux = twice_flux(z_here, directed(shifted(here, 255, 1), 2))
        gain = source_term(here["amounts"][0], here["share"], rates_at(i))
        result = []
        for c in range(5):
            if faces is None:
                y_high, y_low = 0.0, 0.0
            else:
                y_high = jnp.broadcast_to(faces(c, 3, slice(i, i + 1)), (8, 256))
                y_low = jnp.broadcast_to(faces(c, 2, slice(i, i + 1)), (8, 256))
            change = jnp.where(row == 7, y_high, y_flux[c]) - jnp.where(
                row == 0, y_low, pltpu.roll(y_flux[c], 1, 0)
            )
            change = change + (z_flux[c] - pltpu.roll(z_flux[c], 1, 1))
            if above is not None:
                change = change + above[c]
            if below is not None:
                change = change - below[c]
            value = here["amounts"][c] - STEP * change
            if c == 4:
                value = value + gain
            result.append(value)
        emit(i, result)
        here, below = after, above


def rates_reader(rate_ref, patch):
    half = patch // 16
    start = pl.multiple_of(8 * half, 8)
    shift = 128 - 8 * (patch - 16 * half)
    tiles = [pltpu.roll(rate_ref[t, pl.ds(start, 8), :], shift, 1) for t in range(4)]

    def rates_at(i):
        return [jnp.broadcast_to(v[:, i : i + 1], (8, 256)) for v in tiles]

    return rates_at


PER = 4


def open_kernel(
    slot_ref, rho_ref, ux_ref, uy_ref, uz_ref, p_ref, rate_ref, mean_ref, edge_ref
):
    refs = [rho_ref, ux_ref.at[0], uy_ref.at[0], uz_ref.at[0], p_ref]

    def one(n, carry):
        patch = pl.program_id(0) * PER + n
        slot = slot_ref[patch]

        def on_plane(i, prim):
            for c in range(5):
                if i == 0:
                    edge_ref[n, c, 0] = prim[c]
                if i == 7:
                    edge_ref[n, c, 1] = prim[c]
                edge_ref[n, c, 2, i : i + 1, :] = prim[c][0:1, :]
                edge_ref[n, c, 3, i : i + 1, :] = prim[c][7:8, :]

        held = {}

        def emit(i, result):
            for c in range(5):
                at = (i // 2, c)
                held[at] = result[c] if i % 2 == 0 else held[at] + result[c]
                if i % 4 == 3:
                    value = fold(held.pop((i // 2 - 1, c)), held.pop(at))
                    mean_ref[slot, c, 8 * (i // 4) : 8 * (i // 4) + 8, :] = 0.125 * value

        patch_update(refs, n, rates_reader(rate_ref, patch), None, emit, on_plane)
        return carry

    lax.fori_loop(0, PER, one, 0)


def patch_specs(extra):
    one = pl.BlockSpec((PER, 64, 256), lambda i: (i, 0, 0))
    speed = [pl.BlockSpec((1, PER, 64, 256), lambda i, d=d: (d, i, 0, 0)) for d in range(3)]
    return [pl.BlockSpec(memory_space=SMEM)] * extra + [one] + speed + [one]


def open_patches(slot, rho, vel, p, rates, slots):
    count = rho.shape[0]
    return pl.pallas_call(
        open_kernel,
        grid=(count // PER,),
        out_shape=[
            jax.ShapeDtypeStruct((slots, 5, 32, 128), F32),
            jax.ShapeDtypeStruct((count, 5, 4, 8, 256), F32),
        ],
        in_specs=patch_specs(1) + [pl.BlockSpec(memory_space=VMEM)],
        out_specs=[
            pl.BlockSpec((slots, 5, 16, 128), lambda i: (0, 0, 0, 0)),
            pl.BlockSpec((PER, 5, 4, 8, 256), lambda i: (i, 0, 0, 0, 0)),
        ],
        compiler_params=pltpu.CompilerParams(vmem_limit_bytes=GRANT),
        cost_estimate=pl.CostEstimate(
            flops=250 * count * 64 * 256, bytes_accessed=18 * MIB, transcendentals=0
        ),
        name="open_patches",
    )(slot, rho, vel, vel, vel, p, rates)


BATCH = 4


def side_fluxes(rim, edge, ghost_ref):
    lane = lax.broadcasted_iota(jnp.int32, (16, 128), 1) // 2
    coarse = list(rim)
    coarse.append(sound_of(coarse[4], coarse[0]))
    for c in range(6):
        for h in range(2):
            wide = take_lanes(coarse[c], lane + 64 * h)
            ghost_ref[c, h, pl.ds(0, 16, stride=2), :] = wide
            ghost_ref[c, h, pl.ds(1, 16, stride=2), :] = wide
    sides = []
    for side in range(4):
        rows = slice(8 * side, 8 * side + 8)
        outer = [
            jnp.concatenate([ghost_ref[c, 0, rows, :], ghost_ref[c, 1, rows, :]], axis=1)
            for c in range(6)
        ]
        d = side // 2
        ghost = directed(again(*outer), d)
        prim = edge(side)
        inner = directed(again(*prim, sound_of(prim[4], prim[0])), d)
        sides.append(twice_flux(ghost, inner) if side % 2 == 0 else twice_flux(inner, ghost))
    return sides


def face_kernel(slot_ref, rim_ref, edge_ref, _, sum_ref, ghost_ref):
    first = pl.program_id(0) * BATCH
    for n in range(BATCH):
        slot = slot_ref[first + n]
        sides = side_fluxes(
            [rim_ref[slot, c] for c in range(5)],
            lambda side, n=n: [edge_ref[n, c, side] for c in range(5)],
            ghost_ref.at[n],
        )
        for c in range(5):
            for d in range(2):
                value = fold(sides[2 * d][c], sides[2 * d + 1][c])
                sum_ref[slot, c, 8 * d : 8 * d + 8, :] = (0.125 * STEP) * value


def face_fluxes(slot, rims, edges, buffer):
    count = edges.shape[0]
    slots = rims.shape[0]
    return pl.pallas_call(
        face_kernel,
        grid=(count // BATCH,),
        out_shape=jax.ShapeDtypeStruct(buffer.shape, F32),
        in_specs=[
            pl.BlockSpec(memory_space=SMEM),
            pl.BlockSpec((slots, 5, 16, 128), lambda i: (0, 0, 0, 0)),
            pl.BlockSpec((BATCH, 5, 4, 8, 256), lambda i: (i, 0, 0, 0, 0)),
            pl.BlockSpec(memory_space=pl.ANY),
        ],
        out_specs=pl.BlockSpec((slots, 5, 16, 128), lambda i: (0, 0, 1, 0)),
        input_output_aliases={3: 0},
        scratch_shapes=[pltpu.VMEM((BATCH, 6, 2, 32, 128), F32)],
        compiler_params=pltpu.CompilerParams(vmem_limit_bytes=GRANT),
        cost_estimate=pl.CostEstimate(
            flops=100 * count * 32 * 256, bytes_accessed=11 * MIB, transcendentals=0
        ),
        name="face_fluxes",
    )(slot, rims, edges, buffer)


def close_kernel(
    slot_ref, rho_ref, ux_ref, uy_ref, uz_ref, p_ref, rate_ref, rim_ref, edge_ref,
    out_ref, ghost_ref, rows_ref,
):
    refs = [rho_ref, ux_ref.at[0], uy_ref.at[0], uz_ref.at[0], p_ref]

    def one(n, carry):
        patch = pl.program_id(0) * PER + n
        slot = slot_ref[patch]
        sides = side_fluxes(
            [rim_ref[slot, c] for c in range(5)],
            lambda side: [edge_ref[n, c, side] for c in range(5)],
            ghost_ref,
        )
        for c in range(5):
            for d in range(2):
                rows_ref[c, d] = sides[2 + d][c]

        def faces(c, side, rows):
            return sides[side][c] if side < 2 else rows_ref[c, side - 2, rows, :]

        def emit(i, result):
            for c in range(5):
                out_ref[c, n, 8 * i : 8 * i + 8, :] = result[c]

        patch_update(refs, n, rates_reader(rate_ref, patch), faces, emit)
        return carry

    lax.fori_loop(0, PER, one, 0)


def close_patches(slot, rho, vel, p, rates, rims, edges):
    count = rho.shape[0]
    return pl.pallas_call(
        close_kernel,
        grid=(count // PER,),
        out_shape=jax.ShapeDtypeStruct((5,) + rho.shape, F32),
        in_specs=patch_specs(1)
        + [
            pl.BlockSpec(memory_space=VMEM),
            pl.BlockSpec(rims.shape, lambda i: (0, 0, 0, 0)),
            pl.BlockSpec((PER, 5, 4, 8, 256), lambda i: (i, 0, 0, 0, 0)),
        ],
        out_specs=pl.BlockSpec((5, PER, 64, 256), lambda i: (0, i, 0, 0)),
        scratch_shapes=[
            pltpu.VMEM((6, 2, 32, 128), F32),
            pltpu.VMEM((5, 2, 8, 256), F32),
        ],
        compiler_params=pltpu.CompilerParams(vmem_limit_bytes=GRANT),
        cost_estimate=pl.CostEstimate(
            flops=250 * count * 64 * 256, bytes_accessed=29 * MIB, transcendentals=0
        ),
        name="close_patches",
    )(slot, rho, vel, vel, vel, p, rates, rims, edges)


def merge_kernel(corner_ref, base_ref, got_ref, out_ref):
    width = 32
    out_ref[...] = base_ref[...]
    row = lax.broadcasted_iota(jnp.int32, (4, 128), 0)

    def one(s, carry):
        base = corner_ref[s]

        @pl.when(base >= 0)
        def _():
            rims = (
                pl.ds(base - width, 4),
                pl.ds(base + FOOT * width, 4),
                pl.ds(base - 1, 4, stride=width),
                pl.ds(base + FOOT, 4, stride=width),
            )
            result = []
            for c in range(5):
                flux = [
                    got_ref[s, c, pl.ds(16 + 8 * (n // 2) + n % 2, 4, stride=2), :]
                    for n in range(4)
                ]
                rim = [out_ref[c, at, :] for at in rims]
                rim = [rim[n] + flux[n] if n % 2 else rim[n] - flux[n] for n in range(4)]
                foot = []
                for i in range(4):
                    v = got_ref[s, c, pl.ds(8 * (i // 2) + i % 2, 4, stride=2), :]
                    if i == 0:
                        v = v + flux[0]
                    if i == 3:
                        v = v - flux[1]
                    low = jnp.broadcast_to(flux[2][i : i + 1, :], (4, 128))
                    high = jnp.broadcast_to(flux[3][i : i + 1, :], (4, 128))
                    v = v + jnp.where(row == 0, low, 0.0) - jnp.where(row == 3, high, 0.0)
                    foot.append(v)
                result.append((rim, foot))
            for c in range(5):
                rim, foot = result[c]
                for at, v in zip(rims, rim):
                    out_ref[c, at, :] = v
                for i in range(4):
                    out_ref[c, pl.ds(base + i * width, 4), :] = foot[i]

        return carry

    lax.fori_loop(0, corner_ref.shape[0], one, 0)


def merge(corners, base, got):
    whole = pl.BlockSpec(memory_space=VMEM)
    return pl.pallas_call(
        merge_kernel,
        out_shape=jax.ShapeDtypeStruct(base.shape, F32),
        in_specs=[pl.BlockSpec(memory_space=SMEM), whole, whole],
        out_specs=whole,
        compiler_params=pltpu.CompilerParams(vmem_limit_bytes=24 * MIB),
        cost_estimate=pl.CostEstimate(flops=MIB, bytes_accessed=11 * MIB, transcendentals=0),
        name="merge_patches",
    )(corners, base, got)


def exchange(buffer, groups):
    shape = buffer.shape
    rows = buffer.size // (groups * 128)
    moved = lax.all_to_all(
        buffer.reshape(groups, rows, 128), "yz", split_axis=0, concat_axis=0, tiled=True
    )
    return moved.reshape(shape)


def local(
    coarse_density,
    coarse_velocity,
    coarse_pressure,
    coarse_bins,
    fine_density,
    fine_velocity,
    fine_pressure,
    fine_bins,
    patch_host,
    patch_spot,
    heat_rate,
    cool_rate,
):
    groups = lax.axis_size("yz")
    rows = lax.axis_size("gx")
    gx = lax.axis_index("gx")
    me = lax.axis_index("yz")
    count = fine_density.shape[0]
    slots = CAP * groups

    total = groups * count
    hosts = lax.dynamic_slice_in_dim(patch_host, gx * total, total).reshape(groups, count)
    places = lax.dynamic_slice_in_dim(patch_spot, gx * total, total).reshape(groups, count)
    corner = (1 + SIDE * (places // 6)) * 32 + (1 + SIDE * (places % 6))
    order = jnp.arange(count, dtype=jnp.int32)
    earlier = order[None, :] < order[:, None]
    mine = hosts == me
    rank = jnp.sum((mine[:, None, :] & earlier[None]).astype(jnp.int32), axis=2)
    corners = jnp.stack(
        [jnp.max(jnp.where(mine & (rank == r), corner, -1), axis=1) for r in range(CAP)], axis=1
    ).reshape(slots)
    own = lax.dynamic_slice_in_dim(patch_host, (gx * groups + me) * count, count)
    own_rank = jnp.sum(((own[:, None] == own[None, :]) & earlier).astype(jnp.int32), axis=1)
    slot = CAP * own + own_rank

    rho = coarse_density.reshape(-1, 128)
    vel = coarse_velocity.reshape(3, -1, 128)
    press = coarse_pressure.reshape(-1, 128)
    rims, x_first, x_last, y_first, y_last = pack(corners, rho, vel, press, slots)
    arrived = exchange(rims, groups)

    up_x = [(i, (i + 1) % rows) for i in range(rows)]
    down_x = [((i + 1) % rows, i) for i in range(rows)]
    up_y = [(i, (i + 1) % groups) for i in range(groups)]
    down_y = [((i + 1) % groups, i) for i in range(groups)]
    x_low = lax.ppermute(x_last, "gx", up_x)
    x_high = lax.ppermute(x_first, "gx", down_x)
    y_low = lax.ppermute(y_last, "yz", up_y)
    y_high = lax.ppermute(y_first, "yz", down_y)

    fine_columns = fine_bins.reshape(2, 16, 8, 8).transpose(0, 3, 1, 2).reshape(16, 128)
    coarse_columns = jnp.pad(coarse_bins.T, ((0, 0), (0, 128 - coarse_bins.shape[0])))
    tables = jnp.pad(jnp.stack([heat_rate, cool_rate]), ((0, 0), (0, 48))).reshape(2, 16, 128)
    rates = look_up(jnp.concatenate([fine_columns, coarse_columns], axis=0), tables)

    f_rho = fine_density.reshape(count, 64, 256)
    f_vel = fine_velocity.reshape(3, count, 64, 256)
    f_press = fine_pressure.reshape(count, 64, 256)
    means, edges = open_patches(slot, f_rho, f_vel, f_press, rates, slots)
    sums = face_fluxes(slot, arrived, edges, means)
    sums, x_low, x_high, y_low, y_high = lax.optimization_barrier(
        (sums, x_low, x_high, y_low, y_high)
    )
    got = exchange(sums, groups)
    base = coarse_step(corners, rho, vel, press, x_low, x_high, y_low, y_high, rates)
    fine_new = close_patches(slot, f_rho, f_vel, f_press, rates, arrived, edges)
    coarse_new = merge(corners, base, got)
    return (
        coarse_new.reshape((5,) + coarse_density.shape),
        fine_new.reshape((5,) + fine_density.shape),
    )


def solution(mesh):
    placed = (
        P("gx", "yz", None),
        P(None, "gx", "yz", None),
        P("gx", "yz", None),
        P("gx", "yz"),
        P(("gx", "yz"), None, None, None),
        P(None, ("gx", "yz"), None, None, None),
        P(("gx", "yz"), None, None, None),
        P(("gx", "yz"), None, None),
        P(),
        P(),
        P(),
        P(),
    )
    return jax.shard_map(
        local,
        mesh=mesh,
        in_specs=placed,
        out_specs=(P(None, "gx", "yz", None), P(None, ("gx", "yz"), None, None, None)),
        check_vma=False,
    )
```

```python
import functools

import jax
import jax.numpy as jnp
from jax import lax
from jax.experimental import pallas as pl
from jax.experimental.pallas import tpu as pltpu
from jax.sharding import PartitionSpec as P

GAMMA = 5.0 / 3.0
STEP = 0.02
HALF = 0.5 * STEP
FOOT = 4
SIDE = 5
CAP = 2
F32 = jnp.float32
VMEM = pltpu.VMEM
SMEM = pltpu.SMEM
MIB = 1024 * 1024
GRANT = 56 * MIB


def conserve(rho, ux, uy, uz, p):
    mx, my, mz = rho * ux, rho * uy, rho * uz
    xx, yy, zz = mx * ux, my * uy, mz * uz
    energy = 1.5 * p + 0.5 * (xx + yy + zz)
    return {
        "amounts": (rho, mx, my, mz, energy),
        "speed": (ux, uy, uz),
        "p": p,
        "square": (xx, yy, zz),
        "cross": {},
    }


def sound_of(p, rho):
    square = GAMMA * (p / rho)
    return square * lax.rsqrt(square)


def derive(prim):
    rho, p = prim[0], prim[4]
    both = rho + p
    common = p / (rho * both)
    square = GAMMA * (common * both)
    cell = conserve(*prim)
    cell["sound"] = square * lax.rsqrt(square)
    cell["share"] = common * rho
    return cell


def again(rho, ux, uy, uz, p, sound):
    cell = conserve(rho, ux, uy, uz, p)
    cell["sound"] = sound
    return cell


def directed(cell, d):
    amounts, p = cell["amounts"], cell["p"]
    u = cell["speed"][d]
    flux = [amounts[1 + d]]
    for k in range(3):
        if k == d:
            flux.append(cell["square"][d] + p)
            continue
        pair = (min(k, d), max(k, d))
        if pair not in cell["cross"]:
            cell["cross"][pair] = amounts[1 + pair[0]] * cell["speed"][pair[1]]
        flux.append(cell["cross"][pair])
    flux.append((amounts[4] + p) * u)
    return (amounts, flux, jnp.abs(u) + cell["sound"])


def twice_flux(left, right):
    fastest = jnp.maximum(left[2], right[2])
    return [
        (left[1][c] + right[1][c]) - fastest * (right[0][c] - left[0][c]) for c in range(5)
    ]


def shifted(cell, shift, axis):
    rho, p = cell["amounts"][0], cell["p"]
    values = (rho,) + cell["speed"] + (p, cell["sound"])
    return again(*[pltpu.roll(v, shift, axis) for v in values])


def source_term(rho, share, rates):
    heat, heat_slope, cool, cool_slope = rates
    return rho * ((heat + share * heat_slope) - rho * (cool + share * cool_slope))


def lane_pick(tile, lane):
    index = jnp.full((8, 128), lane, jnp.int32)
    return jnp.take_along_axis(tile, index, axis=1, mode="promise_in_bounds")


def plan_places(place_ref, host_ref, spot_ref, corner_ref, slot_ref):
    gx, me = place_ref[0], place_ref[1]
    rows = pl.ds(pl.multiple_of(8 * gx, 8), 8)
    hosts, spots = host_ref[rows, :], spot_ref[rows, :]
    lane = lax.broadcasted_iota(jnp.int32, (8, 128), 1)
    row = lax.broadcasted_iota(jnp.int32, (8, 128), 0)
    place_x = (spots * 43) >> 8
    corner = (1 + SIDE * place_x) * 32 + 1 + SIDE * (spots - 6 * place_x)
    key = jnp.where(hosts == me, lane * 1024 + corner, -1)
    table = jnp.full((8, 128), -1, jnp.int32)
    far = 1 << 20
    for q in range(4):
        inside = (lane // 32 == q) & (key >= 0)
        last = jnp.max(jnp.where(inside, key, -1), axis=1, keepdims=True)
        first = jnp.min(jnp.where(inside, key, far), axis=1, keepdims=True)
        none = last < 0
        single = none | (first == last)
        table = jnp.where(lane == 2 * q, jnp.where(none, -1, first & 1023), table)
        table = jnp.where(lane == 2 * q + 1, jnp.where(single, -1, last & 1023), table)
    corner_ref[...] = table
    own = jnp.sum(jnp.where(row == me // 4, hosts, 0), axis=0, keepdims=True)
    own = pltpu.roll(jnp.broadcast_to(own, (8, 128)), lax.rem(128 - 32 * lax.rem(me, 4), 128), 1)
    own = jnp.broadcast_to(own[0:1, :], (32, 128))
    lane = lax.broadcasted_iota(jnp.int32, (32, 128), 1)
    row = lax.broadcasted_iota(jnp.int32, (32, 128), 0)
    mine = jnp.sum(jnp.where(lane == row, own, 0), axis=1, keepdims=True)
    rank = jnp.sum(jnp.where((own == mine) & (lane < row), 1, 0), axis=1, keepdims=True)
    slot_ref[...] = jnp.broadcast_to(CAP * mine + rank, (32, 128))


def corner_at(corner_ref, s):
    line = s // 8
    return corner_ref[line, s - 8 * line]


def pack_kernel(
    place_ref, host_ref, spot_ref, rho_hbm, vel_hbm, p_hbm,
    rim_ref, xa_ref, xb_ref, ya_ref, yb_ref, corner_ref, slot_ref,
    cell_ref, table_ref, sem, table_sem,
):
    sources = [rho_hbm, vel_hbm.at[0], vel_hbm.at[1], vel_hbm.at[2], p_hbm]
    copies = [pltpu.make_async_copy(f, cell_ref.at[c], sem.at[c]) for c, f in enumerate(sources)]
    for copy in copies:
        copy.start()
    plan_places(place_ref, host_ref, spot_ref, corner_ref, slot_ref)
    move = pltpu.make_async_copy(corner_ref, table_ref, table_sem)
    move.start()
    move.wait()
    for copy in copies:
        copy.wait()
    fields = [cell_ref.at[c] for c in range(5)]
    width = 32
    rows = cell_ref.shape[1]

    def one(s, carry):
        base = corner_at(table_ref, s)

        @pl.when(base >= 0)
        def _():
            for c, f in enumerate(fields):
                rim_ref[s, c, 0:4, :] = f[pl.ds(base - width, 4), :]
                rim_ref[s, c, 4:8, :] = f[pl.ds(base + FOOT * width, 4), :]
                rim_ref[s, c, 8:12, :] = f[pl.ds(base - 1, 4, stride=width), :]
                rim_ref[s, c, 12:16, :] = f[pl.ds(base + FOOT, 4, stride=width), :]

        return carry

    lax.fori_loop(0, rim_ref.shape[0], one, 0)
    for c, f in enumerate(fields):
        xa_ref[c] = f[0:width, :]
        xb_ref[c] = f[rows - width : rows, :]
        ya_ref[c] = f[pl.ds(0, width, stride=width), :]
        yb_ref[c] = f[pl.ds(width - 1, width, stride=width), :]


def pack(place, hosts, spots, rho, vel, p, slots):
    whole = pl.BlockSpec(memory_space=VMEM)
    edge = jax.ShapeDtypeStruct((5, 32, 128), F32)
    return pl.pallas_call(
        pack_kernel,
        out_shape=[jax.ShapeDtypeStruct((slots, 5, 16, 128), F32), edge, edge, edge, edge]
        + [jax.ShapeDtypeStruct((8, 128), jnp.int32), jax.ShapeDtypeStruct((32, 128), jnp.int32)],
        in_specs=[pl.BlockSpec(memory_space=SMEM), whole, whole]
        + [pl.BlockSpec(memory_space=pl.ANY)] * 3,
        out_specs=[whole] * 7,
        scratch_shapes=[
            pltpu.VMEM((5,) + rho.shape, F32),
            pltpu.SMEM((8, 128), jnp.int32),
            pltpu.SemaphoreType.DMA((5,)),
            pltpu.SemaphoreType.DMA,
        ],
        compiler_params=pltpu.CompilerParams(vmem_limit_bytes=GRANT),
        cost_estimate=pl.CostEstimate(flops=0, bytes_accessed=6 * MIB, transcendentals=0),
        name="pack_rims",
    )(place, hosts, spots, rho, vel, p)


def rates_kernel(bins_ref, table_ref, out_ref):
    for g in range(bins_ref.shape[0] // 8):
        rows = slice(8 * g, 8 * g + 8)
        low = None
        for step in range(2):
            b = bins_ref[rows, :] + step
            line = b // 128
            lane = b - line * 128
            found = [jnp.zeros((8, 128), F32) for _ in range(2)]
            for r in range(16):
                hit = line == r
                for t in range(2):
                    entry = jnp.broadcast_to(table_ref[t, r : r + 1, :], (8, 128))
                    value = jnp.take_along_axis(entry, lane, axis=1, mode="promise_in_bounds")
                    found[t] = jnp.where(hit, value, found[t])
            for t in range(2):
                entry = found[t] if step == 0 else found[t] - low[t]
                out_ref[2 * t + step, rows, :] = STEP * entry
            low = found


def look_up(bins, tables):
    whole = pl.BlockSpec(memory_space=VMEM)
    return pl.pallas_call(
        rates_kernel,
        out_shape=jax.ShapeDtypeStruct((4,) + bins.shape, F32),
        in_specs=[whole, whole],
        out_specs=whole,
        cost_estimate=pl.CostEstimate(flops=MIB, bytes_accessed=MIB, transcendentals=0),
        name="rate_lookup",
    )(bins, tables)


PITCH = 48
LOW = 8


def coarse_kernel(
    corner_ref, rho_ref, vel_ref, p_ref, xlo_ref, xhi_ref, ylo_ref, yhi_ref, rate_ref,
    out_ref, cell_ref, fx_ref, fy_ref,
):
    width = 32
    fields = [rho_ref, vel_ref.at[0], vel_ref.at[1], vel_ref.at[2], p_ref]

    def keep(prim, index):
        for n, v in enumerate(prim):
            cell_ref[n, index, :] = v
        cell_ref[5, index, :] = sound_of(prim[4], prim[0])

    def fill(x, carry):
        for q in range(4):
            rows = pl.ds(x * width + 8 * q, 8)
            keep([f[rows, :] for f in fields], pl.ds((x + 1) * PITCH + LOW + 8 * q, 8))
        return carry

    lax.fori_loop(0, width, fill, 0)
    for q in range(4):
        rows = slice(8 * q, 8 * q + 8)
        keep([xlo_ref[c, rows, :] for c in range(5)], pl.ds(LOW + 8 * q, 8))
        keep([xhi_ref[c, rows, :] for c in range(5)], pl.ds(33 * PITCH + LOW + 8 * q, 8))
        first = (8 * q + 1) * PITCH + LOW
        keep([ylo_ref[c, rows, :] for c in range(5)], pl.ds(first - 1, 8, stride=PITCH))
        keep([yhi_ref[c, rows, :] for c in range(5)], pl.ds(first + width, 8, stride=PITCH))

    def fetch(row):
        return again(*[cell_ref[n, pl.ds(row, 8), :] for n in range(6)])

    def step(x, carry):
        result = []
        for q in range(4):
            below = carry[5 * q : 5 * q + 5]
            row = (x + 1) * PITCH + LOW + 8 * q
            here = fetch(row)
            above = twice_flux(directed(here, 0), directed(fetch(row + PITCH), 0))
            y_here = directed(here, 1)
            y_high = twice_flux(y_here, directed(fetch(row + 1), 1))
            y_low = twice_flux(directed(fetch(row - 1), 1), y_here)
            z_high = twice_flux(directed(here, 2), directed(shifted(here, 127, 1), 2))
            rates = [lane_pick(rate_ref[t, 16 + 8 * q : 24 + 8 * q, :], x) for t in range(4)]
            rho = here["amounts"][0]
            gain = source_term(rho, here["p"] / (rho + here["p"]), rates)
            flat = pl.ds(x * width + 8 * q, 8)
            for c in range(5):
                change = (
                    (above[c] - below[c])
                    + (y_high[c] - y_low[c])
                    + (z_high[c] - pltpu.roll(z_high[c], 1, 1))
                )
                value = here["amounts"][c] - HALF * change
                if c == 4:
                    value = value + gain
                out_ref[c, flat, :] = value
                fx_ref[c, flat, :] = above[c]
                fy_ref[c, flat, :] = y_high[c]
            result += above
        return tuple(result)

    first = []
    for q in range(4):
        row = LOW + 8 * q
        first += twice_flux(directed(fetch(row), 0), directed(fetch(row + PITCH), 0))
    lax.fori_loop(0, width, step, tuple(first))

    def reflux(s, carry):
        base = corner_at(corner_ref, s)

        @pl.when(base >= 0)
        def _():
            places = (
                (pl.ds(base - width, 4), pl.ds(base - width, 4), fx_ref, HALF),
                (
                    pl.ds(base + FOOT * width, 4),
                    pl.ds(base + (FOOT - 1) * width, 4),
                    fx_ref,
                    -HALF,
                ),
                (
                    pl.ds(base - 1, 4, stride=width),
                    pl.ds(base - 1, 4, stride=width),
                    fy_ref,
                    HALF,
                ),
                (
                    pl.ds(base + FOOT, 4, stride=width),
                    pl.ds(base + FOOT - 1, 4, stride=width),
                    fy_ref,
                    -HALF,
                ),
            )
            values = [
                [out_ref[c, a, :] + w * f[c, b, :] for a, b, f, w in places] for c in range(5)
            ]
            for c in range(5):
                for n in range(4):
                    out_ref[c, places[n][0], :] = values[c][n]

        return carry

    lax.fori_loop(0, 8 * corner_ref.shape[0], reflux, 0)


def coarse_step(corners, rho, vel, p, xlo, xhi, ylo, yhi, rates):
    whole = pl.BlockSpec(memory_space=VMEM)
    cells = rho.shape[0]
    return pl.pallas_call(
        coarse_kernel,
        out_shape=jax.ShapeDtypeStruct((5, cells, 128), F32),
        in_specs=[pl.BlockSpec(memory_space=SMEM)] + [whole] * 8,
        out_specs=whole,
        scratch_shapes=[
            pltpu.VMEM((6, 34 * PITCH, 128), F32),
            pltpu.VMEM((5, cells, 128), F32),
            pltpu.VMEM((5, cells, 128), F32),
        ],
        compiler_params=pltpu.CompilerParams(vmem_limit_bytes=32 * MIB),
        cost_estimate=pl.CostEstimate(
            flops=300 * cells * 128, bytes_accessed=30 * MIB, transcendentals=0
        ),
        name="coarse_step",
    )(corners, rho, vel, p, xlo, xhi, ylo, yhi, rates)


def take_lanes(tile, index):
    return jnp.take_along_axis(tile, index, axis=1, mode="promise_in_bounds")


def fold(even, odd):
    row = lax.broadcasted_iota(jnp.int32, (8, 128), 0)
    lane = lax.broadcasted_iota(jnp.int32, (8, 128), 1)
    halves = []
    for h in range(2):
        a, b = even[:, 128 * h : 128 * h + 128], odd[:, 128 * h : 128 * h + 128]
        a = a + pltpu.roll(a, 7, 0)
        b = b + pltpu.roll(b, 1, 0)
        m = jnp.where(row % 2 == 0, a, b)
        halves.append(m + pltpu.roll(m, 127 if h == 0 else 1, 1))
    mixed = jnp.where(lane % 2 == 0, halves[0], halves[1])
    return take_lanes(mixed, jnp.where(lane < 64, 2 * lane, 2 * lane - 127))


def patch_update(prim_refs, p_index, rates_at, faces, emit, on_plane=None):
    row = lax.broadcasted_iota(jnp.int32, (8, 256), 0)

    def plane(i):
        return [f[p_index, 8 * i : 8 * i + 8, :] for f in prim_refs]

    prim = plane(0)
    if on_plane is not None:
        on_plane(0, prim)
    here = derive(prim)
    below = None if faces is None else [faces(c, 0, slice(0, 8)) for c in range(5)]
    for i in range(8):
        if i < 7:
            prim = plane(i + 1)
            if on_plane is not None:
                on_plane(i + 1, prim)
            after = derive(prim)
            above = None
            if faces is not None or i % 2 == 1:
                above = twice_flux(directed(here, 0), directed(after, 0))
        else:
            after = None
            above = None if faces is None else [faces(c, 1, slice(0, 8)) for c in range(5)]
        y_here = directed(here, 1)
        y_flux = twice_flux(y_here, directed(shifted(here, 7, 0), 1))
        z_here = directed(here, 2)
        z_flux = twice_flux(z_here, directed(shifted(here, 255, 1), 2))
        gain = source_term(here["amounts"][0], here["share"], rates_at(i))
        result = []
        for c in range(5):
            if faces is None:
                y_high, y_low = 0.0, 0.0
            else:
                y_high = jnp.broadcast_to(faces(c, 3, slice(i, i + 1)), (8, 256))
                y_low = jnp.broadcast_to(faces(c, 2, slice(i, i + 1)), (8, 256))
            change = jnp.where(row == 7, y_high, y_flux[c]) - jnp.where(
                row == 0, y_low, pltpu.roll(y_flux[c], 1, 0)
            )
            change = change + (z_flux[c] - pltpu.roll(z_flux[c], 1, 1))
            if above is not None:
                change = change + above[c]
            if below is not None:
                change = change - below[c]
            value = here["amounts"][c] - STEP * change
            if c == 4:
                value = value + gain
            result.append(value)
        emit(i, result)
        here, below = after, above


def rates_reader(rate_ref, patch):
    half = patch // 16
    start = pl.multiple_of(8 * half, 8)
    shift = 128 - 8 * (patch - 16 * half)
    tiles = [pltpu.roll(rate_ref[t, pl.ds(start, 8), :], shift, 1) for t in range(4)]

    def rates_at(i):
        return [jnp.broadcast_to(v[:, i : i + 1], (8, 256)) for v in tiles]

    return rates_at


PER = 4


def open_kernel(
    slot_ref, rho_ref, ux_ref, uy_ref, uz_ref, p_ref, rate_ref, mean_ref, edge_ref
):
    refs = [rho_ref, ux_ref.at[0], uy_ref.at[0], uz_ref.at[0], p_ref]

    def one(n, carry):
        patch = pl.program_id(0) * PER + n
        slot = slot_ref[patch, 0]

        def on_plane(i, prim):
            for c in range(5):
                if i == 0:
                    edge_ref[n, c, 0] = prim[c]
                if i == 7:
                    edge_ref[n, c, 1] = prim[c]
                edge_ref[n, c, 2, i : i + 1, :] = prim[c][0:1, :]
                edge_ref[n, c, 3, i : i + 1, :] = prim[c][7:8, :]

        held = {}

        def emit(i, result):
            for c in range(5):
                at = (i // 2, c)
                held[at] = result[c] if i % 2 == 0 else held[at] + result[c]
                if i % 4 == 3:
                    value = fold(held.pop((i // 2 - 1, c)), held.pop(at))
                    mean_ref[slot, c, 8 * (i // 4) : 8 * (i // 4) + 8, :] = 0.125 * value

        patch_update(refs, n, rates_reader(rate_ref, patch), None, emit, on_plane)
        return carry

    lax.fori_loop(0, PER, one, 0)


def patch_specs(extra):
    one = pl.BlockSpec((PER, 64, 256), lambda i: (i, 0, 0))
    speed = [pl.BlockSpec((1, PER, 64, 256), lambda i, d=d: (d, i, 0, 0)) for d in range(3)]
    return [pl.BlockSpec(memory_space=SMEM)] * extra + [one] + speed + [one]


def open_patches(slot, rho, vel, p, rates, slots):
    count = rho.shape[0]
    return pl.pallas_call(
        open_kernel,
        grid=(count // PER,),
        out_shape=[
            jax.ShapeDtypeStruct((slots, 5, 32, 128), F32),
            jax.ShapeDtypeStruct((count, 5, 4, 8, 256), F32),
        ],
        in_specs=patch_specs(1) + [pl.BlockSpec(memory_space=VMEM)],
        out_specs=[
            pl.BlockSpec((slots, 5, 16, 128), lambda i: (0, 0, 0, 0)),
            pl.BlockSpec((PER, 5, 4, 8, 256), lambda i: (i, 0, 0, 0, 0)),
        ],
        compiler_params=pltpu.CompilerParams(vmem_limit_bytes=GRANT),
        cost_estimate=pl.CostEstimate(
            flops=250 * count * 64 * 256, bytes_accessed=18 * MIB, transcendentals=0
        ),
        name="open_patches",
    )(slot, rho, vel, vel, vel, p, rates)


BATCH = 4


def side_fluxes(rim, edge, ghost_ref):
    lane = lax.broadcasted_iota(jnp.int32, (16, 128), 1) // 2
    coarse = list(rim)
    coarse.append(sound_of(coarse[4], coarse[0]))
    for c in range(6):
        for h in range(2):
            wide = take_lanes(coarse[c], lane + 64 * h)
            ghost_ref[c, h, pl.ds(0, 16, stride=2), :] = wide
            ghost_ref[c, h, pl.ds(1, 16, stride=2), :] = wide
    sides = []
    for side in range(4):
        rows = slice(8 * side, 8 * side + 8)
        outer = [
            jnp.concatenate([ghost_ref[c, 0, rows, :], ghost_ref[c, 1, rows, :]], axis=1)
            for c in range(6)
        ]
        d = side // 2
        ghost = directed(again(*outer), d)
        prim = edge(side)
        inner = directed(again(*prim, sound_of(prim[4], prim[0])), d)
        sides.append(twice_flux(ghost, inner) if side % 2 == 0 else twice_flux(inner, ghost))
    return sides


def face_kernel(slot_ref, rim_ref, edge_ref, _, sum_ref, ghost_ref):
    first = pl.program_id(0) * BATCH
    for n in range(BATCH):
        slot = slot_ref[first + n, 0]
        sides = side_fluxes(
            [rim_ref[slot, c] for c in range(5)],
            lambda side, n=n: [edge_ref[n, c, side] for c in range(5)],
            ghost_ref.at[n],
        )
        for c in range(5):
            for d in range(2):
                value = fold(sides[2 * d][c], sides[2 * d + 1][c])
                sum_ref[slot, c, 8 * d : 8 * d + 8, :] = (0.125 * STEP) * value


def face_fluxes(slot, rims, edges, buffer):
    count = edges.shape[0]
    slots = rims.shape[0]
    return pl.pallas_call(
        face_kernel,
        grid=(count // BATCH,),
        out_shape=jax.ShapeDtypeStruct(buffer.shape, F32),
        in_specs=[
            pl.BlockSpec(memory_space=SMEM),
            pl.BlockSpec((slots, 5, 16, 128), lambda i: (0, 0, 0, 0)),
            pl.BlockSpec((BATCH, 5, 4, 8, 256), lambda i: (i, 0, 0, 0, 0)),
            pl.BlockSpec(memory_space=pl.ANY),
        ],
        out_specs=pl.BlockSpec((slots, 5, 16, 128), lambda i: (0, 0, 1, 0)),
        input_output_aliases={3: 0},
        scratch_shapes=[pltpu.VMEM((BATCH, 6, 2, 32, 128), F32)],
        compiler_params=pltpu.CompilerParams(vmem_limit_bytes=20 * MIB),
        cost_estimate=pl.CostEstimate(
            flops=100 * count * 32 * 256, bytes_accessed=11 * MIB, transcendentals=0
        ),
        name="face_fluxes",
    )(slot, rims, edges, buffer)


def close_kernel(
    slot_ref, rho_ref, ux_ref, uy_ref, uz_ref, p_ref, rate_ref, rim_ref, edge_ref,
    out_ref, ghost_ref, rows_ref,
):
    refs = [rho_ref, ux_ref.at[0], uy_ref.at[0], uz_ref.at[0], p_ref]

    def one(n, carry):
        patch = pl.program_id(0) * PER + n
        slot = slot_ref[patch, 0]
        sides = side_fluxes(
            [rim_ref[slot, c] for c in range(5)],
            lambda side: [edge_ref[n, c, side] for c in range(5)],
            ghost_ref,
        )
        for c in range(5):
            for d in range(2):
                rows_ref[c, d] = sides[2 + d][c]

        def faces(c, side, rows):
            return sides[side][c] if side < 2 else rows_ref[c, side - 2, rows, :]

        def emit(i, result):
            for c in range(5):
                out_ref[c, n, 8 * i : 8 * i + 8, :] = result[c]

        patch_update(refs, n, rates_reader(rate_ref, patch), faces, emit)
        return carry

    lax.fori_loop(0, PER, one, 0)


def close_patches(slot, rho, vel, p, rates, rims, edges):
    count = rho.shape[0]
    return pl.pallas_call(
        close_kernel,
        grid=(count // PER,),
        out_shape=jax.ShapeDtypeStruct((5,) + rho.shape, F32),
        in_specs=patch_specs(1)
        + [
            pl.BlockSpec(memory_space=VMEM),
            pl.BlockSpec(rims.shape, lambda i: (0, 0, 0, 0)),
            pl.BlockSpec((PER, 5, 4, 8, 256), lambda i: (i, 0, 0, 0, 0)),
        ],
        out_specs=pl.BlockSpec((5, PER, 64, 256), lambda i: (0, i, 0, 0)),
        scratch_shapes=[
            pltpu.VMEM((6, 2, 32, 128), F32),
            pltpu.VMEM((5, 2, 8, 256), F32),
        ],
        compiler_params=pltpu.CompilerParams(vmem_limit_bytes=GRANT),
        cost_estimate=pl.CostEstimate(
            flops=250 * count * 64 * 256, bytes_accessed=29 * MIB, transcendentals=0
        ),
        name="close_patches",
    )(slot, rho, vel, vel, vel, p, rates, rims, edges)


def merge_kernel(corner_ref, base_ref, got_ref, out_ref):
    width = 32
    count = got_ref.shape[0]

    @pl.when(pl.program_id(0) == 0)
    def _():
        out_ref[...] = base_ref[...]

    row = lax.broadcasted_iota(jnp.int32, (4, 128), 0)

    def one(s, carry):
        base = corner_at(corner_ref, pl.program_id(0) * count + s)

        @pl.when(base >= 0)
        def _():
            rims = (
                pl.ds(base - width, 4),
                pl.ds(base + FOOT * width, 4),
                pl.ds(base - 1, 4, stride=width),
                pl.ds(base + FOOT, 4, stride=width),
            )
            result = []
            for c in range(5):
                flux = [
                    got_ref[s, c, pl.ds(16 + 8 * (n // 2) + n % 2, 4, stride=2), :]
                    for n in range(4)
                ]
                rim = [out_ref[c, at, :] for at in rims]
                rim = [rim[n] + flux[n] if n % 2 else rim[n] - flux[n] for n in range(4)]
                foot = []
                for i in range(4):
                    v = got_ref[s, c, pl.ds(8 * (i // 2) + i % 2, 4, stride=2), :]
                    if i == 0:
                        v = v + flux[0]
                    if i == 3:
                        v = v - flux[1]
                    low = jnp.broadcast_to(flux[2][i : i + 1, :], (4, 128))
                    high = jnp.broadcast_to(flux[3][i : i + 1, :], (4, 128))
                    v = v + jnp.where(row == 0, low, 0.0) - jnp.where(row == 3, high, 0.0)
                    foot.append(v)
                result.append((rim, foot))
            for c in range(5):
                rim, foot = result[c]
                for at, v in zip(rims, rim):
                    out_ref[c, at, :] = v
                for i in range(4):
                    out_ref[c, pl.ds(base + i * width, 4), :] = foot[i]

        return carry

    lax.fori_loop(0, count, one, 0)


def merge(corners, base, got):
    slots = got.shape[0]
    whole = pl.BlockSpec(base.shape, lambda i: (0, 0, 0))
    return pl.pallas_call(
        merge_kernel,
        grid=(4,),
        out_shape=jax.ShapeDtypeStruct(base.shape, F32),
        in_specs=[
            pl.BlockSpec(memory_space=SMEM),
            whole,
            pl.BlockSpec((slots // 4, 5, 32, 128), lambda i: (i, 0, 0, 0)),
        ],
        out_specs=whole,
        compiler_params=pltpu.CompilerParams(vmem_limit_bytes=24 * MIB),
        cost_estimate=pl.CostEstimate(flops=MIB, bytes_accessed=11 * MIB, transcendentals=0),
        name="merge_patches",
    )(corners, base, got)


def exchange(buffer, groups):
    shape = buffer.shape
    rows = buffer.size // (groups * 128)
    moved = lax.all_to_all(
        buffer.reshape(groups, rows, 128), "yz", split_axis=0, concat_axis=0, tiled=True
    )
    return moved.reshape(shape)


def local(
    coarse_density,
    coarse_velocity,
    coarse_pressure,
    coarse_bins,
    fine_density,
    fine_velocity,
    fine_pressure,
    fine_bins,
    patch_host,
    patch_spot,
    heat_rate,
    cool_rate,
):
    groups = lax.axis_size("yz")
    rows = lax.axis_size("gx")
    gx = lax.axis_index("gx")
    me = lax.axis_index("yz")
    count = fine_density.shape[0]
    slots = CAP * groups

    rho = coarse_density.reshape(-1, 128)
    vel = coarse_velocity.reshape(3, -1, 128)
    press = coarse_pressure.reshape(-1, 128)
    place = jnp.stack([gx, me]).astype(jnp.int32)
    host_lines, spot_lines = patch_host.reshape(-1, 128), patch_spot.reshape(-1, 128)
    rims, x_first, x_last, y_first, y_last, corners, slot = pack(
        place, host_lines, spot_lines, rho, vel, press, slots
    )
    arrived = exchange(rims, groups)

    up_x = [(i, (i + 1) % rows) for i in range(rows)]
    down_x = [((i + 1) % rows, i) for i in range(rows)]
    up_y = [(i, (i + 1) % groups) for i in range(groups)]
    down_y = [((i + 1) % groups, i) for i in range(groups)]
    x_low = lax.ppermute(x_last, "gx", up_x)
    x_high = lax.ppermute(x_first, "gx", down_x)
    y_low = lax.ppermute(y_last, "yz", up_y)
    y_high = lax.ppermute(y_first, "yz", down_y)

    fine_columns = fine_bins.reshape(2, 16, 8, 8).transpose(0, 3, 1, 2).reshape(16, 128)
    coarse_columns = jnp.pad(coarse_bins.T, ((0, 0), (0, 128 - coarse_bins.shape[0])))
    tables = jnp.pad(jnp.stack([heat_rate, cool_rate]), ((0, 0), (0, 48))).reshape(2, 16, 128)
    rates = look_up(jnp.concatenate([fine_columns, coarse_columns], axis=0), tables)

    f_rho = fine_density.reshape(count, 64, 256)
    f_vel = fine_velocity.reshape(3, count, 64, 256)
    f_press = fine_pressure.reshape(count, 64, 256)
    means, edges = open_patches(slot, f_rho, f_vel, f_press, rates, slots)
    sums = face_fluxes(slot, arrived, edges, means)
    sums, x_low, x_high, y_low, y_high = lax.optimization_barrier(
        (sums, x_low, x_high, y_low, y_high)
    )
    got = exchange(sums, groups)
    base = coarse_step(corners, rho, vel, press, x_low, x_high, y_low, y_high, rates)
    fine_new = close_patches(slot, f_rho, f_vel, f_press, rates, arrived, edges)
    coarse_new = merge(corners, base, got)
    return (
        coarse_new.reshape((5,) + coarse_density.shape),
        fine_new.reshape((5,) + fine_density.shape),
    )


def solution(mesh):
    placed = (
        P("gx", "yz", None),
        P(None, "gx", "yz", None),
        P("gx", "yz", None),
        P("gx", "yz"),
        P(("gx", "yz"), None, None, None),
        P(None, ("gx", "yz"), None, None, None),
        P(("gx", "yz"), None, None, None),
        P(("gx", "yz"), None, None),
        P(),
        P(),
        P(),
        P(),
    )
    return jax.shard_map(
        local,
        mesh=mesh,
        in_specs=placed,
        out_specs=(P(None, "gx", "yz", None), P(None, ("gx", "yz"), None, None, None)),
        check_vma=False,
    )
```

```python
import functools

import jax
import jax.numpy as jnp
from jax import lax
from jax.experimental import pallas as pl
from jax.experimental.pallas import tpu as pltpu
from jax.sharding import PartitionSpec as P

GAMMA = 5.0 / 3.0
STEP = 0.02
HALF = 0.5 * STEP
FOOT = 4
SIDE = 5
CAP = 2
F32 = jnp.float32
VMEM = pltpu.VMEM
SMEM = pltpu.SMEM
MIB = 1024 * 1024
GRANT = 56 * MIB


def conserve(rho, ux, uy, uz, p):
    mx, my, mz = rho * ux, rho * uy, rho * uz
    xx, yy, zz = mx * ux, my * uy, mz * uz
    energy = 1.5 * p + 0.5 * (xx + yy + zz)
    return {
        "amounts": (rho, mx, my, mz, energy),
        "speed": (ux, uy, uz),
        "p": p,
        "square": (xx, yy, zz),
        "cross": {},
    }


def sound_of(p, rho):
    square = GAMMA * (p / rho)
    return square * lax.rsqrt(square)


def derive(prim):
    rho, p = prim[0], prim[4]
    both = rho + p
    common = p / (rho * both)
    square = GAMMA * (common * both)
    cell = conserve(*prim)
    cell["sound"] = square * lax.rsqrt(square)
    cell["share"] = common * rho
    return cell


def again(rho, ux, uy, uz, p, sound):
    cell = conserve(rho, ux, uy, uz, p)
    cell["sound"] = sound
    return cell


def directed(cell, d):
    amounts, p = cell["amounts"], cell["p"]
    u = cell["speed"][d]
    flux = [amounts[1 + d]]
    for k in range(3):
        if k == d:
            flux.append(cell["square"][d] + p)
            continue
        pair = (min(k, d), max(k, d))
        if pair not in cell["cross"]:
            cell["cross"][pair] = amounts[1 + pair[0]] * cell["speed"][pair[1]]
        flux.append(cell["cross"][pair])
    flux.append((amounts[4] + p) * u)
    return (amounts, flux, jnp.abs(u) + cell["sound"])


def twice_flux(left, right):
    fastest = jnp.maximum(left[2], right[2])
    return [
        (left[1][c] + right[1][c]) - fastest * (right[0][c] - left[0][c]) for c in range(5)
    ]


def shifted(cell, shift, axis):
    rho, p = cell["amounts"][0], cell["p"]
    values = (rho,) + cell["speed"] + (p, cell["sound"])
    return again(*[pltpu.roll(v, shift, axis) for v in values])


def source_term(rho, share, rates):
    heat, heat_slope, cool, cool_slope = rates
    return rho * ((heat + share * heat_slope) - rho * (cool + share * cool_slope))


def lane_pick(tile, lane):
    index = jnp.full((8, 128), lane, jnp.int32)
    return jnp.take_along_axis(tile, index, axis=1, mode="promise_in_bounds")


def plan_places(place_ref, host_ref, spot_ref, corner_ref, slot_ref):
    gx, me = place_ref[0], place_ref[1]
    rows = pl.ds(pl.multiple_of(8 * gx, 8), 8)
    hosts, spots = host_ref[rows, :], spot_ref[rows, :]
    lane = lax.broadcasted_iota(jnp.int32, (8, 128), 1)
    row = lax.broadcasted_iota(jnp.int32, (8, 128), 0)
    place_x = (spots * 43) >> 8
    corner = (1 + SIDE * place_x) * 32 + 1 + SIDE * (spots - 6 * place_x)
    key = jnp.where(hosts == me, lane * 1024 + corner, -1)
    table = jnp.full((8, 128), -1, jnp.int32)
    far = 1 << 20
    for q in range(4):
        inside = (lane // 32 == q) & (key >= 0)
        last = jnp.max(jnp.where(inside, key, -1), axis=1, keepdims=True)
        first = jnp.min(jnp.where(inside, key, far), axis=1, keepdims=True)
        none = last < 0
        single = none | (first == last)
        table = jnp.where(lane == 2 * q, jnp.where(none, -1, first & 1023), table)
        table = jnp.where(lane == 2 * q + 1, jnp.where(single, -1, last & 1023), table)
    corner_ref[...] = table
    own = jnp.sum(jnp.where(row == me // 4, hosts, 0), axis=0, keepdims=True)
    own = pltpu.roll(jnp.broadcast_to(own, (8, 128)), lax.rem(128 - 32 * lax.rem(me, 4), 128), 1)
    own = jnp.broadcast_to(own[0:1, :], (32, 128))
    lane = lax.broadcasted_iota(jnp.int32, (32, 128), 1)
    row = lax.broadcasted_iota(jnp.int32, (32, 128), 0)
    mine = jnp.sum(jnp.where(lane == row, own, 0), axis=1, keepdims=True)
    rank = jnp.sum(jnp.where((own == mine) & (lane < row), 1, 0), axis=1, keepdims=True)
    slot_ref[...] = jnp.broadcast_to(CAP * mine + rank, (32, 128))


def corner_at(corner_ref, s):
    line = s // 8
    return corner_ref[line, s - 8 * line]


def pack_kernel(
    place_ref, host_ref, spot_ref, rho_hbm, vel_hbm, p_hbm,
    rim_ref, xa_ref, xb_ref, ya_ref, yb_ref, corner_ref, slot_ref,
    cell_ref, table_ref, sem, table_sem,
):
    sources = [rho_hbm, vel_hbm.at[0], vel_hbm.at[1], vel_hbm.at[2], p_hbm]
    copies = [pltpu.make_async_copy(f, cell_ref.at[c], sem.at[c]) for c, f in enumerate(sources)]
    for copy in copies:
        copy.start()
    plan_places(place_ref, host_ref, spot_ref, corner_ref, slot_ref)
    move = pltpu.make_async_copy(corner_ref, table_ref, table_sem)
    move.start()
    move.wait()
    for copy in copies:
        copy.wait()
    fields = [cell_ref.at[c] for c in range(5)]
    width = 32
    rows = cell_ref.shape[1]

    def one(s, carry):
        base = corner_at(table_ref, s)

        @pl.when(base >= 0)
        def _():
            for c, f in enumerate(fields):
                rim_ref[s, c, 0:4, :] = f[pl.ds(base - width, 4), :]
                rim_ref[s, c, 4:8, :] = f[pl.ds(base + FOOT * width, 4), :]
                rim_ref[s, c, 8:12, :] = f[pl.ds(base - 1, 4, stride=width), :]
                rim_ref[s, c, 12:16, :] = f[pl.ds(base + FOOT, 4, stride=width), :]

        return carry

    lax.fori_loop(0, rim_ref.shape[0], one, 0)
    for c, f in enumerate(fields):
        xa_ref[c] = f[0:width, :]
        xb_ref[c] = f[rows - width : rows, :]
        ya_ref[c] = f[pl.ds(0, width, stride=width), :]
        yb_ref[c] = f[pl.ds(width - 1, width, stride=width), :]


def pack(place, hosts, spots, rho, vel, p, slots):
    whole = pl.BlockSpec(memory_space=VMEM)
    edge = jax.ShapeDtypeStruct((5, 32, 128), F32)
    return pl.pallas_call(
        pack_kernel,
        out_shape=[jax.ShapeDtypeStruct((slots, 5, 16, 128), F32), edge, edge, edge, edge]
        + [jax.ShapeDtypeStruct((8, 128), jnp.int32), jax.ShapeDtypeStruct((32, 128), jnp.int32)],
        in_specs=[pl.BlockSpec(memory_space=SMEM), whole, whole]
        + [pl.BlockSpec(memory_space=pl.ANY)] * 3,
        out_specs=[whole] * 7,
        scratch_shapes=[
            pltpu.VMEM((5,) + rho.shape, F32),
            pltpu.SMEM((8, 128), jnp.int32),
            pltpu.SemaphoreType.DMA((5,)),
            pltpu.SemaphoreType.DMA,
        ],
        compiler_params=pltpu.CompilerParams(vmem_limit_bytes=GRANT),
        cost_estimate=pl.CostEstimate(flops=0, bytes_accessed=6 * MIB, transcendentals=0),
        name="pack_rims",
    )(place, hosts, spots, rho, vel, p)


def rates_kernel(bins_ref, table_ref, out_ref):
    for g in range(bins_ref.shape[0] // 8):
        rows = slice(8 * g, 8 * g + 8)
        low = None
        for step in range(2):
            b = bins_ref[rows, :] + step
            line = b // 128
            lane = b - line * 128
            found = [jnp.zeros((8, 128), F32) for _ in range(2)]
            for r in range(16):
                hit = line == r
                for t in range(2):
                    entry = jnp.broadcast_to(table_ref[t, r : r + 1, :], (8, 128))
                    value = jnp.take_along_axis(entry, lane, axis=1, mode="promise_in_bounds")
                    found[t] = jnp.where(hit, value, found[t])
            for t in range(2):
                entry = found[t] if step == 0 else found[t] - low[t]
                out_ref[2 * t + step, rows, :] = STEP * entry
            low = found


def look_up(bins, tables):
    whole = pl.BlockSpec(memory_space=VMEM)
    return pl.pallas_call(
        rates_kernel,
        out_shape=jax.ShapeDtypeStruct((4,) + bins.shape, F32),
        in_specs=[whole, whole],
        out_specs=whole,
        cost_estimate=pl.CostEstimate(flops=MIB, bytes_accessed=MIB, transcendentals=0),
        name="rate_lookup",
    )(bins, tables)


PITCH = 48
LOW = 8


def coarse_kernel(
    corner_ref, rho_ref, vel_ref, p_ref, xlo_ref, xhi_ref, ylo_ref, yhi_ref, rate_ref,
    out_ref, cell_ref, fx_ref, fy_ref,
):
    width = 32
    fields = [rho_ref, vel_ref.at[0], vel_ref.at[1], vel_ref.at[2], p_ref]

    def keep(prim, index):
        for n, v in enumerate(prim):
            cell_ref[n, index, :] = v
        cell_ref[5, index, :] = sound_of(prim[4], prim[0])

    def fill(x, carry):
        for q in range(4):
            rows = pl.ds(x * width + 8 * q, 8)
            keep([f[rows, :] for f in fields], pl.ds((x + 1) * PITCH + LOW + 8 * q, 8))
        return carry

    lax.fori_loop(0, width, fill, 0)
    for q in range(4):
        rows = slice(8 * q, 8 * q + 8)
        keep([xlo_ref[c, rows, :] for c in range(5)], pl.ds(LOW + 8 * q, 8))
        keep([xhi_ref[c, rows, :] for c in range(5)], pl.ds(33 * PITCH + LOW + 8 * q, 8))
        first = (8 * q + 1) * PITCH + LOW
        keep([ylo_ref[c, rows, :] for c in range(5)], pl.ds(first - 1, 8, stride=PITCH))
        keep([yhi_ref[c, rows, :] for c in range(5)], pl.ds(first + width, 8, stride=PITCH))

    def fetch(row):
        return again(*[cell_ref[n, pl.ds(row, 8), :] for n in range(6)])

    def step(x, carry):
        result = []
        for q in range(4):
            below = carry[5 * q : 5 * q + 5]
            row = (x + 1) * PITCH + LOW + 8 * q
            here = fetch(row)
            above = twice_flux(directed(here, 0), directed(fetch(row + PITCH), 0))
            y_here = directed(here, 1)
            y_high = twice_flux(y_here, directed(fetch(row + 1), 1))
            y_low = twice_flux(directed(fetch(row - 1), 1), y_here)
            z_high = twice_flux(directed(here, 2), directed(shifted(here, 127, 1), 2))
            rates = [lane_pick(rate_ref[t, 16 + 8 * q : 24 + 8 * q, :], x) for t in range(4)]
            rho = here["amounts"][0]
            gain = source_term(rho, here["p"] / (rho + here["p"]), rates)
            flat = pl.ds(x * width + 8 * q, 8)
            for c in range(5):
                change = (
                    (above[c] - below[c])
                    + (y_high[c] - y_low[c])
                    + (z_high[c] - pltpu.roll(z_high[c], 1, 1))
                )
                value = here["amounts"][c] - HALF * change
                if c == 4:
                    value = value + gain
                out_ref[c, flat, :] = value
                fx_ref[c, flat, :] = above[c]
                fy_ref[c, flat, :] = y_high[c]
            result += above
        return tuple(result)

    first = []
    for q in range(4):
        row = LOW + 8 * q
        first += twice_flux(directed(fetch(row), 0), directed(fetch(row + PITCH), 0))
    lax.fori_loop(0, width, step, tuple(first))

    def reflux(s, carry):
        base = corner_at(corner_ref, s)

        @pl.when(base >= 0)
        def _():
            places = (
                (pl.ds(base - width, 4), pl.ds(base - width, 4), fx_ref, HALF),
                (
                    pl.ds(base + FOOT * width, 4),
                    pl.ds(base + (FOOT - 1) * width, 4),
                    fx_ref,
                    -HALF,
                ),
                (
                    pl.ds(base - 1, 4, stride=width),
                    pl.ds(base - 1, 4, stride=width),
                    fy_ref,
                    HALF,
                ),
                (
                    pl.ds(base + FOOT, 4, stride=width),
                    pl.ds(base + FOOT - 1, 4, stride=width),
                    fy_ref,
                    -HALF,
                ),
            )
            values = [
                [out_ref[c, a, :] + w * f[c, b, :] for a, b, f, w in places] for c in range(5)
            ]
            for c in range(5):
                for n in range(4):
                    out_ref[c, places[n][0], :] = values[c][n]

        return carry

    lax.fori_loop(0, 8 * corner_ref.shape[0], reflux, 0)


def coarse_step(corners, rho, vel, p, xlo, xhi, ylo, yhi, rates):
    whole = pl.BlockSpec(memory_space=VMEM)
    cells = rho.shape[0]
    return pl.pallas_call(
        coarse_kernel,
        out_shape=jax.ShapeDtypeStruct((5, cells, 128), F32),
        in_specs=[pl.BlockSpec(memory_space=SMEM)] + [whole] * 8,
        out_specs=whole,
        scratch_shapes=[
            pltpu.VMEM((6, 34 * PITCH, 128), F32),
            pltpu.VMEM((5, cells, 128), F32),
            pltpu.VMEM((5, cells, 128), F32),
        ],
        compiler_params=pltpu.CompilerParams(vmem_limit_bytes=32 * MIB),
        cost_estimate=pl.CostEstimate(
            flops=300 * cells * 128, bytes_accessed=30 * MIB, transcendentals=0
        ),
        name="coarse_step",
    )(corners, rho, vel, p, xlo, xhi, ylo, yhi, rates)


def take_lanes(tile, index):
    return jnp.take_along_axis(tile, index, axis=1, mode="promise_in_bounds")


def fold(even, odd):
    row = lax.broadcasted_iota(jnp.int32, (8, 128), 0)
    lane = lax.broadcasted_iota(jnp.int32, (8, 128), 1)
    halves = []
    for h in range(2):
        a, b = even[:, 128 * h : 128 * h + 128], odd[:, 128 * h : 128 * h + 128]
        a = a + pltpu.roll(a, 7, 0)
        b = b + pltpu.roll(b, 1, 0)
        m = jnp.where(row % 2 == 0, a, b)
        halves.append(m + pltpu.roll(m, 127 if h == 0 else 1, 1))
    mixed = jnp.where(lane % 2 == 0, halves[0], halves[1])
    return take_lanes(mixed, jnp.where(lane < 64, 2 * lane, 2 * lane - 127))


def patch_update(prim_refs, p_index, rates_at, faces, emit, on_plane=None):
    row = lax.broadcasted_iota(jnp.int32, (8, 256), 0)
    cells, fluxes, x_flux = {}, {}, {}
    x_flux[-1] = None if faces is None else [faces(c, 0, slice(0, 8)) for c in range(5)]
    x_flux[7] = None if faces is None else [faces(c, 1, slice(0, 8)) for c in range(5)]

    def enter(i):
        prim = [f[p_index, 8 * i : 8 * i + 8, :] for f in prim_refs]
        if on_plane is not None:
            on_plane(i, prim)
        here = derive(prim)
        cells[i] = (here, shifted(here, 7, 0), shifted(here, 255, 1), rates_at(i))

    def cross(i):
        here, y_next, z_next, _ = cells[i]
        y_flux = twice_flux(directed(here, 1), directed(y_next, 1))
        z_flux = twice_flux(directed(here, 2), directed(z_next, 2))
        y_back = [pltpu.roll(v, 1, 0) for v in y_flux]
        z_back = [pltpu.roll(v, 1, 1) for v in z_flux]
        fluxes[i] = (y_flux, y_back, z_flux, z_back)
        if i < 7:
            x_flux[i] = None
            if faces is not None or i % 2 == 1:
                x_flux[i] = twice_flux(directed(here, 0), directed(cells[i + 1][0], 0))

    def leave(i):
        here, _, _, rates = cells.pop(i)
        y_flux, y_back, z_flux, z_back = fluxes.pop(i)
        gain = source_term(here["amounts"][0], here["share"], rates)
        result = []
        for c in range(5):
            if faces is None:
                y_high, y_low = 0.0, 0.0
            else:
                y_high = jnp.broadcast_to(faces(c, 3, slice(i, i + 1)), (8, 256))
                y_low = jnp.broadcast_to(faces(c, 2, slice(i, i + 1)), (8, 256))
            change = jnp.where(row == 7, y_high, y_flux[c]) - jnp.where(
                row == 0, y_low, y_back[c]
            )
            change = change + (z_flux[c] - z_back[c])
            if x_flux[i] is not None:
                change = change + x_flux[i][c]
            if x_flux[i - 1] is not None:
                change = change - x_flux[i - 1][c]
            value = here["amounts"][c] - STEP * change
            if c == 4:
                value = value + gain
            result.append(value)
        emit(i, result)

    enter(0)
    for i in range(9):
        if i < 7:
            enter(i + 1)
        if i < 8:
            cross(i)
        if i > 0:
            leave(i - 1)


def rates_reader(rate_ref, patch):
    half = patch // 16
    start = pl.multiple_of(8 * half, 8)
    shift = 128 - 8 * (patch - 16 * half)
    tiles = [pltpu.roll(rate_ref[t, pl.ds(start, 8), :], shift, 1) for t in range(4)]

    def rates_at(i):
        return [jnp.broadcast_to(v[:, i : i + 1], (8, 256)) for v in tiles]

    return rates_at


PER = 4


def open_kernel(
    slot_ref, rho_ref, ux_ref, uy_ref, uz_ref, p_ref, rate_ref, mean_ref, edge_ref
):
    refs = [rho_ref, ux_ref.at[0], uy_ref.at[0], uz_ref.at[0], p_ref]

    def one(n, carry):
        patch = pl.program_id(0) * PER + n
        slot = slot_ref[patch, 0]

        def on_plane(i, prim):
            for c in range(5):
                if i == 0:
                    edge_ref[n, c, 0] = prim[c]
                if i == 7:
                    edge_ref[n, c, 1] = prim[c]
                edge_ref[n, c, 2, i : i + 1, :] = prim[c][0:1, :]
                edge_ref[n, c, 3, i : i + 1, :] = prim[c][7:8, :]

        held = {}

        def emit(i, result):
            for c in range(5):
                at = (i // 2, c)
                held[at] = result[c] if i % 2 == 0 else held[at] + result[c]
                if i % 4 == 3:
                    value = fold(held.pop((i // 2 - 1, c)), held.pop(at))
                    mean_ref[slot, c, 8 * (i // 4) : 8 * (i // 4) + 8, :] = 0.125 * value

        patch_update(refs, n, rates_reader(rate_ref, patch), None, emit, on_plane)
        return carry

    lax.fori_loop(0, PER, one, 0)


def patch_specs(extra):
    one = pl.BlockSpec((PER, 64, 256), lambda i: (i, 0, 0))
    speed = [pl.BlockSpec((1, PER, 64, 256), lambda i, d=d: (d, i, 0, 0)) for d in range(3)]
    return [pl.BlockSpec(memory_space=SMEM)] * extra + [one] + speed + [one]


def open_patches(slot, rho, vel, p, rates, slots):
    count = rho.shape[0]
    return pl.pallas_call(
        open_kernel,
        grid=(count // PER,),
        out_shape=[
            jax.ShapeDtypeStruct((slots, 5, 32, 128), F32),
            jax.ShapeDtypeStruct((count, 5, 4, 8, 256), F32),
        ],
        in_specs=patch_specs(1) + [pl.BlockSpec(memory_space=VMEM)],
        out_specs=[
            pl.BlockSpec((slots, 5, 16, 128), lambda i: (0, 0, 0, 0)),
            pl.BlockSpec((PER, 5, 4, 8, 256), lambda i: (i, 0, 0, 0, 0)),
        ],
        compiler_params=pltpu.CompilerParams(vmem_limit_bytes=GRANT),
        cost_estimate=pl.CostEstimate(
            flops=250 * count * 64 * 256, bytes_accessed=18 * MIB, transcendentals=0
        ),
        name="open_patches",
    )(slot, rho, vel, vel, vel, p, rates)


BATCH = 4


def side_fluxes(rim, edge, ghost_ref):
    lane = lax.broadcasted_iota(jnp.int32, (16, 128), 1) // 2
    coarse = list(rim)
    coarse.append(sound_of(coarse[4], coarse[0]))
    for c in range(6):
        for h in range(2):
            wide = take_lanes(coarse[c], lane + 64 * h)
            ghost_ref[c, h, pl.ds(0, 16, stride=2), :] = wide
            ghost_ref[c, h, pl.ds(1, 16, stride=2), :] = wide
    sides = []
    for side in range(4):
        rows = slice(8 * side, 8 * side + 8)
        outer = [
            jnp.concatenate([ghost_ref[c, 0, rows, :], ghost_ref[c, 1, rows, :]], axis=1)
            for c in range(6)
        ]
        d = side // 2
        ghost = directed(again(*outer), d)
        prim = edge(side)
        inner = directed(again(*prim, sound_of(prim[4], prim[0])), d)
        sides.append(twice_flux(ghost, inner) if side % 2 == 0 else twice_flux(inner, ghost))
    return sides


def face_kernel(
    slot_ref, rim_ref, edge_hbm, _, out_hbm, edge_ref, sum_ref, ghost_ref, edge_sem, sum_sem
):
    count = edge_ref.shape[0]

    def load(g):
        part = pl.ds(g * BATCH, BATCH)
        return pltpu.make_async_copy(edge_hbm.at[part], edge_ref.at[part], edge_sem.at[g])

    def save(p):
        place = out_hbm.at[slot_ref[p, 0], :, pl.ds(16, 16), :]
        return pltpu.make_async_copy(sum_ref.at[p], place, sum_sem.at[p])

    for g in range(count // BATCH):
        load(g).start()

    def chunk(g, carry):
        load(g).wait()
        for n in range(BATCH):
            p = g * BATCH + n
            slot = slot_ref[p, 0]
            sides = side_fluxes(
                [rim_ref[slot, c] for c in range(5)],
                lambda side, p=p: [edge_ref[p, c, side] for c in range(5)],
                ghost_ref.at[n],
            )
            for c in range(5):
                for d in range(2):
                    value = fold(sides[2 * d][c], sides[2 * d + 1][c])
                    sum_ref[p, c, 8 * d : 8 * d + 8, :] = (0.125 * STEP) * value
        for n in range(BATCH):
            save(g * BATCH + n).start()
        return carry

    lax.fori_loop(0, count // BATCH, chunk, 0)

    def settle(p, carry):
        save(p).wait()
        return carry

    lax.fori_loop(0, count, settle, 0)


def face_fluxes(slot, rims, edges, buffer):
    count = edges.shape[0]
    anywhere = pl.BlockSpec(memory_space=pl.ANY)
    return pl.pallas_call(
        face_kernel,
        out_shape=jax.ShapeDtypeStruct(buffer.shape, F32),
        in_specs=[
            pl.BlockSpec(memory_space=SMEM),
            pl.BlockSpec(memory_space=VMEM),
            anywhere,
            anywhere,
        ],
        out_specs=anywhere,
        input_output_aliases={3: 0},
        scratch_shapes=[
            pltpu.VMEM(edges.shape, F32),
            pltpu.VMEM((count, 5, 16, 128), F32),
            pltpu.VMEM((BATCH, 6, 2, 32, 128), F32),
            pltpu.SemaphoreType.DMA((count // BATCH,)),
            pltpu.SemaphoreType.DMA((count,)),
        ],
        compiler_params=pltpu.CompilerParams(vmem_limit_bytes=58 * MIB),
        cost_estimate=pl.CostEstimate(
            flops=100 * count * 32 * 256, bytes_accessed=11 * MIB, transcendentals=0
        ),
        name="face_fluxes",
    )(slot, rims, edges, buffer)


def close_kernel(
    slot_ref, rho_ref, ux_ref, uy_ref, uz_ref, p_ref, rate_ref, rim_ref, edge_ref,
    out_ref, ghost_ref, rows_ref,
):
    refs = [rho_ref, ux_ref.at[0], uy_ref.at[0], uz_ref.at[0], p_ref]

    def one(n, carry):
        patch = pl.program_id(0) * PER + n
        slot = slot_ref[patch, 0]
        sides = side_fluxes(
            [rim_ref[slot, c] for c in range(5)],
            lambda side: [edge_ref[n, c, side] for c in range(5)],
            ghost_ref,
        )
        for c in range(5):
            for d in range(2):
                rows_ref[c, d] = sides[2 + d][c]

        def faces(c, side, rows):
            return sides[side][c] if side < 2 else rows_ref[c, side - 2, rows, :]

        def emit(i, result):
            for c in range(5):
                out_ref[c, n, 8 * i : 8 * i + 8, :] = result[c]

        patch_update(refs, n, rates_reader(rate_ref, patch), faces, emit)
        return carry

    lax.fori_loop(0, PER, one, 0)


def close_patches(slot, rho, vel, p, rates, rims, edges):
    count = rho.shape[0]
    return pl.pallas_call(
        close_kernel,
        grid=(count // PER,),
        out_shape=jax.ShapeDtypeStruct((5,) + rho.shape, F32),
        in_specs=patch_specs(1)
        + [
            pl.BlockSpec(memory_space=VMEM),
            pl.BlockSpec(rims.shape, lambda i: (0, 0, 0, 0)),
            pl.BlockSpec((PER, 5, 4, 8, 256), lambda i: (i, 0, 0, 0, 0)),
        ],
        out_specs=pl.BlockSpec((5, PER, 64, 256), lambda i: (0, i, 0, 0)),
        scratch_shapes=[
            pltpu.VMEM((6, 2, 32, 128), F32),
            pltpu.VMEM((5, 2, 8, 256), F32),
        ],
        compiler_params=pltpu.CompilerParams(vmem_limit_bytes=20 * MIB),
        cost_estimate=pl.CostEstimate(
            flops=250 * count * 64 * 256, bytes_accessed=29 * MIB, transcendentals=0
        ),
        name="close_patches",
    )(slot, rho, vel, vel, vel, p, rates, rims, edges)


def merge_kernel(corner_ref, base_ref, got_ref, out_ref):
    width = 32
    out_ref[...] = base_ref[...]
    row = lax.broadcasted_iota(jnp.int32, (4, 128), 0)

    def one(s, carry):
        base = corner_at(corner_ref, s)

        @pl.when(base >= 0)
        def _():
            rims = (
                pl.ds(base - width, 4),
                pl.ds(base + FOOT * width, 4),
                pl.ds(base - 1, 4, stride=width),
                pl.ds(base + FOOT, 4, stride=width),
            )
            result = []
            for c in range(5):
                flux = [
                    got_ref[s, c, pl.ds(16 + 8 * (n // 2) + n % 2, 4, stride=2), :]
                    for n in range(4)
                ]
                rim = [out_ref[c, at, :] for at in rims]
                rim = [rim[n] + flux[n] if n % 2 else rim[n] - flux[n] for n in range(4)]
                foot = []
                for i in range(4):
                    v = got_ref[s, c, pl.ds(8 * (i // 2) + i % 2, 4, stride=2), :]
                    if i == 0:
                        v = v + flux[0]
                    if i == 3:
                        v = v - flux[1]
                    low = jnp.broadcast_to(flux[2][i : i + 1, :], (4, 128))
                    high = jnp.broadcast_to(flux[3][i : i + 1, :], (4, 128))
                    v = v + jnp.where(row == 0, low, 0.0) - jnp.where(row == 3, high, 0.0)
                    foot.append(v)
                result.append((rim, foot))
            for c in range(5):
                rim, foot = result[c]
                for at, v in zip(rims, rim):
                    out_ref[c, at, :] = v
                for i in range(4):
                    out_ref[c, pl.ds(base + i * width, 4), :] = foot[i]

        return carry

    lax.fori_loop(0, got_ref.shape[0], one, 0)


def merge(corners, base, got):
    whole = pl.BlockSpec(memory_space=VMEM)
    return pl.pallas_call(
        merge_kernel,
        out_shape=jax.ShapeDtypeStruct(base.shape, F32),
        in_specs=[pl.BlockSpec(memory_space=SMEM), whole, whole],
        out_specs=whole,
        compiler_params=pltpu.CompilerParams(vmem_limit_bytes=24 * MIB),
        cost_estimate=pl.CostEstimate(flops=MIB, bytes_accessed=11 * MIB, transcendentals=0),
        name="merge_patches",
    )(corners, base, got)


def exchange(buffer, groups):
    shape = buffer.shape
    rows = buffer.size // (groups * 128)
    moved = lax.all_to_all(
        buffer.reshape(groups, rows, 128), "yz", split_axis=0, concat_axis=0, tiled=True
    )
    return moved.reshape(shape)


def local(
    coarse_density,
    coarse_velocity,
    coarse_pressure,
    coarse_bins,
    fine_density,
    fine_velocity,
    fine_pressure,
    fine_bins,
    patch_host,
    patch_spot,
    heat_rate,
    cool_rate,
):
    groups = lax.axis_size("yz")
    rows = lax.axis_size("gx")
    gx = lax.axis_index("gx")
    me = lax.axis_index("yz")
    count = fine_density.shape[0]
    slots = CAP * groups

    rho = coarse_density.reshape(-1, 128)
    vel = coarse_velocity.reshape(3, -1, 128)
    press = coarse_pressure.reshape(-1, 128)
    place = jnp.stack([gx, me]).astype(jnp.int32)
    host_lines, spot_lines = patch_host.reshape(-1, 128), patch_spot.reshape(-1, 128)
    rims, x_first, x_last, y_first, y_last, corners, slot = pack(
        place, host_lines, spot_lines, rho, vel, press, slots
    )
    arrived = exchange(rims, groups)

    up_x = [(i, (i + 1) % rows) for i in range(rows)]
    down_x = [((i + 1) % rows, i) for i in range(rows)]
    up_y = [(i, (i + 1) % groups) for i in range(groups)]
    down_y = [((i + 1) % groups, i) for i in range(groups)]
    x_low = lax.ppermute(x_last, "gx", up_x)
    x_high = lax.ppermute(x_first, "gx", down_x)
    y_low = lax.ppermute(y_last, "yz", up_y)
    y_high = lax.ppermute(y_first, "yz", down_y)

    fine_columns = fine_bins.reshape(2, 16, 8, 8).transpose(0, 3, 1, 2).reshape(16, 128)
    coarse_columns = jnp.pad(coarse_bins.T, ((0, 0), (0, 128 - coarse_bins.shape[0])))
    tables = jnp.pad(jnp.stack([heat_rate, cool_rate]), ((0, 0), (0, 48))).reshape(2, 16, 128)
    rates = look_up(jnp.concatenate([fine_columns, coarse_columns], axis=0), tables)

    f_rho = fine_density.reshape(count, 64, 256)
    f_vel = fine_velocity.reshape(3, count, 64, 256)
    f_press = fine_pressure.reshape(count, 64, 256)
    means, edges = open_patches(slot, f_rho, f_vel, f_press, rates, slots)
    sums = face_fluxes(slot, arrived, edges, means)
    sums, x_low, x_high, y_low, y_high = lax.optimization_barrier(
        (sums, x_low, x_high, y_low, y_high)
    )
    got = exchange(sums, groups)
    base = coarse_step(corners, rho, vel, press, x_low, x_high, y_low, y_high, rates)
    fine_new = close_patches(slot, f_rho, f_vel, f_press, rates, arrived, edges)
    coarse_new = merge(corners, base, got)
    return (
        coarse_new.reshape((5,) + coarse_density.shape),
        fine_new.reshape((5,) + fine_density.shape),
    )


def solution(mesh):
    placed = (
        P("gx", "yz", None),
        P(None, "gx", "yz", None),
        P("gx", "yz", None),
        P("gx", "yz"),
        P(("gx", "yz"), None, None, None),
        P(None, ("gx", "yz"), None, None, None),
        P(("gx", "yz"), None, None, None),
        P(("gx", "yz"), None, None),
        P(),
        P(),
        P(),
        P(),
    )
    return jax.shard_map(
        local,
        mesh=mesh,
        in_specs=placed,
        out_specs=(P(None, "gx", "yz", None), P(None, ("gx", "yz"), None, None, None)),
        check_vma=False,
    )
```

```python
import functools

import jax
import jax.numpy as jnp
from jax import lax
from jax.experimental import pallas as pl
from jax.experimental.pallas import tpu as pltpu
from jax.sharding import PartitionSpec as P

GAMMA = 5.0 / 3.0
STEP = 0.02
HALF = 0.5 * STEP
FOOT = 4
SIDE = 5
CAP = 2
F32 = jnp.float32
VMEM = pltpu.VMEM
SMEM = pltpu.SMEM
MIB = 1024 * 1024
GRANT = 56 * MIB


def conserve(rho, ux, uy, uz, p):
    mx, my, mz = rho * ux, rho * uy, rho * uz
    xx, yy, zz = mx * ux, my * uy, mz * uz
    energy = 1.5 * p + 0.5 * (xx + yy + zz)
    return {
        "amounts": (rho, mx, my, mz, energy),
        "speed": (ux, uy, uz),
        "p": p,
        "square": (xx, yy, zz),
        "cross": {},
    }


def sound_of(p, rho):
    square = GAMMA * (p / rho)
    return square * lax.rsqrt(square)


def derive(prim):
    rho, p = prim[0], prim[4]
    both = rho + p
    common = p / (rho * both)
    square = GAMMA * (common * both)
    cell = conserve(*prim)
    cell["sound"] = square * lax.rsqrt(square)
    cell["share"] = common * rho
    return cell


def again(rho, ux, uy, uz, p, sound):
    cell = conserve(rho, ux, uy, uz, p)
    cell["sound"] = sound
    return cell


def directed(cell, d):
    amounts, p = cell["amounts"], cell["p"]
    u = cell["speed"][d]
    flux = [amounts[1 + d]]
    for k in range(3):
        if k == d:
            flux.append(cell["square"][d] + p)
            continue
        pair = (min(k, d), max(k, d))
        if pair not in cell["cross"]:
            cell["cross"][pair] = amounts[1 + pair[0]] * cell["speed"][pair[1]]
        flux.append(cell["cross"][pair])
    flux.append((amounts[4] + p) * u)
    return (amounts, flux, jnp.abs(u) + cell["sound"])


def twice_flux(left, right):
    fastest = jnp.maximum(left[2], right[2])
    return [
        (left[1][c] + right[1][c]) - fastest * (right[0][c] - left[0][c]) for c in range(5)
    ]


def shifted(cell, shift, axis):
    rho, p = cell["amounts"][0], cell["p"]
    values = (rho,) + cell["speed"] + (p, cell["sound"])
    return again(*[pltpu.roll(v, shift, axis) for v in values])


def source_term(rho, share, rates):
    heat, heat_slope, cool, cool_slope = rates
    return rho * ((heat + share * heat_slope) - rho * (cool + share * cool_slope))


def lane_pick(tile, lane):
    index = jnp.full((8, 128), lane, jnp.int32)
    return jnp.take_along_axis(tile, index, axis=1, mode="promise_in_bounds")


def plan_places(place_ref, host_ref, spot_ref, corner_ref, slot_ref):
    gx, me = place_ref[0], place_ref[1]
    rows = pl.ds(pl.multiple_of(8 * gx, 8), 8)
    hosts, spots = host_ref[rows, :], spot_ref[rows, :]
    lane = lax.broadcasted_iota(jnp.int32, (8, 128), 1)
    row = lax.broadcasted_iota(jnp.int32, (8, 128), 0)
    place_x = (spots * 43) >> 8
    corner = (1 + SIDE * place_x) * 32 + 1 + SIDE * (spots - 6 * place_x)
    key = jnp.where(hosts == me, lane * 1024 + corner, -1)
    table = jnp.full((8, 128), -1, jnp.int32)
    far = 1 << 20
    for q in range(4):
        inside = (lane // 32 == q) & (key >= 0)
        last = jnp.max(jnp.where(inside, key, -1), axis=1, keepdims=True)
        first = jnp.min(jnp.where(inside, key, far), axis=1, keepdims=True)
        none = last < 0
        single = none | (first == last)
        table = jnp.where(lane == 2 * q, jnp.where(none, -1, first & 1023), table)
        table = jnp.where(lane == 2 * q + 1, jnp.where(single, -1, last & 1023), table)
    corner_ref[...] = table
    own = jnp.sum(jnp.where(row == me // 4, hosts, 0), axis=0, keepdims=True)
    own = pltpu.roll(jnp.broadcast_to(own, (8, 128)), lax.rem(128 - 32 * lax.rem(me, 4), 128), 1)
    own = jnp.broadcast_to(own[0:1, :], (32, 128))
    lane = lax.broadcasted_iota(jnp.int32, (32, 128), 1)
    row = lax.broadcasted_iota(jnp.int32, (32, 128), 0)
    mine = jnp.sum(jnp.where(lane == row, own, 0), axis=1, keepdims=True)
    rank = jnp.sum(jnp.where((own == mine) & (lane < row), 1, 0), axis=1, keepdims=True)
    slot_ref[...] = jnp.broadcast_to(CAP * mine + rank, (32, 128))


def corner_at(corner_ref, s):
    line = s // 8
    return corner_ref[line, s - 8 * line]


def pack_kernel(
    place_ref, host_ref, spot_ref, rho_hbm, vel_hbm, p_hbm,
    rim_ref, xa_ref, xb_ref, ya_ref, yb_ref, corner_ref, slot_ref,
    cell_ref, table_ref, sem, table_sem,
):
    sources = [rho_hbm, vel_hbm.at[0], vel_hbm.at[1], vel_hbm.at[2], p_hbm]
    copies = [pltpu.make_async_copy(f, cell_ref.at[c], sem.at[c]) for c, f in enumerate(sources)]
    for copy in copies:
        copy.start()
    plan_places(place_ref, host_ref, spot_ref, corner_ref, slot_ref)
    move = pltpu.make_async_copy(corner_ref, table_ref, table_sem)
    move.start()
    move.wait()
    for copy in copies:
        copy.wait()
    fields = [cell_ref.at[c] for c in range(5)]
    width = 32
    rows = cell_ref.shape[1]

    def one(s, carry):
        base = corner_at(table_ref, s)

        @pl.when(base >= 0)
        def _():
            for c, f in enumerate(fields):
                rim_ref[s, c, 0:4, :] = f[pl.ds(base - width, 4), :]
                rim_ref[s, c, 4:8, :] = f[pl.ds(base + FOOT * width, 4), :]
                rim_ref[s, c, 8:12, :] = f[pl.ds(base - 1, 4, stride=width), :]
                rim_ref[s, c, 12:16, :] = f[pl.ds(base + FOOT, 4, stride=width), :]

        return carry

    lax.fori_loop(0, rim_ref.shape[0], one, 0)
    for c, f in enumerate(fields):
        xa_ref[c] = f[0:width, :]
        xb_ref[c] = f[rows - width : rows, :]
        ya_ref[c] = f[pl.ds(0, width, stride=width), :]
        yb_ref[c] = f[pl.ds(width - 1, width, stride=width), :]


def pack(place, hosts, spots, rho, vel, p, slots):
    whole = pl.BlockSpec(memory_space=VMEM)
    edge = jax.ShapeDtypeStruct((5, 32, 128), F32)
    return pl.pallas_call(
        pack_kernel,
        out_shape=[jax.ShapeDtypeStruct((slots, 5, 16, 128), F32), edge, edge, edge, edge]
        + [jax.ShapeDtypeStruct((8, 128), jnp.int32), jax.ShapeDtypeStruct((32, 128), jnp.int32)],
        in_specs=[pl.BlockSpec(memory_space=SMEM), whole, whole]
        + [pl.BlockSpec(memory_space=pl.ANY)] * 3,
        out_specs=[whole] * 7,
        scratch_shapes=[
            pltpu.VMEM((5,) + rho.shape, F32),
            pltpu.SMEM((8, 128), jnp.int32),
            pltpu.SemaphoreType.DMA((5,)),
            pltpu.SemaphoreType.DMA,
        ],
        compiler_params=pltpu.CompilerParams(vmem_limit_bytes=GRANT),
        cost_estimate=pl.CostEstimate(flops=0, bytes_accessed=6 * MIB, transcendentals=0),
        name="pack_rims",
    )(place, hosts, spots, rho, vel, p)


def rates_kernel(bins_ref, table_ref, out_ref):
    for g in range(bins_ref.shape[0] // 8):
        rows = slice(8 * g, 8 * g + 8)
        low = None
        for step in range(2):
            b = bins_ref[rows, :] + step
            line = b // 128
            lane = b - line * 128
            found = [jnp.zeros((8, 128), F32) for _ in range(2)]
            for r in range(16):
                hit = line == r
                for t in range(2):
                    entry = jnp.broadcast_to(table_ref[t, r : r + 1, :], (8, 128))
                    value = jnp.take_along_axis(entry, lane, axis=1, mode="promise_in_bounds")
                    found[t] = jnp.where(hit, value, found[t])
            for t in range(2):
                entry = found[t] if step == 0 else found[t] - low[t]
                out_ref[2 * t + step, rows, :] = STEP * entry
            low = found


def look_up(bins, tables):
    whole = pl.BlockSpec(memory_space=VMEM)
    return pl.pallas_call(
        rates_kernel,
        out_shape=jax.ShapeDtypeStruct((4,) + bins.shape, F32),
        in_specs=[whole, whole],
        out_specs=whole,
        cost_estimate=pl.CostEstimate(flops=MIB, bytes_accessed=MIB, transcendentals=0),
        name="rate_lookup",
    )(bins, tables)


PITCH = 48
LOW = 8


def coarse_kernel(
    corner_ref, rho_ref, vel_ref, p_ref, xlo_ref, xhi_ref, ylo_ref, yhi_ref, rate_ref,
    out_ref, cell_ref, fx_ref, fy_ref,
):
    width = 32
    fields = [rho_ref, vel_ref.at[0], vel_ref.at[1], vel_ref.at[2], p_ref]

    def keep(prim, index):
        for n, v in enumerate(prim):
            cell_ref[n, index, :] = v
        cell_ref[5, index, :] = sound_of(prim[4], prim[0])

    def fill(x, carry):
        for q in range(4):
            rows = pl.ds(x * width + 8 * q, 8)
            keep([f[rows, :] for f in fields], pl.ds((x + 1) * PITCH + LOW + 8 * q, 8))
        return carry

    lax.fori_loop(0, width, fill, 0)
    for q in range(4):
        rows = slice(8 * q, 8 * q + 8)
        keep([xlo_ref[c, rows, :] for c in range(5)], pl.ds(LOW + 8 * q, 8))
        keep([xhi_ref[c, rows, :] for c in range(5)], pl.ds(33 * PITCH + LOW + 8 * q, 8))
        first = (8 * q + 1) * PITCH + LOW
        keep([ylo_ref[c, rows, :] for c in range(5)], pl.ds(first - 1, 8, stride=PITCH))
        keep([yhi_ref[c, rows, :] for c in range(5)], pl.ds(first + width, 8, stride=PITCH))

    def fetch(row):
        return again(*[cell_ref[n, pl.ds(row, 8), :] for n in range(6)])

    def step(x, carry):
        result = []
        for q in range(4):
            below = carry[5 * q : 5 * q + 5]
            row = (x + 1) * PITCH + LOW + 8 * q
            here = fetch(row)
            above = twice_flux(directed(here, 0), directed(fetch(row + PITCH), 0))
            y_here = directed(here, 1)
            y_high = twice_flux(y_here, directed(fetch(row + 1), 1))
            y_low = twice_flux(directed(fetch(row - 1), 1), y_here)
            z_high = twice_flux(directed(here, 2), directed(shifted(here, 127, 1), 2))
            rates = [lane_pick(rate_ref[t, 16 + 8 * q : 24 + 8 * q, :], x) for t in range(4)]
            rho = here["amounts"][0]
            gain = source_term(rho, here["p"] / (rho + here["p"]), rates)
            flat = pl.ds(x * width + 8 * q, 8)
            for c in range(5):
                change = (
                    (above[c] - below[c])
                    + (y_high[c] - y_low[c])
                    + (z_high[c] - pltpu.roll(z_high[c], 1, 1))
                )
                value = here["amounts"][c] - HALF * change
                if c == 4:
                    value = value + gain
                out_ref[c, flat, :] = value
                fx_ref[c, flat, :] = above[c]
                fy_ref[c, flat, :] = y_high[c]
            result += above
        return tuple(result)

    first = []
    for q in range(4):
        row = LOW + 8 * q
        first += twice_flux(directed(fetch(row), 0), directed(fetch(row + PITCH), 0))
    lax.fori_loop(0, width, step, tuple(first))

    def reflux(s, carry):
        base = corner_at(corner_ref, s)

        @pl.when(base >= 0)
        def _():
            places = (
                (pl.ds(base - width, 4), pl.ds(base - width, 4), fx_ref, HALF),
                (
                    pl.ds(base + FOOT * width, 4),
                    pl.ds(base + (FOOT - 1) * width, 4),
                    fx_ref,
                    -HALF,
                ),
                (
                    pl.ds(base - 1, 4, stride=width),
                    pl.ds(base - 1, 4, stride=width),
                    fy_ref,
                    HALF,
                ),
                (
                    pl.ds(base + FOOT, 4, stride=width),
                    pl.ds(base + FOOT - 1, 4, stride=width),
                    fy_ref,
                    -HALF,
                ),
            )
            values = [
                [out_ref[c, a, :] + w * f[c, b, :] for a, b, f, w in places] for c in range(5)
            ]
            for c in range(5):
                for n in range(4):
                    out_ref[c, places[n][0], :] = values[c][n]

        return carry

    lax.fori_loop(0, 8 * corner_ref.shape[0], reflux, 0)


def coarse_step(corners, rho, vel, p, xlo, xhi, ylo, yhi, rates):
    whole = pl.BlockSpec(memory_space=VMEM)
    cells = rho.shape[0]
    return pl.pallas_call(
        coarse_kernel,
        out_shape=jax.ShapeDtypeStruct((5, cells, 128), F32),
        in_specs=[pl.BlockSpec(memory_space=SMEM)] + [whole] * 8,
        out_specs=whole,
        scratch_shapes=[
            pltpu.VMEM((6, 34 * PITCH, 128), F32),
            pltpu.VMEM((5, cells, 128), F32),
            pltpu.VMEM((5, cells, 128), F32),
        ],
        compiler_params=pltpu.CompilerParams(vmem_limit_bytes=32 * MIB),
        cost_estimate=pl.CostEstimate(
            flops=300 * cells * 128, bytes_accessed=30 * MIB, transcendentals=0
        ),
        name="coarse_step",
    )(corners, rho, vel, p, xlo, xhi, ylo, yhi, rates)


def take_lanes(tile, index):
    return jnp.take_along_axis(tile, index, axis=1, mode="promise_in_bounds")


def fold(even, odd):
    row = lax.broadcasted_iota(jnp.int32, (8, 128), 0)
    lane = lax.broadcasted_iota(jnp.int32, (8, 128), 1)
    halves = []
    for h in range(2):
        a, b = even[:, 128 * h : 128 * h + 128], odd[:, 128 * h : 128 * h + 128]
        a = a + pltpu.roll(a, 7, 0)
        b = b + pltpu.roll(b, 1, 0)
        m = jnp.where(row % 2 == 0, a, b)
        halves.append(m + pltpu.roll(m, 127 if h == 0 else 1, 1))
    mixed = jnp.where(lane % 2 == 0, halves[0], halves[1])
    return take_lanes(mixed, jnp.where(lane < 64, 2 * lane, 2 * lane - 127))


def patch_update(prim_refs, p_index, rates_at, faces, emit, on_plane=None):
    row = lax.broadcasted_iota(jnp.int32, (8, 256), 0)
    cells, fluxes, x_flux = {}, {}, {}
    x_flux[-1] = None if faces is None else [faces(c, 0, slice(0, 8)) for c in range(5)]
    x_flux[7] = None if faces is None else [faces(c, 1, slice(0, 8)) for c in range(5)]

    def enter(i):
        prim = [f[p_index, 8 * i : 8 * i + 8, :] for f in prim_refs]
        if on_plane is not None:
            on_plane(i, prim)
        here = derive(prim)
        cells[i] = (here, shifted(here, 7, 0), shifted(here, 255, 1), rates_at(i))

    def cross(i):
        here, y_next, z_next, _ = cells[i]
        y_flux = twice_flux(directed(here, 1), directed(y_next, 1))
        z_flux = twice_flux(directed(here, 2), directed(z_next, 2))
        y_back = [pltpu.roll(v, 1, 0) for v in y_flux]
        z_back = [pltpu.roll(v, 1, 1) for v in z_flux]
        fluxes[i] = (y_flux, y_back, z_flux, z_back)
        if i < 7:
            x_flux[i] = None
            if faces is not None or i % 2 == 1:
                x_flux[i] = twice_flux(directed(here, 0), directed(cells[i + 1][0], 0))

    def leave(i):
        here, _, _, rates = cells.pop(i)
        y_flux, y_back, z_flux, z_back = fluxes.pop(i)
        gain = source_term(here["amounts"][0], here["share"], rates)
        result = []
        for c in range(5):
            if faces is None:
                y_high, y_low = 0.0, 0.0
            else:
                y_high = jnp.broadcast_to(faces(c, 3, slice(i, i + 1)), (8, 256))
                y_low = jnp.broadcast_to(faces(c, 2, slice(i, i + 1)), (8, 256))
            change = jnp.where(row == 7, y_high, y_flux[c]) - jnp.where(
                row == 0, y_low, y_back[c]
            )
            change = change + (z_flux[c] - z_back[c])
            if x_flux[i] is not None:
                change = change + x_flux[i][c]
            if x_flux[i - 1] is not None:
                change = change - x_flux[i - 1][c]
            value = here["amounts"][c] - STEP * change
            if c == 4:
                value = value + gain
            result.append(value)
        emit(i, result)

    enter(0)
    for i in range(9):
        if i < 7:
            enter(i + 1)
        if i < 8:
            cross(i)
        if i > 0:
            leave(i - 1)


def rates_reader(rate_ref, patch):
    half = patch // 16
    start = pl.multiple_of(8 * half, 8)
    shift = 128 - 8 * (patch - 16 * half)
    tiles = [pltpu.roll(rate_ref[t, pl.ds(start, 8), :], shift, 1) for t in range(4)]

    def rates_at(i):
        return [jnp.broadcast_to(v[:, i : i + 1], (8, 256)) for v in tiles]

    return rates_at


PER = 4


def open_kernel(
    slot_ref, rho_ref, ux_ref, uy_ref, uz_ref, p_ref, rate_ref, mean_ref, edge_ref
):
    refs = [rho_ref, ux_ref.at[0], uy_ref.at[0], uz_ref.at[0], p_ref]

    def one(n, carry):
        patch = pl.program_id(0) * PER + n
        slot = slot_ref[patch, 0]

        def on_plane(i, prim):
            for c in range(5):
                if i == 0:
                    edge_ref[n, c, 0] = prim[c]
                if i == 7:
                    edge_ref[n, c, 1] = prim[c]
                edge_ref[n, c, 2, i : i + 1, :] = prim[c][0:1, :]
                edge_ref[n, c, 3, i : i + 1, :] = prim[c][7:8, :]

        held = {}

        def emit(i, result):
            for c in range(5):
                at = (i // 2, c)
                held[at] = result[c] if i % 2 == 0 else held[at] + result[c]
                if i % 4 == 3:
                    value = fold(held.pop((i // 2 - 1, c)), held.pop(at))
                    mean_ref[slot, c, 8 * (i // 4) : 8 * (i // 4) + 8, :] = 0.125 * value

        patch_update(refs, n, rates_reader(rate_ref, patch), None, emit, on_plane)
        return carry

    lax.fori_loop(0, PER, one, 0)


def patch_specs(extra):
    one = pl.BlockSpec((PER, 64, 256), lambda i: (i, 0, 0))
    speed = [pl.BlockSpec((1, PER, 64, 256), lambda i, d=d: (d, i, 0, 0)) for d in range(3)]
    return [pl.BlockSpec(memory_space=SMEM)] * extra + [one] + speed + [one]


def open_patches(slot, rho, vel, p, rates, slots):
    count = rho.shape[0]
    return pl.pallas_call(
        open_kernel,
        grid=(count // PER,),
        out_shape=[
            jax.ShapeDtypeStruct((slots, 5, 32, 128), F32),
            jax.ShapeDtypeStruct((count, 5, 4, 8, 256), F32),
        ],
        in_specs=patch_specs(1) + [pl.BlockSpec(memory_space=VMEM)],
        out_specs=[
            pl.BlockSpec((slots, 5, 16, 128), lambda i: (0, 0, 0, 0)),
            pl.BlockSpec((PER, 5, 4, 8, 256), lambda i: (i, 0, 0, 0, 0)),
        ],
        compiler_params=pltpu.CompilerParams(vmem_limit_bytes=GRANT),
        cost_estimate=pl.CostEstimate(
            flops=250 * count * 64 * 256, bytes_accessed=18 * MIB, transcendentals=0
        ),
        name="open_patches",
    )(slot, rho, vel, vel, vel, p, rates)


BATCH = 4


def side_fluxes(rim, edge, ghost_ref):
    lane = lax.broadcasted_iota(jnp.int32, (16, 128), 1) // 2
    coarse = list(rim)
    coarse.append(sound_of(coarse[4], coarse[0]))
    for c in range(6):
        for h in range(2):
            wide = take_lanes(coarse[c], lane + 64 * h)
            ghost_ref[c, h, pl.ds(0, 16, stride=2), :] = wide
            ghost_ref[c, h, pl.ds(1, 16, stride=2), :] = wide
    sides = []
    for side in range(4):
        rows = slice(8 * side, 8 * side + 8)
        outer = [
            jnp.concatenate([ghost_ref[c, 0, rows, :], ghost_ref[c, 1, rows, :]], axis=1)
            for c in range(6)
        ]
        d = side // 2
        ghost = directed(again(*outer), d)
        prim = edge(side)
        inner = directed(again(*prim, sound_of(prim[4], prim[0])), d)
        sides.append(twice_flux(ghost, inner) if side % 2 == 0 else twice_flux(inner, ghost))
    return sides


def face_kernel(
    slot_ref, rim_hbm, edge_hbm, _, out_hbm,
    rim_ref, edge_ref, sum_ref, ghost_ref, rim_sem, edge_sem, sum_sem,
):
    count = edge_ref.shape[0]

    def load(g):
        part = pl.ds(g * BATCH, BATCH)
        return pltpu.make_async_copy(edge_hbm.at[part], edge_ref.at[part], edge_sem.at[g])

    def save(p):
        place = out_hbm.at[slot_ref[p, 0], :, pl.ds(16, 16), :]
        return pltpu.make_async_copy(sum_ref.at[p], place, sum_sem.at[p])

    def fetch(p):
        return pltpu.make_async_copy(rim_hbm.at[slot_ref[p, 0]], rim_ref.at[p], rim_sem.at[p])

    for g in range(count // BATCH):
        load(g).start()
        for n in range(BATCH):
            fetch(g * BATCH + n).start()

    def chunk(g, carry):
        load(g).wait()
        for n in range(BATCH):
            fetch(g * BATCH + n).wait()
        for n in range(BATCH):
            p = g * BATCH + n
            sides = side_fluxes(
                [rim_ref[p, c] for c in range(5)],
                lambda side, p=p: [edge_ref[p, c, side] for c in range(5)],
                ghost_ref.at[n],
            )
            for c in range(5):
                for d in range(2):
                    value = fold(sides[2 * d][c], sides[2 * d + 1][c])
                    sum_ref[p, c, 8 * d : 8 * d + 8, :] = (0.125 * STEP) * value
        for n in range(BATCH):
            save(g * BATCH + n).start()
        return carry

    lax.fori_loop(0, count // BATCH, chunk, 0)

    def settle(p, carry):
        save(p).wait()
        return carry

    lax.fori_loop(0, count, settle, 0)


def face_fluxes(slot, rims, edges, buffer):
    count = edges.shape[0]
    anywhere = pl.BlockSpec(memory_space=pl.ANY)
    return pl.pallas_call(
        face_kernel,
        out_shape=jax.ShapeDtypeStruct(buffer.shape, F32),
        in_specs=[
            pl.BlockSpec(memory_space=SMEM),
            anywhere,
            anywhere,
            anywhere,
        ],
        out_specs=anywhere,
        input_output_aliases={3: 0},
        scratch_shapes=[
            pltpu.VMEM((count, 5, 16, 128), F32),
            pltpu.VMEM(edges.shape, F32),
            pltpu.VMEM((count, 5, 16, 128), F32),
            pltpu.VMEM((BATCH, 6, 2, 32, 128), F32),
            pltpu.SemaphoreType.DMA((count,)),
            pltpu.SemaphoreType.DMA((count // BATCH,)),
            pltpu.SemaphoreType.DMA((count,)),
        ],
        compiler_params=pltpu.CompilerParams(vmem_limit_bytes=62 * MIB),
        cost_estimate=pl.CostEstimate(
            flops=100 * count * 32 * 256, bytes_accessed=11 * MIB, transcendentals=0
        ),
        name="face_fluxes",
    )(slot, rims, edges, buffer)


def close_kernel(
    slot_ref, rho_ref, ux_ref, uy_ref, uz_ref, p_ref, rate_ref, rim_ref, edge_ref,
    out_ref, ghost_ref, rows_ref,
):
    refs = [rho_ref, ux_ref.at[0], uy_ref.at[0], uz_ref.at[0], p_ref]

    def one(n, carry):
        patch = pl.program_id(0) * PER + n
        slot = slot_ref[patch, 0]
        sides = side_fluxes(
            [rim_ref[slot, c] for c in range(5)],
            lambda side: [edge_ref[n, c, side] for c in range(5)],
            ghost_ref,
        )
        for c in range(5):
            for d in range(2):
                rows_ref[c, d] = sides[2 + d][c]

        def faces(c, side, rows):
            return sides[side][c] if side < 2 else rows_ref[c, side - 2, rows, :]

        def emit(i, result):
            for c in range(5):
                out_ref[c, n, 8 * i : 8 * i + 8, :] = result[c]

        patch_update(refs, n, rates_reader(rate_ref, patch), faces, emit)
        return carry

    lax.fori_loop(0, PER, one, 0)


def close_patches(slot, rho, vel, p, rates, rims, edges):
    count = rho.shape[0]
    return pl.pallas_call(
        close_kernel,
        grid=(count // PER,),
        out_shape=jax.ShapeDtypeStruct((5,) + rho.shape, F32),
        in_specs=patch_specs(1)
        + [
            pl.BlockSpec(memory_space=VMEM),
            pl.BlockSpec(rims.shape, lambda i: (0, 0, 0, 0)),
            pl.BlockSpec((PER, 5, 4, 8, 256), lambda i: (i, 0, 0, 0, 0)),
        ],
        out_specs=pl.BlockSpec((5, PER, 64, 256), lambda i: (0, i, 0, 0)),
        scratch_shapes=[
            pltpu.VMEM((6, 2, 32, 128), F32),
            pltpu.VMEM((5, 2, 8, 256), F32),
        ],
        compiler_params=pltpu.CompilerParams(vmem_limit_bytes=20 * MIB),
        cost_estimate=pl.CostEstimate(
            flops=250 * count * 64 * 256, bytes_accessed=29 * MIB, transcendentals=0
        ),
        name="close_patches",
    )(slot, rho, vel, vel, vel, p, rates, rims, edges)


CHUNKS = 4


def merge_kernel(corner_ref, base_ref, got_hbm, out_ref, got_ref, sem):
    width = 32
    slots = got_ref.shape[0]

    size = slots // CHUNKS

    def fetch(g):
        part = pl.ds(g * size, size)
        return pltpu.make_async_copy(got_hbm.at[part], got_ref.at[part], sem.at[g])

    for g in range(CHUNKS):
        fetch(g).start()
    out_ref[...] = base_ref[...]
    row = lax.broadcasted_iota(jnp.int32, (4, 128), 0)

    def one(s, carry):
        base = corner_at(corner_ref, s)

        @pl.when(base >= 0)
        def _():
            rims = (
                pl.ds(base - width, 4),
                pl.ds(base + FOOT * width, 4),
                pl.ds(base - 1, 4, stride=width),
                pl.ds(base + FOOT, 4, stride=width),
            )
            result = []
            for c in range(5):
                flux = [
                    got_ref[s, c, pl.ds(16 + 8 * (n // 2) + n % 2, 4, stride=2), :]
                    for n in range(4)
                ]
                rim = [out_ref[c, at, :] for at in rims]
                rim = [rim[n] + flux[n] if n % 2 else rim[n] - flux[n] for n in range(4)]
                foot = []
                for i in range(4):
                    v = got_ref[s, c, pl.ds(8 * (i // 2) + i % 2, 4, stride=2), :]
                    if i == 0:
                        v = v + flux[0]
                    if i == 3:
                        v = v - flux[1]
                    low = jnp.broadcast_to(flux[2][i : i + 1, :], (4, 128))
                    high = jnp.broadcast_to(flux[3][i : i + 1, :], (4, 128))
                    v = v + jnp.where(row == 0, low, 0.0) - jnp.where(row == 3, high, 0.0)
                    foot.append(v)
                result.append((rim, foot))
            for c in range(5):
                rim, foot = result[c]
                for at, v in zip(rims, rim):
                    out_ref[c, at, :] = v
                for i in range(4):
                    out_ref[c, pl.ds(base + i * width, 4), :] = foot[i]

        return carry

    for g in range(CHUNKS):
        fetch(g).wait()
        lax.fori_loop(g * size, (g + 1) * size, one, 0)


def merge(corners, base, got):
    whole = pl.BlockSpec(memory_space=VMEM)
    return pl.pallas_call(
        merge_kernel,
        out_shape=jax.ShapeDtypeStruct(base.shape, F32),
        in_specs=[pl.BlockSpec(memory_space=SMEM), whole, pl.BlockSpec(memory_space=pl.ANY)],
        out_specs=whole,
        scratch_shapes=[pltpu.VMEM(got.shape, F32), pltpu.SemaphoreType.DMA((CHUNKS,))],
        compiler_params=pltpu.CompilerParams(vmem_limit_bytes=24 * MIB),
        cost_estimate=pl.CostEstimate(flops=MIB, bytes_accessed=11 * MIB, transcendentals=0),
        name="merge_patches",
    )(corners, base, got)


def exchange(buffer, groups):
    shape = buffer.shape
    rows = buffer.size // (groups * 128)
    moved = lax.all_to_all(
        buffer.reshape(groups, rows, 128), "yz", split_axis=0, concat_axis=0, tiled=True
    )
    return moved.reshape(shape)


def local(
    coarse_density,
    coarse_velocity,
    coarse_pressure,
    coarse_bins,
    fine_density,
    fine_velocity,
    fine_pressure,
    fine_bins,
    patch_host,
    patch_spot,
    heat_rate,
    cool_rate,
):
    groups = lax.axis_size("yz")
    rows = lax.axis_size("gx")
    gx = lax.axis_index("gx")
    me = lax.axis_index("yz")
    count = fine_density.shape[0]
    slots = CAP * groups

    rho = coarse_density.reshape(-1, 128)
    vel = coarse_velocity.reshape(3, -1, 128)
    press = coarse_pressure.reshape(-1, 128)
    place = jnp.stack([gx, me]).astype(jnp.int32)
    host_lines, spot_lines = patch_host.reshape(-1, 128), patch_spot.reshape(-1, 128)
    rims, x_first, x_last, y_first, y_last, corners, slot = pack(
        place, host_lines, spot_lines, rho, vel, press, slots
    )
    arrived = exchange(rims, groups)

    up_x = [(i, (i + 1) % rows) for i in range(rows)]
    down_x = [((i + 1) % rows, i) for i in range(rows)]
    up_y = [(i, (i + 1) % groups) for i in range(groups)]
    down_y = [((i + 1) % groups, i) for i in range(groups)]
    x_low = lax.ppermute(x_last, "gx", up_x)
    x_high = lax.ppermute(x_first, "gx", down_x)
    y_low = lax.ppermute(y_last, "yz", up_y)
    y_high = lax.ppermute(y_first, "yz", down_y)

    fine_columns = fine_bins.reshape(2, 16, 8, 8).transpose(0, 3, 1, 2).reshape(16, 128)
    coarse_columns = jnp.pad(coarse_bins.T, ((0, 0), (0, 128 - coarse_bins.shape[0])))
    tables = jnp.pad(jnp.stack([heat_rate, cool_rate]), ((0, 0), (0, 48))).reshape(2, 16, 128)
    rates = look_up(jnp.concatenate([fine_columns, coarse_columns], axis=0), tables)

    f_rho = fine_density.reshape(count, 64, 256)
    f_vel = fine_velocity.reshape(3, count, 64, 256)
    f_press = fine_pressure.reshape(count, 64, 256)
    means, edges = open_patches(slot, f_rho, f_vel, f_press, rates, slots)
    sums = face_fluxes(slot, arrived, edges, means)
    sums, x_low, x_high, y_low, y_high = lax.optimization_barrier(
        (sums, x_low, x_high, y_low, y_high)
    )
    got = exchange(sums, groups)
    base = coarse_step(corners, rho, vel, press, x_low, x_high, y_low, y_high, rates)
    fine_new = close_patches(slot, f_rho, f_vel, f_press, rates, arrived, edges)
    coarse_new = merge(corners, base, got)
    return (
        coarse_new.reshape((5,) + coarse_density.shape),
        fine_new.reshape((5,) + fine_density.shape),
    )


def solution(mesh):
    placed = (
        P("gx", "yz", None),
        P(None, "gx", "yz", None),
        P("gx", "yz", None),
        P("gx", "yz"),
        P(("gx", "yz"), None, None, None),
        P(None, ("gx", "yz"), None, None, None),
        P(("gx", "yz"), None, None, None),
        P(("gx", "yz"), None, None),
        P(),
        P(),
        P(),
        P(),
    )
    return jax.shard_map(
        local,
        mesh=mesh,
        in_specs=placed,
        out_specs=(P(None, "gx", "yz", None), P(None, ("gx", "yz"), None, None, None)),
        check_vma=False,
    )
```

```python
import functools

import jax
import jax.numpy as jnp
from jax import lax
from jax.experimental import pallas as pl
from jax.experimental.pallas import tpu as pltpu
from jax.sharding import PartitionSpec as P

GAMMA = 5.0 / 3.0
STEP = 0.02
HALF = 0.5 * STEP
FOOT = 4
SIDE = 5
CAP = 2
F32 = jnp.float32
VMEM = pltpu.VMEM
SMEM = pltpu.SMEM
MIB = 1024 * 1024
GRANT = 56 * MIB


def conserve(rho, ux, uy, uz, p):
    mx, my, mz = rho * ux, rho * uy, rho * uz
    xx, yy, zz = mx * ux, my * uy, mz * uz
    energy = 1.5 * p + 0.5 * (xx + yy + zz)
    return {
        "amounts": (rho, mx, my, mz, energy),
        "speed": (ux, uy, uz),
        "p": p,
        "square": (xx, yy, zz),
        "cross": {},
    }


def sound_of(p, rho):
    square = GAMMA * (p / rho)
    return square * lax.rsqrt(square)


def derive(prim):
    rho, p = prim[0], prim[4]
    both = rho + p
    common = p / (rho * both)
    square = GAMMA * (common * both)
    cell = conserve(*prim)
    cell["sound"] = square * lax.rsqrt(square)
    cell["share"] = common * rho
    return cell


def again(rho, ux, uy, uz, p, sound):
    cell = conserve(rho, ux, uy, uz, p)
    cell["sound"] = sound
    return cell


def directed(cell, d):
    amounts, p = cell["amounts"], cell["p"]
    u = cell["speed"][d]
    flux = [amounts[1 + d]]
    for k in range(3):
        if k == d:
            flux.append(cell["square"][d] + p)
            continue
        pair = (min(k, d), max(k, d))
        if pair not in cell["cross"]:
            cell["cross"][pair] = amounts[1 + pair[0]] * cell["speed"][pair[1]]
        flux.append(cell["cross"][pair])
    flux.append((amounts[4] + p) * u)
    return (amounts, flux, jnp.abs(u) + cell["sound"])


def twice_flux(left, right):
    fastest = jnp.maximum(left[2], right[2])
    return [
        (left[1][c] + right[1][c]) - fastest * (right[0][c] - left[0][c]) for c in range(5)
    ]


def shifted(cell, shift, axis):
    rho, p = cell["amounts"][0], cell["p"]
    values = (rho,) + cell["speed"] + (p, cell["sound"])
    return again(*[pltpu.roll(v, shift, axis) for v in values])


def source_term(rho, share, rates):
    heat, heat_slope, cool, cool_slope = rates
    return rho * ((heat + share * heat_slope) - rho * (cool + share * cool_slope))


def lane_pick(tile, lane):
    index = jnp.full((8, 128), lane, jnp.int32)
    return jnp.take_along_axis(tile, index, axis=1, mode="promise_in_bounds")


def plan_places(place_ref, host_ref, spot_ref, corner_ref, slot_ref):
    gx, me = place_ref[0], place_ref[1]
    rows = pl.ds(pl.multiple_of(8 * gx, 8), 8)
    hosts, spots = host_ref[rows, :], spot_ref[rows, :]
    lane = lax.broadcasted_iota(jnp.int32, (8, 128), 1)
    row = lax.broadcasted_iota(jnp.int32, (8, 128), 0)
    place_x = (spots * 43) >> 8
    corner = (1 + SIDE * place_x) * 32 + 1 + SIDE * (spots - 6 * place_x)
    key = jnp.where(hosts == me, lane * 1024 + corner, -1)
    table = jnp.full((8, 128), -1, jnp.int32)
    far = 1 << 20
    for q in range(4):
        inside = (lane // 32 == q) & (key >= 0)
        last = jnp.max(jnp.where(inside, key, -1), axis=1, keepdims=True)
        first = jnp.min(jnp.where(inside, key, far), axis=1, keepdims=True)
        none = last < 0
        single = none | (first == last)
        table = jnp.where(lane == 2 * q, jnp.where(none, -1, first & 1023), table)
        table = jnp.where(lane == 2 * q + 1, jnp.where(single, -1, last & 1023), table)
    corner_ref[...] = table
    own = jnp.sum(jnp.where(row == me // 4, hosts, 0), axis=0, keepdims=True)
    own = pltpu.roll(jnp.broadcast_to(own, (8, 128)), lax.rem(128 - 32 * lax.rem(me, 4), 128), 1)
    own = jnp.broadcast_to(own[0:1, :], (32, 128))
    lane = lax.broadcasted_iota(jnp.int32, (32, 128), 1)
    row = lax.broadcasted_iota(jnp.int32, (32, 128), 0)
    mine = jnp.sum(jnp.where(lane == row, own, 0), axis=1, keepdims=True)
    rank = jnp.sum(jnp.where((own == mine) & (lane < row), 1, 0), axis=1, keepdims=True)
    slot_ref[...] = jnp.broadcast_to(CAP * mine + rank, (32, 128))


def corner_at(corner_ref, s):
    line = s // 8
    return corner_ref[line, s - 8 * line]


def pack_kernel(
    place_ref, host_ref, spot_ref, rho_hbm, vel_hbm, p_hbm,
    rim_ref, xa_ref, xb_ref, ya_ref, yb_ref, corner_ref, slot_ref,
    cell_ref, table_ref, sem, table_sem,
):
    sources = [rho_hbm, vel_hbm.at[0], vel_hbm.at[1], vel_hbm.at[2], p_hbm]
    copies = [pltpu.make_async_copy(f, cell_ref.at[c], sem.at[c]) for c, f in enumerate(sources)]
    for copy in copies:
        copy.start()
    plan_places(place_ref, host_ref, spot_ref, corner_ref, slot_ref)
    move = pltpu.make_async_copy(corner_ref, table_ref, table_sem)
    move.start()
    move.wait()
    for copy in copies:
        copy.wait()
    fields = [cell_ref.at[c] for c in range(5)]
    width = 32
    rows = cell_ref.shape[1]

    def one(s, carry):
        base = corner_at(table_ref, s)

        @pl.when(base >= 0)
        def _():
            for c, f in enumerate(fields):
                rim_ref[s, c, 0:4, :] = f[pl.ds(base - width, 4), :]
                rim_ref[s, c, 4:8, :] = f[pl.ds(base + FOOT * width, 4), :]
                rim_ref[s, c, 8:12, :] = f[pl.ds(base - 1, 4, stride=width), :]
                rim_ref[s, c, 12:16, :] = f[pl.ds(base + FOOT, 4, stride=width), :]

        return carry

    lax.fori_loop(0, rim_ref.shape[0], one, 0)
    for c, f in enumerate(fields):
        xa_ref[c] = f[0:width, :]
        xb_ref[c] = f[rows - width : rows, :]
        ya_ref[c] = f[pl.ds(0, width, stride=width), :]
        yb_ref[c] = f[pl.ds(width - 1, width, stride=width), :]


def pack(place, hosts, spots, rho, vel, p, slots):
    whole = pl.BlockSpec(memory_space=VMEM)
    edge = jax.ShapeDtypeStruct((5, 32, 128), F32)
    return pl.pallas_call(
        pack_kernel,
        out_shape=[jax.ShapeDtypeStruct((slots, 5, 16, 128), F32), edge, edge, edge, edge]
        + [jax.ShapeDtypeStruct((8, 128), jnp.int32), jax.ShapeDtypeStruct((32, 128), jnp.int32)],
        in_specs=[pl.BlockSpec(memory_space=SMEM), whole, whole]
        + [pl.BlockSpec(memory_space=pl.ANY)] * 3,
        out_specs=[whole] * 7,
        scratch_shapes=[
            pltpu.VMEM((5,) + rho.shape, F32),
            pltpu.SMEM((8, 128), jnp.int32),
            pltpu.SemaphoreType.DMA((5,)),
            pltpu.SemaphoreType.DMA,
        ],
        compiler_params=pltpu.CompilerParams(vmem_limit_bytes=GRANT),
        cost_estimate=pl.CostEstimate(flops=0, bytes_accessed=6 * MIB, transcendentals=0),
        name="pack_rims",
    )(place, hosts, spots, rho, vel, p)


def rates_kernel(bins_ref, table_ref, out_ref):
    for g in range(bins_ref.shape[0] // 8):
        rows = slice(8 * g, 8 * g + 8)
        low = None
        for step in range(2):
            b = bins_ref[rows, :] + step
            line = b // 128
            lane = b - line * 128
            found = [jnp.zeros((8, 128), F32) for _ in range(2)]
            for r in range(16):
                hit = line == r
                for t in range(2):
                    entry = jnp.broadcast_to(table_ref[t, r : r + 1, :], (8, 128))
                    value = jnp.take_along_axis(entry, lane, axis=1, mode="promise_in_bounds")
                    found[t] = jnp.where(hit, value, found[t])
            for t in range(2):
                entry = found[t] if step == 0 else found[t] - low[t]
                out_ref[2 * t + step, rows, :] = STEP * entry
            low = found


def look_up(bins, tables):
    whole = pl.BlockSpec(memory_space=VMEM)
    return pl.pallas_call(
        rates_kernel,
        out_shape=jax.ShapeDtypeStruct((4,) + bins.shape, F32),
        in_specs=[whole, whole],
        out_specs=whole,
        cost_estimate=pl.CostEstimate(flops=MIB, bytes_accessed=MIB, transcendentals=0),
        name="rate_lookup",
    )(bins, tables)


PITCH = 48
LOW = 8


def coarse_kernel(
    corner_ref, rho_ref, vel_ref, p_ref, xlo_ref, xhi_ref, ylo_ref, yhi_ref, rate_ref,
    out_ref, cell_ref, fx_ref, fy_ref,
):
    width = 32
    fields = [rho_ref, vel_ref.at[0], vel_ref.at[1], vel_ref.at[2], p_ref]

    def keep(prim, index):
        for n, v in enumerate(prim):
            cell_ref[n, index, :] = v
        cell_ref[5, index, :] = sound_of(prim[4], prim[0])

    def fill(x, carry):
        for q in range(4):
            rows = pl.ds(x * width + 8 * q, 8)
            keep([f[rows, :] for f in fields], pl.ds((x + 1) * PITCH + LOW + 8 * q, 8))
        return carry

    lax.fori_loop(0, width, fill, 0)
    for q in range(4):
        rows = slice(8 * q, 8 * q + 8)
        keep([xlo_ref[c, rows, :] for c in range(5)], pl.ds(LOW + 8 * q, 8))
        keep([xhi_ref[c, rows, :] for c in range(5)], pl.ds(33 * PITCH + LOW + 8 * q, 8))
        first = (8 * q + 1) * PITCH + LOW
        keep([ylo_ref[c, rows, :] for c in range(5)], pl.ds(first - 1, 8, stride=PITCH))
        keep([yhi_ref[c, rows, :] for c in range(5)], pl.ds(first + width, 8, stride=PITCH))

    def fetch(row):
        return again(*[cell_ref[n, pl.ds(row, 8), :] for n in range(6)])

    def step(x, carry):
        result = []
        for q in range(4):
            below = carry[5 * q : 5 * q + 5]
            row = (x + 1) * PITCH + LOW + 8 * q
            here = fetch(row)
            above = twice_flux(directed(here, 0), directed(fetch(row + PITCH), 0))
            y_here = directed(here, 1)
            y_high = twice_flux(y_here, directed(fetch(row + 1), 1))
            y_low = twice_flux(directed(fetch(row - 1), 1), y_here)
            z_high = twice_flux(directed(here, 2), directed(shifted(here, 127, 1), 2))
            rates = [lane_pick(rate_ref[t, 16 + 8 * q : 24 + 8 * q, :], x) for t in range(4)]
            rho = here["amounts"][0]
            gain = source_term(rho, here["p"] / (rho + here["p"]), rates)
            flat = pl.ds(x * width + 8 * q, 8)
            for c in range(5):
                change = (
                    (above[c] - below[c])
                    + (y_high[c] - y_low[c])
                    + (z_high[c] - pltpu.roll(z_high[c], 1, 1))
                )
                value = here["amounts"][c] - HALF * change
                if c == 4:
                    value = value + gain
                out_ref[c, flat, :] = value
                fx_ref[c, flat, :] = above[c]
                fy_ref[c, flat, :] = y_high[c]
            result += above
        return tuple(result)

    first = []
    for q in range(4):
        row = LOW + 8 * q
        first += twice_flux(directed(fetch(row), 0), directed(fetch(row + PITCH), 0))
    lax.fori_loop(0, width, step, tuple(first))

    def reflux(s, carry):
        base = corner_at(corner_ref, s)

        @pl.when(base >= 0)
        def _():
            places = (
                (pl.ds(base - width, 4), pl.ds(base - width, 4), fx_ref, HALF),
                (
                    pl.ds(base + FOOT * width, 4),
                    pl.ds(base + (FOOT - 1) * width, 4),
                    fx_ref,
                    -HALF,
                ),
                (
                    pl.ds(base - 1, 4, stride=width),
                    pl.ds(base - 1, 4, stride=width),
                    fy_ref,
                    HALF,
                ),
                (
                    pl.ds(base + FOOT, 4, stride=width),
                    pl.ds(base + FOOT - 1, 4, stride=width),
                    fy_ref,
                    -HALF,
                ),
            )
            values = [
                [out_ref[c, a, :] + w * f[c, b, :] for a, b, f, w in places] for c in range(5)
            ]
            for c in range(5):
                for n in range(4):
                    out_ref[c, places[n][0], :] = values[c][n]

        return carry

    lax.fori_loop(0, 8 * corner_ref.shape[0], reflux, 0)


def coarse_step(corners, rho, vel, p, xlo, xhi, ylo, yhi, rates):
    whole = pl.BlockSpec(memory_space=VMEM)
    cells = rho.shape[0]
    return pl.pallas_call(
        coarse_kernel,
        out_shape=jax.ShapeDtypeStruct((5, cells, 128), F32),
        in_specs=[pl.BlockSpec(memory_space=SMEM)] + [whole] * 8,
        out_specs=whole,
        scratch_shapes=[
            pltpu.VMEM((6, 34 * PITCH, 128), F32),
            pltpu.VMEM((5, cells, 128), F32),
            pltpu.VMEM((5, cells, 128), F32),
        ],
        compiler_params=pltpu.CompilerParams(vmem_limit_bytes=32 * MIB),
        cost_estimate=pl.CostEstimate(
            flops=300 * cells * 128, bytes_accessed=30 * MIB, transcendentals=0
        ),
        name="coarse_step",
    )(corners, rho, vel, p, xlo, xhi, ylo, yhi, rates)


def take_lanes(tile, index):
    return jnp.take_along_axis(tile, index, axis=1, mode="promise_in_bounds")


def fold(even, odd):
    row = lax.broadcasted_iota(jnp.int32, (8, 128), 0)
    lane = lax.broadcasted_iota(jnp.int32, (8, 128), 1)
    halves = []
    for h in range(2):
        a, b = even[:, 128 * h : 128 * h + 128], odd[:, 128 * h : 128 * h + 128]
        a = a + pltpu.roll(a, 7, 0)
        b = b + pltpu.roll(b, 1, 0)
        m = jnp.where(row % 2 == 0, a, b)
        halves.append(m + pltpu.roll(m, 127 if h == 0 else 1, 1))
    mixed = jnp.where(lane % 2 == 0, halves[0], halves[1])
    return take_lanes(mixed, jnp.where(lane < 64, 2 * lane, 2 * lane - 127))


def patch_update(prim_refs, p_index, rates_at, faces, emit, on_plane=None):
    row = lax.broadcasted_iota(jnp.int32, (8, 256), 0)
    cells, fluxes, x_flux = {}, {}, {}
    x_flux[-1] = None if faces is None else [faces(c, 0, slice(0, 8)) for c in range(5)]
    x_flux[7] = None if faces is None else [faces(c, 1, slice(0, 8)) for c in range(5)]

    def enter(i):
        prim = [f[p_index, 8 * i : 8 * i + 8, :] for f in prim_refs]
        if on_plane is not None:
            on_plane(i, prim)
        here = derive(prim)
        cells[i] = (here, shifted(here, 7, 0), shifted(here, 255, 1), rates_at(i))

    def cross(i):
        here, y_next, z_next, _ = cells[i]
        y_flux = twice_flux(directed(here, 1), directed(y_next, 1))
        z_flux = twice_flux(directed(here, 2), directed(z_next, 2))
        y_back = [pltpu.roll(v, 1, 0) for v in y_flux]
        z_back = [pltpu.roll(v, 1, 1) for v in z_flux]
        fluxes[i] = (y_flux, y_back, z_flux, z_back)
        if i < 7:
            x_flux[i] = None
            if faces is not None or i % 2 == 1:
                x_flux[i] = twice_flux(directed(here, 0), directed(cells[i + 1][0], 0))

    def leave(i):
        here, _, _, rates = cells.pop(i)
        y_flux, y_back, z_flux, z_back = fluxes.pop(i)
        gain = source_term(here["amounts"][0], here["share"], rates)
        result = []
        for c in range(5):
            if faces is None:
                y_high, y_low = 0.0, 0.0
            else:
                y_high = jnp.broadcast_to(faces(c, 3, slice(i, i + 1)), (8, 256))
                y_low = jnp.broadcast_to(faces(c, 2, slice(i, i + 1)), (8, 256))
            change = jnp.where(row == 7, y_high, y_flux[c]) - jnp.where(
                row == 0, y_low, y_back[c]
            )
            change = change + (z_flux[c] - z_back[c])
            if x_flux[i] is not None:
                change = change + x_flux[i][c]
            if x_flux[i - 1] is not None:
                change = change - x_flux[i - 1][c]
            value = here["amounts"][c] - STEP * change
            if c == 4:
                value = value + gain
            result.append(value)
        emit(i, result)

    enter(0)
    for i in range(9):
        if i < 7:
            enter(i + 1)
        if i < 8:
            cross(i)
        if i > 0:
            leave(i - 1)


def rates_reader(rate_ref, patch):
    half = patch // 16
    start = pl.multiple_of(8 * half, 8)
    shift = 128 - 8 * (patch - 16 * half)
    tiles = [pltpu.roll(rate_ref[t, pl.ds(start, 8), :], shift, 1) for t in range(4)]

    def rates_at(i):
        return [jnp.broadcast_to(v[:, i : i + 1], (8, 256)) for v in tiles]

    return rates_at


PER = 4


def open_kernel(
    slot_ref, rho_ref, ux_ref, uy_ref, uz_ref, p_ref, rate_ref, mean_ref, edge_ref
):
    refs = [rho_ref, ux_ref.at[0], uy_ref.at[0], uz_ref.at[0], p_ref]

    def one(n, carry):
        patch = pl.program_id(0) * PER + n
        slot = slot_ref[patch, 0]

        def on_plane(i, prim):
            for c in range(5):
                if i == 0:
                    edge_ref[n, c, 0] = prim[c]
                if i == 7:
                    edge_ref[n, c, 1] = prim[c]
                edge_ref[n, c, 2, i : i + 1, :] = prim[c][0:1, :]
                edge_ref[n, c, 3, i : i + 1, :] = prim[c][7:8, :]

        held = {}

        def emit(i, result):
            for c in range(5):
                at = (i // 2, c)
                held[at] = result[c] if i % 2 == 0 else held[at] + result[c]
                if i % 4 == 3:
                    value = fold(held.pop((i // 2 - 1, c)), held.pop(at))
                    mean_ref[slot, c, 8 * (i // 4) : 8 * (i // 4) + 8, :] = 0.125 * value

        patch_update(refs, n, rates_reader(rate_ref, patch), None, emit, on_plane)
        return carry

    lax.fori_loop(0, PER, one, 0)


def patch_specs(extra):
    one = pl.BlockSpec((PER, 64, 256), lambda i: (i, 0, 0))
    speed = [pl.BlockSpec((1, PER, 64, 256), lambda i, d=d: (d, i, 0, 0)) for d in range(3)]
    return [pl.BlockSpec(memory_space=SMEM)] * extra + [one] + speed + [one]


def open_patches(slot, rho, vel, p, rates, slots):
    count = rho.shape[0]
    return pl.pallas_call(
        open_kernel,
        grid=(count // PER,),
        out_shape=[
            jax.ShapeDtypeStruct((slots, 5, 32, 128), F32),
            jax.ShapeDtypeStruct((count, 5, 4, 8, 256), F32),
        ],
        in_specs=patch_specs(1) + [pl.BlockSpec(memory_space=VMEM)],
        out_specs=[
            pl.BlockSpec((slots, 5, 16, 128), lambda i: (0, 0, 0, 0)),
            pl.BlockSpec((PER, 5, 4, 8, 256), lambda i: (i, 0, 0, 0, 0)),
        ],
        compiler_params=pltpu.CompilerParams(vmem_limit_bytes=GRANT),
        cost_estimate=pl.CostEstimate(
            flops=250 * count * 64 * 256, bytes_accessed=18 * MIB, transcendentals=0
        ),
        name="open_patches",
    )(slot, rho, vel, vel, vel, p, rates)


BATCH = 4


def side_fluxes(rim, edge, ghost_ref):
    lane = lax.broadcasted_iota(jnp.int32, (16, 128), 1) // 2
    coarse = list(rim)
    coarse.append(sound_of(coarse[4], coarse[0]))
    for c in range(6):
        for h in range(2):
            wide = take_lanes(coarse[c], lane + 64 * h)
            ghost_ref[c, h, pl.ds(0, 16, stride=2), :] = wide
            ghost_ref[c, h, pl.ds(1, 16, stride=2), :] = wide
    sides = []
    for side in range(4):
        rows = slice(8 * side, 8 * side + 8)
        outer = [
            jnp.concatenate([ghost_ref[c, 0, rows, :], ghost_ref[c, 1, rows, :]], axis=1)
            for c in range(6)
        ]
        d = side // 2
        ghost = directed(again(*outer), d)
        prim = edge(side)
        inner = directed(again(*prim, sound_of(prim[4], prim[0])), d)
        sides.append(twice_flux(ghost, inner) if side % 2 == 0 else twice_flux(inner, ghost))
    return sides


def face_kernel(
    slot_ref, rim_hbm, edge_hbm, _, out_hbm,
    rim_ref, edge_ref, sum_ref, ghost_ref, rim_sem, edge_sem, sum_sem,
):
    count = edge_ref.shape[0]

    def load(g):
        part = pl.ds(g * BATCH, BATCH)
        return pltpu.make_async_copy(edge_hbm.at[part], edge_ref.at[part], edge_sem.at[g])

    def save(p):
        place = out_hbm.at[slot_ref[p, 0], :, pl.ds(16, 16), :]
        return pltpu.make_async_copy(sum_ref.at[p], place, sum_sem.at[p])

    def fetch(p):
        return pltpu.make_async_copy(rim_hbm.at[slot_ref[p, 0]], rim_ref.at[p], rim_sem.at[p])

    for g in range(count // BATCH):
        load(g).start()
        for n in range(BATCH):
            fetch(g * BATCH + n).start()

    def chunk(g, carry):
        load(g).wait()
        for n in range(BATCH):
            fetch(g * BATCH + n).wait()
        for n in range(BATCH):
            p = g * BATCH + n
            sides = side_fluxes(
                [rim_ref[p, c] for c in range(5)],
                lambda side, p=p: [edge_ref[p, c, side] for c in range(5)],
                ghost_ref.at[n],
            )
            for c in range(5):
                for d in range(2):
                    value = fold(sides[2 * d][c], sides[2 * d + 1][c])
                    sum_ref[p, c, 8 * d : 8 * d + 8, :] = (0.125 * STEP) * value
        for n in range(BATCH):
            save(g * BATCH + n).start()
        return carry

    lax.fori_loop(0, count // BATCH, chunk, 0)

    def settle(p, carry):
        save(p).wait()
        return carry

    lax.fori_loop(0, count, settle, 0)


def face_fluxes(slot, rims, edges, buffer):
    count = edges.shape[0]
    anywhere = pl.BlockSpec(memory_space=pl.ANY)
    return pl.pallas_call(
        face_kernel,
        out_shape=jax.ShapeDtypeStruct(buffer.shape, F32),
        in_specs=[
            pl.BlockSpec(memory_space=SMEM),
            anywhere,
            anywhere,
            anywhere,
        ],
        out_specs=anywhere,
        input_output_aliases={3: 0},
        scratch_shapes=[
            pltpu.VMEM((count, 5, 16, 128), F32),
            pltpu.VMEM(edges.shape, F32),
            pltpu.VMEM((count, 5, 16, 128), F32),
            pltpu.VMEM((BATCH, 6, 2, 32, 128), F32),
            pltpu.SemaphoreType.DMA((count,)),
            pltpu.SemaphoreType.DMA((count // BATCH,)),
            pltpu.SemaphoreType.DMA((count,)),
        ],
        compiler_params=pltpu.CompilerParams(vmem_limit_bytes=62 * MIB),
        cost_estimate=pl.CostEstimate(
            flops=100 * count * 32 * 256, bytes_accessed=11 * MIB, transcendentals=0
        ),
        name="face_fluxes",
    )(slot, rims, edges, buffer)


def close_kernel(
    slot_ref, rho_ref, ux_ref, uy_ref, uz_ref, p_ref, rate_ref, rim_ref, edge_ref,
    out_ref, ghost_ref, rows_ref,
):
    refs = [rho_ref, ux_ref.at[0], uy_ref.at[0], uz_ref.at[0], p_ref]

    def one(n, carry):
        patch = pl.program_id(0) * PER + n
        slot = slot_ref[patch, 0]
        sides = side_fluxes(
            [rim_ref[slot, c] for c in range(5)],
            lambda side: [edge_ref[n, c, side] for c in range(5)],
            ghost_ref,
        )
        for c in range(5):
            for d in range(2):
                rows_ref[c, d] = sides[2 + d][c]

        def faces(c, side, rows):
            return sides[side][c] if side < 2 else rows_ref[c, side - 2, rows, :]

        def emit(i, result):
            for c in range(5):
                out_ref[c, n, 8 * i : 8 * i + 8, :] = result[c]

        patch_update(refs, n, rates_reader(rate_ref, patch), faces, emit)
        return carry

    lax.fori_loop(0, PER, one, 0)


def close_patches(slot, rho, vel, p, rates, rims, edges):
    count = rho.shape[0]
    return pl.pallas_call(
        close_kernel,
        grid=(count // PER,),
        out_shape=jax.ShapeDtypeStruct((5,) + rho.shape, F32),
        in_specs=patch_specs(1)
        + [
            pl.BlockSpec(memory_space=VMEM),
            pl.BlockSpec(rims.shape, lambda i: (0, 0, 0, 0)),
            pl.BlockSpec((PER, 5, 4, 8, 256), lambda i: (i, 0, 0, 0, 0)),
        ],
        out_specs=pl.BlockSpec((5, PER, 64, 256), lambda i: (0, i, 0, 0)),
        scratch_shapes=[
            pltpu.VMEM((6, 2, 32, 128), F32),
            pltpu.VMEM((5, 2, 8, 256), F32),
        ],
        compiler_params=pltpu.CompilerParams(vmem_limit_bytes=20 * MIB),
        cost_estimate=pl.CostEstimate(
            flops=250 * count * 64 * 256, bytes_accessed=29 * MIB, transcendentals=0
        ),
        name="close_patches",
    )(slot, rho, vel, vel, vel, p, rates, rims, edges)


CHUNKS = 4


def merge_kernel(corner_ref, base_ref, got_hbm, out_ref, got_ref, sem):
    width = 32
    slots = got_ref.shape[0]

    size = slots // CHUNKS

    def fetch(g):
        part = pl.ds(g * size, size)
        return pltpu.make_async_copy(got_hbm.at[part], got_ref.at[part], sem.at[g])

    for g in range(CHUNKS):
        fetch(g).start()
    out_ref[...] = base_ref[...]
    row = lax.broadcasted_iota(jnp.int32, (4, 128), 0)

    def one(s, carry):
        base = corner_at(corner_ref, s)

        @pl.when(base >= 0)
        def _():
            rims = (
                pl.ds(base - width, 4),
                pl.ds(base + FOOT * width, 4),
                pl.ds(base - 1, 4, stride=width),
                pl.ds(base + FOOT, 4, stride=width),
            )
            result = []
            for c in range(5):
                flux = [
                    got_ref[s, c, pl.ds(16 + 8 * (n // 2) + n % 2, 4, stride=2), :]
                    for n in range(4)
                ]
                rim = [out_ref[c, at, :] for at in rims]
                rim = [rim[n] + flux[n] if n % 2 else rim[n] - flux[n] for n in range(4)]
                foot = []
                for i in range(4):
                    v = got_ref[s, c, pl.ds(8 * (i // 2) + i % 2, 4, stride=2), :]
                    if i == 0:
                        v = v + flux[0]
                    if i == 3:
                        v = v - flux[1]
                    low = jnp.broadcast_to(flux[2][i : i + 1, :], (4, 128))
                    high = jnp.broadcast_to(flux[3][i : i + 1, :], (4, 128))
                    v = v + jnp.where(row == 0, low, 0.0) - jnp.where(row == 3, high, 0.0)
                    foot.append(v)
                result.append((rim, foot))
            for c in range(5):
                rim, foot = result[c]
                for at, v in zip(rims, rim):
                    out_ref[c, at, :] = v
                for i in range(4):
                    out_ref[c, pl.ds(base + i * width, 4), :] = foot[i]

        return carry

    for g in range(CHUNKS):
        fetch(g).wait()
        lax.fori_loop(g * size, (g + 1) * size, one, 0)


def merge(corners, base, got):
    whole = pl.BlockSpec(memory_space=VMEM)
    return pl.pallas_call(
        merge_kernel,
        out_shape=jax.ShapeDtypeStruct(base.shape, F32),
        in_specs=[pl.BlockSpec(memory_space=SMEM), whole, pl.BlockSpec(memory_space=pl.ANY)],
        out_specs=whole,
        scratch_shapes=[pltpu.VMEM(got.shape, F32), pltpu.SemaphoreType.DMA((CHUNKS,))],
        compiler_params=pltpu.CompilerParams(vmem_limit_bytes=24 * MIB),
        cost_estimate=pl.CostEstimate(flops=MIB, bytes_accessed=11 * MIB, transcendentals=0),
        name="merge_patches",
    )(corners, base, got)


def exchange(buffer, groups):
    shape = buffer.shape
    rows = buffer.size // (groups * 128)
    moved = lax.all_to_all(
        buffer.reshape(groups, rows, 128), "yz", split_axis=0, concat_axis=0, tiled=True
    )
    return moved.reshape(shape)


def local(
    coarse_density,
    coarse_velocity,
    coarse_pressure,
    coarse_bins,
    fine_density,
    fine_velocity,
    fine_pressure,
    fine_bins,
    patch_host,
    patch_spot,
    heat_rate,
    cool_rate,
):
    groups = lax.axis_size("yz")
    rows = lax.axis_size("gx")
    gx = lax.axis_index("gx")
    me = lax.axis_index("yz")
    count = fine_density.shape[0]
    slots = CAP * groups

    rho = coarse_density.reshape(-1, 128)
    vel = coarse_velocity.reshape(3, -1, 128)
    press = coarse_pressure.reshape(-1, 128)
    place = jnp.stack([gx, me]).astype(jnp.int32)
    host_lines, spot_lines = patch_host.reshape(-1, 128), patch_spot.reshape(-1, 128)
    rims, x_first, x_last, y_first, y_last, corners, slot = pack(
        place, host_lines, spot_lines, rho, vel, press, slots
    )
    arrived = exchange(rims, groups)

    up_x = [(i, (i + 1) % rows) for i in range(rows)]
    down_x = [((i + 1) % rows, i) for i in range(rows)]
    up_y = [(i, (i + 1) % groups) for i in range(groups)]
    down_y = [((i + 1) % groups, i) for i in range(groups)]
    y_low = lax.ppermute(y_last, "yz", up_y)
    y_high = lax.ppermute(y_first, "yz", down_y)

    fine_columns = fine_bins.reshape(2, 16, 8, 8).transpose(0, 3, 1, 2).reshape(16, 128)
    coarse_columns = jnp.pad(coarse_bins.T, ((0, 0), (0, 128 - coarse_bins.shape[0])))
    tables = jnp.pad(jnp.stack([heat_rate, cool_rate]), ((0, 0), (0, 48))).reshape(2, 16, 128)
    rates = look_up(jnp.concatenate([fine_columns, coarse_columns], axis=0), tables)

    f_rho = fine_density.reshape(count, 64, 256)
    f_vel = fine_velocity.reshape(3, count, 64, 256)
    f_press = fine_pressure.reshape(count, 64, 256)
    means, edges = open_patches(slot, f_rho, f_vel, f_press, rates, slots)
    sums = face_fluxes(slot, arrived, edges, means)
    sums, y_low, y_high = lax.optimization_barrier((sums, y_low, y_high))
    got = exchange(sums, groups)
    fine_new = close_patches(slot, f_rho, f_vel, f_press, rates, arrived, edges)
    fine_new, x_first, x_last = lax.optimization_barrier((fine_new, x_first, x_last))
    x_low = lax.ppermute(x_last, "gx", up_x)
    x_high = lax.ppermute(x_first, "gx", down_x)
    base = coarse_step(corners, rho, vel, press, x_low, x_high, y_low, y_high, rates)
    coarse_new = merge(corners, base, got)
    return (
        coarse_new.reshape((5,) + coarse_density.shape),
        fine_new.reshape((5,) + fine_density.shape),
    )


def solution(mesh):
    placed = (
        P("gx", "yz", None),
        P(None, "gx", "yz", None),
        P("gx", "yz", None),
        P("gx", "yz"),
        P(("gx", "yz"), None, None, None),
        P(None, ("gx", "yz"), None, None, None),
        P(("gx", "yz"), None, None, None),
        P(("gx", "yz"), None, None),
        P(),
        P(),
        P(),
        P(),
    )
    return jax.shard_map(
        local,
        mesh=mesh,
        in_specs=placed,
        out_specs=(P(None, "gx", "yz", None), P(None, ("gx", "yz"), None, None, None)),
        check_vma=False,
    )
```

```python
import functools

import jax
import jax.numpy as jnp
from jax import lax
from jax.experimental import pallas as pl
from jax.experimental.pallas import tpu as pltpu
from jax.sharding import PartitionSpec as P

GAMMA = 5.0 / 3.0
STEP = 0.02
HALF = 0.5 * STEP
FOOT = 4
SIDE = 5
CAP = 2
F32 = jnp.float32
VMEM = pltpu.VMEM
SMEM = pltpu.SMEM
MIB = 1024 * 1024
GRANT = 56 * MIB


def conserve(rho, ux, uy, uz, p):
    mx, my, mz = rho * ux, rho * uy, rho * uz
    xx, yy, zz = mx * ux, my * uy, mz * uz
    energy = 1.5 * p + 0.5 * (xx + yy + zz)
    return {
        "amounts": (rho, mx, my, mz, energy),
        "speed": (ux, uy, uz),
        "p": p,
        "square": (xx, yy, zz),
        "cross": {},
    }


def sound_of(p, rho):
    square = GAMMA * (p / rho)
    return square * lax.rsqrt(square)


def derive(prim):
    rho, p = prim[0], prim[4]
    both = rho + p
    common = p / (rho * both)
    square = GAMMA * (common * both)
    cell = conserve(*prim)
    cell["sound"] = square * lax.rsqrt(square)
    cell["share"] = common * rho
    return cell


def again(rho, ux, uy, uz, p, sound):
    cell = conserve(rho, ux, uy, uz, p)
    cell["sound"] = sound
    return cell


def directed(cell, d):
    amounts, p = cell["amounts"], cell["p"]
    u = cell["speed"][d]
    flux = [amounts[1 + d]]
    for k in range(3):
        if k == d:
            flux.append(cell["square"][d] + p)
            continue
        pair = (min(k, d), max(k, d))
        if pair not in cell["cross"]:
            cell["cross"][pair] = amounts[1 + pair[0]] * cell["speed"][pair[1]]
        flux.append(cell["cross"][pair])
    flux.append((amounts[4] + p) * u)
    return (amounts, flux, jnp.abs(u) + cell["sound"])


def twice_flux(left, right):
    fastest = jnp.maximum(left[2], right[2])
    return [
        (left[1][c] + right[1][c]) - fastest * (right[0][c] - left[0][c]) for c in range(5)
    ]


def shifted(cell, shift, axis):
    rho, p = cell["amounts"][0], cell["p"]
    values = (rho,) + cell["speed"] + (p, cell["sound"])
    return again(*[pltpu.roll(v, shift, axis) for v in values])


def source_term(rho, share, rates):
    heat, heat_slope, cool, cool_slope = rates
    return rho * ((heat + share * heat_slope) - rho * (cool + share * cool_slope))


def lane_pick(tile, lane):
    index = jnp.full((8, 128), lane, jnp.int32)
    return jnp.take_along_axis(tile, index, axis=1, mode="promise_in_bounds")


def plan_places(place_ref, host_ref, spot_ref, corner_ref, slot_ref):
    gx, me = place_ref[0], place_ref[1]
    rows = pl.ds(pl.multiple_of(8 * gx, 8), 8)
    hosts, spots = host_ref[rows, :], spot_ref[rows, :]
    lane = lax.broadcasted_iota(jnp.int32, (8, 128), 1)
    row = lax.broadcasted_iota(jnp.int32, (8, 128), 0)
    place_x = (spots * 43) >> 8
    corner = (1 + SIDE * place_x) * 32 + 1 + SIDE * (spots - 6 * place_x)
    key = jnp.where(hosts == me, lane * 1024 + corner, -1)
    table = jnp.full((8, 128), -1, jnp.int32)
    far = 1 << 20
    for q in range(4):
        inside = (lane // 32 == q) & (key >= 0)
        last = jnp.max(jnp.where(inside, key, -1), axis=1, keepdims=True)
        first = jnp.min(jnp.where(inside, key, far), axis=1, keepdims=True)
        none = last < 0
        single = none | (first == last)
        table = jnp.where(lane == 2 * q, jnp.where(none, -1, first & 1023), table)
        table = jnp.where(lane == 2 * q + 1, jnp.where(single, -1, last & 1023), table)
    corner_ref[...] = table
    own = jnp.sum(jnp.where(row == me // 4, hosts, 0), axis=0, keepdims=True)
    own = pltpu.roll(jnp.broadcast_to(own, (8, 128)), lax.rem(128 - 32 * lax.rem(me, 4), 128), 1)
    own = jnp.broadcast_to(own[0:1, :], (32, 128))
    lane = lax.broadcasted_iota(jnp.int32, (32, 128), 1)
    row = lax.broadcasted_iota(jnp.int32, (32, 128), 0)
    mine = jnp.sum(jnp.where(lane == row, own, 0), axis=1, keepdims=True)
    rank = jnp.sum(jnp.where((own == mine) & (lane < row), 1, 0), axis=1, keepdims=True)
    slot_ref[...] = jnp.broadcast_to(CAP * mine + rank, (32, 128))


def corner_at(corner_ref, s):
    line = s // 8
    return corner_ref[line, s - 8 * line]


def pack_kernel(
    place_ref, host_ref, spot_ref, rho_hbm, vel_hbm, p_hbm,
    rim_ref, xa_ref, xb_ref, ya_ref, yb_ref, corner_ref, slot_ref,
    cell_ref, table_ref, sem, table_sem,
):
    sources = [rho_hbm, vel_hbm.at[0], vel_hbm.at[1], vel_hbm.at[2], p_hbm]
    copies = [pltpu.make_async_copy(f, cell_ref.at[c], sem.at[c]) for c, f in enumerate(sources)]
    for copy in copies:
        copy.start()
    plan_places(place_ref, host_ref, spot_ref, corner_ref, slot_ref)
    move = pltpu.make_async_copy(corner_ref, table_ref, table_sem)
    move.start()
    move.wait()
    for copy in copies:
        copy.wait()
    fields = [cell_ref.at[c] for c in range(5)]
    width = 32
    rows = cell_ref.shape[1]

    def one(s, carry):
        base = corner_at(table_ref, s)

        @pl.when(base >= 0)
        def _():
            for c, f in enumerate(fields):
                rim_ref[s, c, 0:4, :] = f[pl.ds(base - width, 4), :]
                rim_ref[s, c, 4:8, :] = f[pl.ds(base + FOOT * width, 4), :]
                rim_ref[s, c, 8:12, :] = f[pl.ds(base - 1, 4, stride=width), :]
                rim_ref[s, c, 12:16, :] = f[pl.ds(base + FOOT, 4, stride=width), :]

        return carry

    lax.fori_loop(0, rim_ref.shape[0], one, 0)
    for c, f in enumerate(fields):
        xa_ref[c] = f[0:width, :]
        xb_ref[c] = f[rows - width : rows, :]
        ya_ref[c] = f[pl.ds(0, width, stride=width), :]
        yb_ref[c] = f[pl.ds(width - 1, width, stride=width), :]


def pack(place, hosts, spots, rho, vel, p, slots):
    whole = pl.BlockSpec(memory_space=VMEM)
    edge = jax.ShapeDtypeStruct((5, 32, 128), F32)
    return pl.pallas_call(
        pack_kernel,
        out_shape=[jax.ShapeDtypeStruct((slots, 5, 16, 128), F32), edge, edge, edge, edge]
        + [jax.ShapeDtypeStruct((8, 128), jnp.int32), jax.ShapeDtypeStruct((32, 128), jnp.int32)],
        in_specs=[pl.BlockSpec(memory_space=SMEM), whole, whole]
        + [pl.BlockSpec(memory_space=pl.ANY)] * 3,
        out_specs=[whole] * 7,
        scratch_shapes=[
            pltpu.VMEM((5,) + rho.shape, F32),
            pltpu.SMEM((8, 128), jnp.int32),
            pltpu.SemaphoreType.DMA((5,)),
            pltpu.SemaphoreType.DMA,
        ],
        compiler_params=pltpu.CompilerParams(vmem_limit_bytes=GRANT),
        cost_estimate=pl.CostEstimate(flops=0, bytes_accessed=6 * MIB, transcendentals=0),
        name="pack_rims",
    )(place, hosts, spots, rho, vel, p)


def rates_kernel(bins_ref, table_ref, out_ref):
    for g in range(bins_ref.shape[0] // 8):
        rows = slice(8 * g, 8 * g + 8)
        low = None
        for step in range(2):
            b = bins_ref[rows, :] + step
            line = b // 128
            lane = b - line * 128
            found = [jnp.zeros((8, 128), F32) for _ in range(2)]
            for r in range(16):
                hit = line == r
                for t in range(2):
                    entry = jnp.broadcast_to(table_ref[t, r : r + 1, :], (8, 128))
                    value = jnp.take_along_axis(entry, lane, axis=1, mode="promise_in_bounds")
                    found[t] = jnp.where(hit, value, found[t])
            for t in range(2):
                entry = found[t] if step == 0 else found[t] - low[t]
                out_ref[2 * t + step, rows, :] = STEP * entry
            low = found


def look_up(bins, tables):
    whole = pl.BlockSpec(memory_space=VMEM)
    return pl.pallas_call(
        rates_kernel,
        out_shape=jax.ShapeDtypeStruct((4,) + bins.shape, F32),
        in_specs=[whole, whole],
        out_specs=whole,
        cost_estimate=pl.CostEstimate(flops=MIB, bytes_accessed=MIB, transcendentals=0),
        name="rate_lookup",
    )(bins, tables)


PITCH = 48
LOW = 8


def coarse_kernel(
    corner_ref, rho_ref, vel_ref, p_ref, xlo_ref, xhi_ref, ylo_ref, yhi_ref, rate_ref,
    out_ref, cell_ref, fx_ref, fy_ref,
):
    width = 32
    fields = [rho_ref, vel_ref.at[0], vel_ref.at[1], vel_ref.at[2], p_ref]

    def keep(prim, index):
        for n, v in enumerate(prim):
            cell_ref[n, index, :] = v
        cell_ref[5, index, :] = sound_of(prim[4], prim[0])

    def fill(x, carry):
        for q in range(4):
            rows = pl.ds(x * width + 8 * q, 8)
            keep([f[rows, :] for f in fields], pl.ds((x + 1) * PITCH + LOW + 8 * q, 8))
        return carry

    lax.fori_loop(0, width, fill, 0)
    for q in range(4):
        rows = slice(8 * q, 8 * q + 8)
        keep([xlo_ref[c, rows, :] for c in range(5)], pl.ds(LOW + 8 * q, 8))
        keep([xhi_ref[c, rows, :] for c in range(5)], pl.ds(33 * PITCH + LOW + 8 * q, 8))
        first = (8 * q + 1) * PITCH + LOW
        keep([ylo_ref[c, rows, :] for c in range(5)], pl.ds(first - 1, 8, stride=PITCH))
        keep([yhi_ref[c, rows, :] for c in range(5)], pl.ds(first + width, 8, stride=PITCH))

    def fetch(row):
        return again(*[cell_ref[n, pl.ds(row, 8), :] for n in range(6)])

    def step(x, carry):
        result = []
        for q in range(4):
            below = carry[5 * q : 5 * q + 5]
            row = (x + 1) * PITCH + LOW + 8 * q
            here = fetch(row)
            above = twice_flux(directed(here, 0), directed(fetch(row + PITCH), 0))
            y_here = directed(here, 1)
            y_high = twice_flux(y_here, directed(fetch(row + 1), 1))
            y_low = twice_flux(directed(fetch(row - 1), 1), y_here)
            z_high = twice_flux(directed(here, 2), directed(shifted(here, 127, 1), 2))
            rates = [lane_pick(rate_ref[t, 16 + 8 * q : 24 + 8 * q, :], x) for t in range(4)]
            rho = here["amounts"][0]
            gain = source_term(rho, here["p"] / (rho + here["p"]), rates)
            flat = pl.ds(x * width + 8 * q, 8)
            for c in range(5):
                change = (
                    (above[c] - below[c])
                    + (y_high[c] - y_low[c])
                    + (z_high[c] - pltpu.roll(z_high[c], 1, 1))
                )
                value = here["amounts"][c] - HALF * change
                if c == 4:
                    value = value + gain
                out_ref[c, flat, :] = value
                fx_ref[c, flat, :] = above[c]
                fy_ref[c, flat, :] = y_high[c]
            result += above
        return tuple(result)

    first = []
    for q in range(4):
        row = LOW + 8 * q
        first += twice_flux(directed(fetch(row), 0), directed(fetch(row + PITCH), 0))
    lax.fori_loop(0, width, step, tuple(first))

    def reflux(s, carry):
        base = corner_at(corner_ref, s)

        @pl.when(base >= 0)
        def _():
            places = (
                (pl.ds(base - width, 4), pl.ds(base - width, 4), fx_ref, HALF),
                (
                    pl.ds(base + FOOT * width, 4),
                    pl.ds(base + (FOOT - 1) * width, 4),
                    fx_ref,
                    -HALF,
                ),
                (
                    pl.ds(base - 1, 4, stride=width),
                    pl.ds(base - 1, 4, stride=width),
                    fy_ref,
                    HALF,
                ),
                (
                    pl.ds(base + FOOT, 4, stride=width),
                    pl.ds(base + FOOT - 1, 4, stride=width),
                    fy_ref,
                    -HALF,
                ),
            )
            values = [
                [out_ref[c, a, :] + w * f[c, b, :] for a, b, f, w in places] for c in range(5)
            ]
            for c in range(5):
                for n in range(4):
                    out_ref[c, places[n][0], :] = values[c][n]

        return carry

    lax.fori_loop(0, 8 * corner_ref.shape[0], reflux, 0)


def coarse_step(corners, rho, vel, p, xlo, xhi, ylo, yhi, rates):
    whole = pl.BlockSpec(memory_space=VMEM)
    cells = rho.shape[0]
    return pl.pallas_call(
        coarse_kernel,
        out_shape=jax.ShapeDtypeStruct((5, cells, 128), F32),
        in_specs=[pl.BlockSpec(memory_space=SMEM)] + [whole] * 8,
        out_specs=whole,
        scratch_shapes=[
            pltpu.VMEM((6, 34 * PITCH, 128), F32),
            pltpu.VMEM((5, cells, 128), F32),
            pltpu.VMEM((5, cells, 128), F32),
        ],
        compiler_params=pltpu.CompilerParams(vmem_limit_bytes=32 * MIB),
        cost_estimate=pl.CostEstimate(
            flops=300 * cells * 128, bytes_accessed=30 * MIB, transcendentals=0
        ),
        name="coarse_step",
    )(corners, rho, vel, p, xlo, xhi, ylo, yhi, rates)


def take_lanes(tile, index):
    return jnp.take_along_axis(tile, index, axis=1, mode="promise_in_bounds")


def fold(even, odd):
    row = lax.broadcasted_iota(jnp.int32, (8, 128), 0)
    lane = lax.broadcasted_iota(jnp.int32, (8, 128), 1)
    halves = []
    for h in range(2):
        a, b = even[:, 128 * h : 128 * h + 128], odd[:, 128 * h : 128 * h + 128]
        a = a + pltpu.roll(a, 7, 0)
        b = b + pltpu.roll(b, 1, 0)
        m = jnp.where(row % 2 == 0, a, b)
        halves.append(m + pltpu.roll(m, 127 if h == 0 else 1, 1))
    mixed = jnp.where(lane % 2 == 0, halves[0], halves[1])
    return take_lanes(mixed, jnp.where(lane < 64, 2 * lane, 2 * lane - 127))


def patch_update(prim_refs, p_index, rates_at, faces, emit, on_plane=None):
    row = lax.broadcasted_iota(jnp.int32, (8, 256), 0)
    cells, fluxes, x_flux = {}, {}, {}
    x_flux[-1] = None if faces is None else [faces(c, 0, slice(0, 8)) for c in range(5)]
    x_flux[7] = None if faces is None else [faces(c, 1, slice(0, 8)) for c in range(5)]

    def enter(i):
        prim = [f[p_index, 8 * i : 8 * i + 8, :] for f in prim_refs]
        if on_plane is not None:
            on_plane(i, prim)
        here = derive(prim)
        cells[i] = (here, shifted(here, 7, 0), shifted(here, 255, 1), rates_at(i))

    def cross(i):
        here, y_next, z_next, _ = cells[i]
        y_flux = twice_flux(directed(here, 1), directed(y_next, 1))
        z_flux = twice_flux(directed(here, 2), directed(z_next, 2))
        y_back = [pltpu.roll(v, 1, 0) for v in y_flux]
        z_back = [pltpu.roll(v, 1, 1) for v in z_flux]
        fluxes[i] = (y_flux, y_back, z_flux, z_back)
        if i < 7:
            x_flux[i] = None
            if faces is not None or i % 2 == 1:
                x_flux[i] = twice_flux(directed(here, 0), directed(cells[i + 1][0], 0))

    def leave(i):
        here, _, _, rates = cells.pop(i)
        y_flux, y_back, z_flux, z_back = fluxes.pop(i)
        gain = source_term(here["amounts"][0], here["share"], rates)
        result = []
        for c in range(5):
            if faces is None:
                y_high, y_low = 0.0, 0.0
            else:
                y_high = jnp.broadcast_to(faces(c, 3, slice(i, i + 1)), (8, 256))
                y_low = jnp.broadcast_to(faces(c, 2, slice(i, i + 1)), (8, 256))
            change = jnp.where(row == 7, y_high, y_flux[c]) - jnp.where(
                row == 0, y_low, y_back[c]
            )
            change = change + (z_flux[c] - z_back[c])
            if x_flux[i] is not None:
                change = change + x_flux[i][c]
            if x_flux[i - 1] is not None:
                change = change - x_flux[i - 1][c]
            value = here["amounts"][c] - STEP * change
            if c == 4:
                value = value + gain
            result.append(value)
        emit(i, result)

    enter(0)
    for i in range(9):
        if i < 7:
            enter(i + 1)
        if i < 8:
            cross(i)
        if i > 0:
            leave(i - 1)


def rates_reader(rate_ref, patch):
    half = patch // 16
    start = pl.multiple_of(8 * half, 8)
    shift = 128 - 8 * (patch - 16 * half)
    tiles = [pltpu.roll(rate_ref[t, pl.ds(start, 8), :], shift, 1) for t in range(4)]

    def rates_at(i):
        return [jnp.broadcast_to(v[:, i : i + 1], (8, 256)) for v in tiles]

    return rates_at


PER = 4


def open_kernel(
    slot_ref, rho_ref, ux_ref, uy_ref, uz_ref, p_ref, rate_ref, mean_ref, edge_ref
):
    refs = [rho_ref, ux_ref.at[0], uy_ref.at[0], uz_ref.at[0], p_ref]

    def one(n, carry):
        patch = pl.program_id(0) * PER + n
        slot = slot_ref[patch, 0]

        def on_plane(i, prim):
            for c in range(5):
                if i == 0:
                    edge_ref[n, c, 0] = prim[c]
                if i == 7:
                    edge_ref[n, c, 1] = prim[c]
                edge_ref[n, c, 2, i : i + 1, :] = prim[c][0:1, :]
                edge_ref[n, c, 3, i : i + 1, :] = prim[c][7:8, :]

        held = {}

        def emit(i, result):
            for c in range(5):
                at = (i // 2, c)
                held[at] = result[c] if i % 2 == 0 else held[at] + result[c]
                if i % 4 == 3:
                    value = fold(held.pop((i // 2 - 1, c)), held.pop(at))
                    mean_ref[slot, c, 8 * (i // 4) : 8 * (i // 4) + 8, :] = 0.125 * value

        patch_update(refs, n, rates_reader(rate_ref, patch), None, emit, on_plane)
        return carry

    lax.fori_loop(0, PER, one, 0)


def patch_specs(extra):
    one = pl.BlockSpec((PER, 64, 256), lambda i: (i, 0, 0))
    speed = [pl.BlockSpec((1, PER, 64, 256), lambda i, d=d: (d, i, 0, 0)) for d in range(3)]
    return [pl.BlockSpec(memory_space=SMEM)] * extra + [one] + speed + [one]


def open_patches(slot, rho, vel, p, rates, slots):
    count = rho.shape[0]
    return pl.pallas_call(
        open_kernel,
        grid=(count // PER,),
        out_shape=[
            jax.ShapeDtypeStruct((slots, 5, 32, 128), F32),
            jax.ShapeDtypeStruct((count, 5, 4, 8, 256), F32),
        ],
        in_specs=patch_specs(1) + [pl.BlockSpec(memory_space=VMEM)],
        out_specs=[
            pl.BlockSpec((slots, 5, 16, 128), lambda i: (0, 0, 0, 0)),
            pl.BlockSpec((PER, 5, 4, 8, 256), lambda i: (i, 0, 0, 0, 0)),
        ],
        compiler_params=pltpu.CompilerParams(vmem_limit_bytes=GRANT),
        cost_estimate=pl.CostEstimate(
            flops=250 * count * 64 * 256, bytes_accessed=18 * MIB, transcendentals=0
        ),
        name="open_patches",
    )(slot, rho, vel, vel, vel, p, rates)


BATCH = 4


def side_fluxes(rim, edge, ghost_ref):
    lane = lax.broadcasted_iota(jnp.int32, (16, 128), 1) // 2
    coarse = list(rim)
    coarse.append(sound_of(coarse[4], coarse[0]))
    for c in range(6):
        for h in range(2):
            wide = take_lanes(coarse[c], lane + 64 * h)
            ghost_ref[c, h, pl.ds(0, 16, stride=2), :] = wide
            ghost_ref[c, h, pl.ds(1, 16, stride=2), :] = wide
    sides = []
    for side in range(4):
        rows = slice(8 * side, 8 * side + 8)
        outer = [
            jnp.concatenate([ghost_ref[c, 0, rows, :], ghost_ref[c, 1, rows, :]], axis=1)
            for c in range(6)
        ]
        d = side // 2
        ghost = directed(again(*outer), d)
        prim = edge(side)
        inner = directed(again(*prim, sound_of(prim[4], prim[0])), d)
        sides.append(twice_flux(ghost, inner) if side % 2 == 0 else twice_flux(inner, ghost))
    return sides


def face_kernel(
    slot_ref, rim_hbm, edge_ref, _, out_hbm, rim_ref, sum_ref, ghost_ref, rim_sem, sum_sem
):
    count = edge_ref.shape[0]

    def save(p):
        place = out_hbm.at[slot_ref[p, 0], :, pl.ds(16, 16), :]
        return pltpu.make_async_copy(sum_ref.at[p], place, sum_sem.at[p])

    def fetch(p):
        return pltpu.make_async_copy(rim_hbm.at[slot_ref[p, 0]], rim_ref.at[p], rim_sem.at[p])

    for p in range(count):
        fetch(p).start()

    def chunk(g, carry):
        for n in range(BATCH):
            fetch(g * BATCH + n).wait()
        for n in range(BATCH):
            p = g * BATCH + n
            sides = side_fluxes(
                [rim_ref[p, c] for c in range(5)],
                lambda side, p=p: [edge_ref[p, c, side] for c in range(5)],
                ghost_ref.at[n],
            )
            for c in range(5):
                for d in range(2):
                    value = fold(sides[2 * d][c], sides[2 * d + 1][c])
                    sum_ref[p, c, 8 * d : 8 * d + 8, :] = (0.125 * STEP) * value
        for n in range(BATCH):
            save(g * BATCH + n).start()
        return carry

    lax.fori_loop(0, count // BATCH, chunk, 0)

    def settle(p, carry):
        save(p).wait()
        return carry

    lax.fori_loop(0, count, settle, 0)


def face_fluxes(slot, rims, edges, buffer):
    count = edges.shape[0]
    anywhere = pl.BlockSpec(memory_space=pl.ANY)
    return pl.pallas_call(
        face_kernel,
        out_shape=jax.ShapeDtypeStruct(buffer.shape, F32),
        in_specs=[
            pl.BlockSpec(memory_space=SMEM),
            anywhere,
            pl.BlockSpec(memory_space=VMEM),
            anywhere,
        ],
        out_specs=anywhere,
        input_output_aliases={3: 0},
        scratch_shapes=[
            pltpu.VMEM((count, 5, 16, 128), F32),
            pltpu.VMEM((count, 5, 16, 128), F32),
            pltpu.VMEM((BATCH, 6, 2, 32, 128), F32),
            pltpu.SemaphoreType.DMA((count,)),
            pltpu.SemaphoreType.DMA((count,)),
        ],
        compiler_params=pltpu.CompilerParams(vmem_limit_bytes=57 * MIB),
        cost_estimate=pl.CostEstimate(
            flops=100 * count * 32 * 256, bytes_accessed=11 * MIB, transcendentals=0
        ),
        name="face_fluxes",
    )(slot, rims, edges, buffer)


def close_kernel(
    slot_ref, rho_ref, ux_ref, uy_ref, uz_ref, p_ref, rate_ref, rim_ref, edge_ref,
    out_ref, ghost_ref, rows_ref,
):
    refs = [rho_ref, ux_ref.at[0], uy_ref.at[0], uz_ref.at[0], p_ref]

    def one(n, carry):
        patch = pl.program_id(0) * PER + n
        slot = slot_ref[patch, 0]
        sides = side_fluxes(
            [rim_ref[slot, c] for c in range(5)],
            lambda side: [edge_ref[n, c, side] for c in range(5)],
            ghost_ref,
        )
        for c in range(5):
            for d in range(2):
                rows_ref[c, d] = sides[2 + d][c]

        def faces(c, side, rows):
            return sides[side][c] if side < 2 else rows_ref[c, side - 2, rows, :]

        def emit(i, result):
            for c in range(5):
                out_ref[c, n, 8 * i : 8 * i + 8, :] = result[c]

        patch_update(refs, n, rates_reader(rate_ref, patch), faces, emit)
        return carry

    lax.fori_loop(0, PER, one, 0)


def close_patches(slot, rho, vel, p, rates, rims, edges):
    count = rho.shape[0]
    return pl.pallas_call(
        close_kernel,
        grid=(count // PER,),
        out_shape=jax.ShapeDtypeStruct((5,) + rho.shape, F32),
        in_specs=patch_specs(1)
        + [
            pl.BlockSpec(memory_space=VMEM),
            pl.BlockSpec(rims.shape, lambda i: (0, 0, 0, 0)),
            pl.BlockSpec((PER, 5, 4, 8, 256), lambda i: (i, 0, 0, 0, 0)),
        ],
        out_specs=pl.BlockSpec((5, PER, 64, 256), lambda i: (0, i, 0, 0)),
        scratch_shapes=[
            pltpu.VMEM((6, 2, 32, 128), F32),
            pltpu.VMEM((5, 2, 8, 256), F32),
        ],
        compiler_params=pltpu.CompilerParams(vmem_limit_bytes=20 * MIB),
        cost_estimate=pl.CostEstimate(
            flops=250 * count * 64 * 256, bytes_accessed=29 * MIB, transcendentals=0
        ),
        name="close_patches",
    )(slot, rho, vel, vel, vel, p, rates, rims, edges)


CHUNKS = 4


def merge_kernel(corner_ref, base_ref, got_hbm, out_ref, got_ref, sem):
    width = 32
    slots = got_ref.shape[0]

    size = slots // CHUNKS

    def fetch(g):
        part = pl.ds(g * size, size)
        return pltpu.make_async_copy(got_hbm.at[part], got_ref.at[part], sem.at[g])

    for g in range(CHUNKS):
        fetch(g).start()
    out_ref[...] = base_ref[...]
    row = lax.broadcasted_iota(jnp.int32, (4, 128), 0)

    def one(s, carry):
        base = corner_at(corner_ref, s)

        @pl.when(base >= 0)
        def _():
            rims = (
                pl.ds(base - width, 4),
                pl.ds(base + FOOT * width, 4),
                pl.ds(base - 1, 4, stride=width),
                pl.ds(base + FOOT, 4, stride=width),
            )
            result = []
            for c in range(5):
                flux = [
                    got_ref[s, c, pl.ds(16 + 8 * (n // 2) + n % 2, 4, stride=2), :]
                    for n in range(4)
                ]
                rim = [out_ref[c, at, :] for at in rims]
                rim = [rim[n] + flux[n] if n % 2 else rim[n] - flux[n] for n in range(4)]
                foot = []
                for i in range(4):
                    v = got_ref[s, c, pl.ds(8 * (i // 2) + i % 2, 4, stride=2), :]
                    if i == 0:
                        v = v + flux[0]
                    if i == 3:
                        v = v - flux[1]
                    low = jnp.broadcast_to(flux[2][i : i + 1, :], (4, 128))
                    high = jnp.broadcast_to(flux[3][i : i + 1, :], (4, 128))
                    v = v + jnp.where(row == 0, low, 0.0) - jnp.where(row == 3, high, 0.0)
                    foot.append(v)
                result.append((rim, foot))
            for c in range(5):
                rim, foot = result[c]
                for at, v in zip(rims, rim):
                    out_ref[c, at, :] = v
                for i in range(4):
                    out_ref[c, pl.ds(base + i * width, 4), :] = foot[i]

        return carry

    for g in range(CHUNKS):
        fetch(g).wait()
        lax.fori_loop(g * size, (g + 1) * size, one, 0)


def merge(corners, base, got):
    whole = pl.BlockSpec(memory_space=VMEM)
    return pl.pallas_call(
        merge_kernel,
        out_shape=jax.ShapeDtypeStruct(base.shape, F32),
        in_specs=[pl.BlockSpec(memory_space=SMEM), whole, pl.BlockSpec(memory_space=pl.ANY)],
        out_specs=whole,
        scratch_shapes=[pltpu.VMEM(got.shape, F32), pltpu.SemaphoreType.DMA((CHUNKS,))],
        compiler_params=pltpu.CompilerParams(vmem_limit_bytes=24 * MIB),
        cost_estimate=pl.CostEstimate(flops=MIB, bytes_accessed=11 * MIB, transcendentals=0),
        name="merge_patches",
    )(corners, base, got)


def exchange(buffer, groups):
    shape = buffer.shape
    rows = buffer.size // (groups * 128)
    moved = lax.all_to_all(
        buffer.reshape(groups, rows, 128), "yz", split_axis=0, concat_axis=0, tiled=True
    )
    return moved.reshape(shape)


def local(
    coarse_density,
    coarse_velocity,
    coarse_pressure,
    coarse_bins,
    fine_density,
    fine_velocity,
    fine_pressure,
    fine_bins,
    patch_host,
    patch_spot,
    heat_rate,
    cool_rate,
):
    groups = lax.axis_size("yz")
    rows = lax.axis_size("gx")
    gx = lax.axis_index("gx")
    me = lax.axis_index("yz")
    count = fine_density.shape[0]
    slots = CAP * groups

    rho = coarse_density.reshape(-1, 128)
    vel = coarse_velocity.reshape(3, -1, 128)
    press = coarse_pressure.reshape(-1, 128)
    place = jnp.stack([gx, me]).astype(jnp.int32)
    host_lines, spot_lines = patch_host.reshape(-1, 128), patch_spot.reshape(-1, 128)
    rims, x_first, x_last, y_first, y_last, corners, slot = pack(
        place, host_lines, spot_lines, rho, vel, press, slots
    )
    arrived = exchange(rims, groups)

    up_x = [(i, (i + 1) % rows) for i in range(rows)]
    down_x = [((i + 1) % rows, i) for i in range(rows)]
    up_y = [(i, (i + 1) % groups) for i in range(groups)]
    down_y = [((i + 1) % groups, i) for i in range(groups)]
    y_low = lax.ppermute(y_last, "yz", up_y)
    y_high = lax.ppermute(y_first, "yz", down_y)

    fine_columns = fine_bins.reshape(2, 16, 8, 8).transpose(0, 3, 1, 2).reshape(16, 128)
    coarse_columns = jnp.pad(coarse_bins.T, ((0, 0), (0, 128 - coarse_bins.shape[0])))
    tables = jnp.pad(jnp.stack([heat_rate, cool_rate]), ((0, 0), (0, 48))).reshape(2, 16, 128)
    rates = look_up(jnp.concatenate([fine_columns, coarse_columns], axis=0), tables)

    f_rho = fine_density.reshape(count, 64, 256)
    f_vel = fine_velocity.reshape(3, count, 64, 256)
    f_press = fine_pressure.reshape(count, 64, 256)
    means, edges = open_patches(slot, f_rho, f_vel, f_press, rates, slots)
    sums = face_fluxes(slot, arrived, edges, means)
    sums, y_low, y_high = lax.optimization_barrier((sums, y_low, y_high))
    got = exchange(sums, groups)
    fine_new = close_patches(slot, f_rho, f_vel, f_press, rates, arrived, edges)
    fine_new, x_first, x_last = lax.optimization_barrier((fine_new, x_first, x_last))
    x_low = lax.ppermute(x_last, "gx", up_x)
    x_high = lax.ppermute(x_first, "gx", down_x)
    base = coarse_step(corners, rho, vel, press, x_low, x_high, y_low, y_high, rates)
    coarse_new = merge(corners, base, got)
    return (
        coarse_new.reshape((5,) + coarse_density.shape),
        fine_new.reshape((5,) + fine_density.shape),
    )


def solution(mesh):
    placed = (
        P("gx", "yz", None),
        P(None, "gx", "yz", None),
        P("gx", "yz", None),
        P("gx", "yz"),
        P(("gx", "yz"), None, None, None),
        P(None, ("gx", "yz"), None, None, None),
        P(("gx", "yz"), None, None, None),
        P(("gx", "yz"), None, None),
        P(),
        P(),
        P(),
        P(),
    )
    return jax.shard_map(
        local,
        mesh=mesh,
        in_specs=placed,
        out_specs=(P(None, "gx", "yz", None), P(None, ("gx", "yz"), None, None, None)),
        check_vma=False,
    )
```
